128 devices in a mesh: batch: 4 (over z_lo, core), seq: 32 (over y, x, z_hi).
Axes of the slice: x: 4, y: 4, z: 4 (z_hi: 2, z_lo: 2; z = z_hi * 2 + z_lo), core: 2. Of those that a mesh axis runs over, the one named last changes fastest.
Arguments:
- tokens: bfloat16 [4, 4096, 512], P('batch', 'seq'), may hold values from -6 to 6
- camera: bfloat16 [4, 1024], P('batch'), may hold values from -6 to 6
- features: bfloat16 [4, 1024, 384], P('batch', 'seq'), may hold values from -6 to 6
- foreground: int32 [4, 8], P('batch'), may hold values from 0 to 1, as said below
- layout: int32 [4, 32], P('batch', 'seq'), may hold values from 0 to 31, as said below
- modulation_weight: bfloat16 [1024, 1024], replicated, may hold values from -0.09375 to 0.09375
- modulation_bias: bfloat16 [1024], replicated, may hold values from -3 to 3
- self_in_weight: bfloat16 [512, 1536], replicated, may hold values from -0.25 to 0.25
- self_out_weight: bfloat16 [512, 512], replicated, may hold values from -0.75 to 0.75
- cross_norm_gain: bfloat16 [512], replicated, may hold values from 0.25 to 1.75
- cross_norm_bias: bfloat16 [512], replicated, may hold values from -2 to 2
- cross_query_weight: bfloat16 [512, 512], replicated, may hold values from -0.375 to 0.375
- cross_pair_weight: bfloat16 [384, 1024], replicated, may hold values from -0.4375 to 0.4375
- cross_out_weight: bfloat16 [512, 512], replicated, may hold values from -0.75 to 0.75
- feed_norm_gain: bfloat16 [512], replicated, may hold values from 0.25 to 1.75
- feed_norm_bias: bfloat16 [512], replicated, may hold values from -2 to 2
- up_weight: bfloat16 [512, 2048], replicated, may hold values from -0.25 to 0.25
- down_weight: bfloat16 [2048, 512], replicated, may hold values from -0.125 to 0.125
- cotangent: bfloat16 [4, 4096, 512], P('batch', 'seq'), may hold values from -6 to 6
Outputs:
- block_out: float32 [4, 4096, 512], P('batch', 'seq')
- token_grad: float32 [4, 4096, 512], P('batch', 'seq')
- feature_grad: float32 [4, 1024, 384], P('batch', 'seq')
- modulation_weight_grad: float32 [1024, 1024], replicated
- modulation_bias_grad: float32 [1024], replicated
- self_in_weight_grad: float32 [512, 1536], replicated
- self_out_weight_grad: float32 [512, 512], replicated
- cross_norm_gain_grad: float32 [512], replicated
- cross_norm_bias_grad: float32 [512], replicated
- cross_query_weight_grad: float32 [512, 512], replicated
- cross_pair_weight_grad: float32 [384, 1024], replicated
- cross_out_weight_grad: float32 [512, 512], replicated
- feed_norm_gain_grad: float32 [512], replicated
- feed_norm_bias_grad: float32 [512], replicated
- up_weight_grad: float32 [512, 2048], replicated
- down_weight_grad: float32 [2048, 512], replicated
The draws below stay inside these ranges and needn't reach their ends.
Inputs may be any that keep to these rules, and one draw needn't show every extreme that they name: Each object has at least one patch block with foreground and at least one without. `layout`: each row is a permutation of 0 to 31. Block numbers below 24 are triplane blocks; block number b of 24 or more is patch block b - 24.
All inputs are finite; a program needn't handle non-finite values.
Results may differ from the reference program's by a relative error of at most 0.04.
Values may be sent and summed in bfloat16 or wider, within the bound.
No kernel may reach another device: no remote copies, remote signals or barrier semaphores. Data moves between devices by JAX's collectives and lax.ppermute only.
A program may use at most 192 MiB of HBM per device.

```python
import jax
import jax.numpy as jnp
from jax import lax

HEADS = 8
HEAD_DIM = 64
FF = 2048
DINO = 384
CAMD = 1024
BLOCK = 128
TRIB = 24
PATCHB = 8
D = 512
NBLK = 32
SEQ = 4096
PATCH = 1024
OBJECTS = 4


def draw_foreground(key, part):
    key = jax.random.fold_in(key, 11)
    tier_key, pick_key, gap_key, cell_key = jax.random.split(key, 4)
    tier = jax.random.randint(tier_key, (OBJECTS, 1), 0, 4)
    limit = jnp.right_shift(jnp.full((OBJECTS, 1), PATCHB, jnp.int32), tier)
    rolls = jax.random.randint(cell_key, (OBJECTS, PATCHB), 0, PATCHB)
    kept = rolls < limit
    chosen = jax.random.randint(pick_key, (OBJECTS, 1), 0, PATCHB)
    offset = jax.random.randint(gap_key, (OBJECTS, 1), 1, PATCHB)
    dropped = (chosen + offset) % PATCHB
    position = jnp.arange(PATCHB, dtype=jnp.int32)[None, :]
    kept = jnp.logical_or(kept, position == chosen)
    kept = jnp.logical_and(kept, position != dropped)
    return kept.astype(jnp.int32)


def draw_layout(key, part):
    key = jax.random.fold_in(key, 23)
    object_keys = jax.random.split(key, OBJECTS)
    return jax.vmap(lambda object_key: jax.random.permutation(object_key, NBLK))(object_keys).astype(jnp.int32)


def level_of(rng, dims, pieces, low, top_value):
    level, own = 1.0, jax.random.fold_in(rng, 6)
    for axis_at, blocks in pieces:
        draws = jnp.exp(jax.random.uniform(jax.random.fold_in(own, axis_at), (blocks,), jnp.float32, low / len(pieces), top_value / len(pieces)))
        level = level * jnp.repeat(draws, dims[axis_at] // blocks).reshape([-1 if axis == axis_at else 1 for axis in range(len(dims))])
    return level


def noise(own_key, shape, deviation, most, pieces=(), held_as=jnp.bfloat16):
    factor_of = level_of(own_key, shape, pieces, -0.22, 0.18) if pieces else 1.0
    array = jax.random.normal(own_key, shape, jnp.float32) * deviation * factor_of
    return jnp.minimum(jnp.maximum(array, -most), most).astype(held_as)


def setup_inputs(seed: int = 0) -> dict:
    splits = jax.random.split(jax.random.key(seed), 20)
    return {
        "tokens": noise(splits[0], (OBJECTS, SEQ, D), 1.0, 6.0, ((0, 4), (1, 32))),
        "camera": noise(splits[1], (OBJECTS, CAMD), 1.0, 6.0, ((0, 4),)),
        "features": noise(splits[2], (OBJECTS, PATCH, DINO), 1.0, 6.0, ((0, 4), (1, 32))),
        "foreground": draw_foreground(jax.random.fold_in(splits[19], 71), 0),
        "layout": draw_layout(jax.random.fold_in(splits[19], 71), 0),
        "modulation_weight": noise(splits[5], (CAMD, 2 * D), (4 * CAMD) ** -0.5, 0.09375),
        "modulation_bias": noise(splits[6], (2 * D,), 0.5, 3.0),
        "self_in_weight": noise(splits[7], (D, 3 * D), D ** -0.5, 0.25),
        "self_out_weight": noise(splits[8], (D, D), 64 ** -0.5, 0.75),
        "cross_norm_gain": jnp.clip(1.0 + 0.15 * jax.random.normal(splits[9], (D,), jnp.float32), 0.25, 1.75).astype(jnp.bfloat16),
        "cross_norm_bias": noise(splits[10], (D,), 0.3, 2.0),
        "cross_query_weight": noise(splits[11], (D, D), (D // 2) ** -0.5, 0.375),
        "cross_pair_weight": noise(splits[12], (DINO, 2 * D), (DINO // 2) ** -0.5, 0.4375),
        "cross_out_weight": noise(splits[13], (D, D), 64 ** -0.5, 0.75),
        "feed_norm_gain": jnp.clip(1.0 + 0.15 * jax.random.normal(splits[14], (D,), jnp.float32), 0.25, 1.75).astype(jnp.bfloat16),
        "feed_norm_bias": noise(splits[15], (D,), 0.3, 2.0),
        "up_weight": noise(splits[16], (D, FF), D ** -0.5, 0.25),
        "down_weight": noise(splits[17], (FF, D), FF ** -0.5, 0.125),
        "cotangent": noise(splits[18], (OBJECTS, SEQ, D), 1.0, 6.0, ((0, 4), (1, 32))),
    }


EPSILON = 1e-05
MASKED = -1e+30

@jax.custom_vjp
def low(v):
    return lax.optimization_barrier(v.astype(jnp.bfloat16)).astype(jnp.float32)

@jax.custom_vjp
def low_back(v):
    return v

def low_keep(v):
    return (low(v), None)

def low_pass(kept, grad):
    return (grad,)

def back_keep(v):
    return (v, None)

def back_low(kept, grad):
    return (low(grad),)
low.defvjp(low_keep, low_pass)
low_back.defvjp(back_keep, back_low)

def matmul(left, right):
    return jnp.dot(left, right, preferred_element_type=jnp.float32, precision=lax.Precision.HIGHEST)

def normalize(values):
    centre = lax.optimization_barrier(jnp.mean(values, axis=-1, keepdims=True))
    centred = values - centre
    spread = lax.optimization_barrier(jnp.mean(centred * centred, axis=-1, keepdims=True))
    return centred * lax.rsqrt(spread + EPSILON)

def token_keep(foreground, layout):
    patch_number = (layout - TRIB).astype(jnp.int32)
    match = patch_number[:, :, None] == jnp.arange(PATCHB, dtype=jnp.int32)[None, None, :]
    lit = lax.optimization_barrier(jnp.sum(jnp.where(match, foreground[:, None, :], 0), axis=-1))
    kept = jnp.logical_or(layout < TRIB, lit > 0)
    return jnp.repeat(kept, BLOCK, axis=1)

def attend(queries, keys, values, keep):
    rows = queries.shape[0]
    size = 512 if rows % 512 == 0 else rows
    scale_factor = HEAD_DIM ** (-0.5)
    key_heads = keys.reshape(keys.shape[0], HEADS, HEAD_DIM)
    value_heads = values.reshape(values.shape[0], HEADS, HEAD_DIM)

    def one_block(query_block):
        query_heads = query_block.reshape(size, HEADS, HEAD_DIM)
        scores = jnp.einsum('qhd,khd->hqk', query_heads, key_heads, precision=lax.Precision.HIGHEST) * scale_factor
        scores = low_back(scores)
        scores = jnp.where(keep[None, None, :] > 0.5, scores, MASKED)
        chances = low(jax.nn.softmax(scores, axis=-1))
        mixed = jnp.einsum('hqk,khd->qhd', chances, value_heads, precision=lax.Precision.HIGHEST)
        return mixed.reshape(size, HEADS * HEAD_DIM)
    blocks = queries.reshape(rows // size, size, queries.shape[1])
    return lax.map(jax.checkpoint(one_block), blocks).reshape(rows, queries.shape[1])

def forward(tokens_f, features_f, params, cam_act, keep):
    modulation_weight, modulation_bias, self_in_weight, self_out_weight, cross_norm_gain, cross_norm_bias, cross_query_weight, cross_pair_weight, cross_out_weight, feed_norm_gain, feed_norm_bias, up_weight, down_weight = params
    width = tokens_f.shape[1]
    modulation = matmul(cam_act[None, :], modulation_weight)[0] + modulation_bias
    hidden1 = low(normalize(tokens_f) * (1.0 + modulation[:width]) + modulation[width:])
    projected = low(low_back(matmul(hidden1, self_in_weight)))
    attended = attend(projected[:, :width], projected[:, width:2 * width], projected[:, 2 * width:], keep)
    attended = low(low_back(attended))
    after_self = tokens_f + low_back(matmul(attended, self_out_weight))
    hidden2 = low(normalize(after_self) * cross_norm_gain + cross_norm_bias)
    cross_queries = low(low_back(matmul(hidden2, cross_query_weight)))
    cross_pairs = low(low_back(matmul(features_f, cross_pair_weight)))
    every_patch = jnp.ones((features_f.shape[0],), jnp.float32)
    cross_mixed = attend(cross_queries, cross_pairs[:, :width], cross_pairs[:, width:], every_patch)
    cross_mixed = low(low_back(cross_mixed))
    after_cross = after_self + low_back(matmul(cross_mixed, cross_out_weight))
    hidden3 = low(normalize(after_cross) * feed_norm_gain + feed_norm_bias)
    pre_act = low_back(matmul(hidden3, up_weight))
    activated = low(jax.nn.gelu(pre_act, approximate=True))
    return after_cross + low_back(matmul(activated, down_weight))

def reference(tokens, camera, features, foreground, layout, modulation_weight, modulation_bias, self_in_weight, self_out_weight, cross_norm_gain, cross_norm_bias, cross_query_weight, cross_pair_weight, cross_out_weight, feed_norm_gain, feed_norm_bias, up_weight, down_weight, cotangent):
    keep = token_keep(foreground, layout).astype(jnp.float32)
    weights = tuple((item.astype(jnp.float32) for item in (modulation_weight, modulation_bias, self_in_weight, self_out_weight, cross_norm_gain, cross_norm_bias, cross_query_weight, cross_pair_weight, cross_out_weight, feed_norm_gain, feed_norm_bias, up_weight, down_weight)))

    def one_object(totals, item):
        item_tokens, item_camera, item_features, item_keep, item_cotangent = item
        cam_act = low(jax.nn.silu(item_camera.astype(jnp.float32)))

        def layer(tokens_f, features_f, *params):
            return forward(tokens_f, features_f, params, cam_act, item_keep)
        result, pull = jax.vjp(layer, item_tokens.astype(jnp.float32), item_features.astype(jnp.float32), *weights)
        gradients = pull(item_cotangent.astype(jnp.float32))
        totals = tuple((total + grad for total, grad in zip(totals, gradients[2:])))
        return (totals, (result, gradients[0], gradients[1]))
    start_totals = tuple((jnp.zeros_like(item) for item in weights))
    totals, outputs = lax.scan(one_object, start_totals, (tokens, camera, features, keep, cotangent))
    return (outputs[0], outputs[1], outputs[2], totals[0], totals[1], totals[2], totals[3], totals[4], totals[5], totals[6], totals[7], totals[8], totals[9], totals[10], totals[11], totals[12])
```

```python
import functools

import jax
import jax.numpy as jnp
from jax import lax
from jax.experimental import pallas as pl
from jax.experimental.pallas import tpu as pltpu
from jax.sharding import PartitionSpec as P

HEADS = 8
HEAD_DIM = 64
BLOCK = 128
TRIB = 24
PATCHB = 8
WIDTH = 512
PATCHES = 1024
TOKENS = 4096
EPSILON = 1e-05
MASKED = -1e30
SCALE = HEAD_DIM ** (-0.5)
BF = jnp.bfloat16
F32 = jnp.float32
AXES = ("batch", "seq")
PEERS = 32
QUARTERS = 4
SHARE = BLOCK // QUARTERS
MIB = 1024 * 1024


def nn(a, b):
    return lax.dot_general(a, b, (((1,), (0,)), ((), ())), preferred_element_type=F32)


def nt(a, b):
    return lax.dot_general(a, b, (((1,), (1,)), ((), ())), preferred_element_type=F32)


def tn(a, b):
    return lax.dot_general(a, b, (((0,), (0,)), ((), ())), preferred_element_type=F32)


def half_turn(values):
    return pltpu.roll(values, 64, 1)


def low_lanes(rows):
    return lax.broadcasted_iota(jnp.int32, (rows, 128), 1) < 64


def norm_parts(values):
    centre = jnp.mean(values, axis=-1, keepdims=True)
    centred = values - centre
    spread = jnp.mean(centred * centred, axis=-1, keepdims=True)
    inverse = lax.rsqrt(spread + EPSILON)
    return centred * inverse, inverse


def norm_back(normed, inverse, grad):
    first = jnp.mean(grad, axis=-1, keepdims=True)
    second = jnp.mean(grad * normed, axis=-1, keepdims=True)
    return inverse * (grad - first - normed * second)


def call(kernel, out_shape, inputs, scratch=(), flops=0, traffic=0, limit=48, smem=()):
    vmem = pl.BlockSpec(memory_space=pltpu.VMEM)
    scalar = pl.BlockSpec(memory_space=pltpu.SMEM)
    return pl.pallas_call(
        kernel,
        out_shape=out_shape,
        in_specs=[scalar if k in smem else vmem for k in range(len(inputs))],
        out_specs=jax.tree.map(lambda _: vmem, out_shape),
        scratch_shapes=list(scratch),
        compiler_params=pltpu.CompilerParams(vmem_limit_bytes=limit * MIB),
        cost_estimate=pl.CostEstimate(
            flops=int(flops), bytes_accessed=int(traffic), transcendentals=0
        ),
    )(*inputs)


def shape(dims, dtype=F32):
    return jax.ShapeDtypeStruct(dims, dtype)


def prepare_kernel(
    foreground, layout, tokens, features, camera, mod_weight, mod_bias, in_weight, message, modulation
):
    cam = camera[...].astype(F32)
    cam_act = (cam * jax.nn.sigmoid(cam)).astype(BF)
    mod = nn(jnp.broadcast_to(cam_act, (16, cam_act.shape[1])), mod_weight[...])[0:8]
    mod = mod + mod_bias[...].astype(F32)
    modulation[...] = mod
    block = layout[0, 0]
    lit = jnp.int32(0)
    for k in range(PATCHB):
        lit = lit + jnp.where(block - TRIB == k, foreground[0, k], 0)
    kept = jnp.logical_or(block < TRIB, lit > 0)
    bias = jnp.where(kept, jnp.float32(0.0), jnp.float32(MASKED))
    normed, _ = norm_parts(tokens[...].astype(F32))
    hidden = (normed * (1.0 + mod[0:1, :WIDTH]) + mod[0:1, WIDTH:]).astype(BF)
    projected = nn(hidden, in_weight[...]).astype(BF).astype(F32)
    low = low_lanes(BLOCK)
    for pair in range(HEADS // 2):
        at = 128 * pair
        query = projected[:, at : at + 128] * SCALE
        key = projected[:, WIDTH + at : WIDTH + at + 128]
        value = projected[:, 2 * WIDTH + at : 2 * WIDTH + at + 128]
        for odd in range(2):
            head = 2 * pair + odd
            if odd:
                both = jnp.where(low, half_turn(key), value)
                mine = jnp.where(low, half_turn(query), bias)
            else:
                both = jnp.where(low, key, half_turn(value))
                mine = jnp.where(low, query, bias)
            both = both.astype(BF)
            mine = mine.astype(BF)
            for quarter in range(QUARTERS):
                to = QUARTERS * head + quarter
                message[to, 0:128, :] = both
                message[to, 128:160, :] = mine[SHARE * quarter : SHARE * (quarter + 1)]
                for k in range(3):
                    message[to, 160 + 32 * k : 192 + 32 * k, :] = features[:, 128 * k : 128 * (k + 1)]


def gather_keys(received, masked_keys, pairs, queries):
    low = low_lanes(128)
    lane = lax.broadcasted_iota(jnp.int32, (128, 128), 1)
    lane_q = lax.broadcasted_iota(jnp.int32, (SHARE, 128), 1)
    for k in range(PEERS):
        both = received[k, 0:128, :].astype(F32)
        mine = received[k, 128:160, :].astype(F32)
        masked_keys[128 * k : 128 * (k + 1), :] = jnp.where(
            low, both, jnp.where(lane == 64, mine[0:1, :], 0.0)
        ).astype(BF)
        if pairs is not None:
            pairs[128 * k : 128 * (k + 1), :] = received[k, 0:128, :]
        queries[SHARE * k : SHARE * (k + 1), :] = jnp.where(
            lane_q < 64, mine, jnp.where(lane_q == 64, 1.0, 0.0)
        ).astype(BF)


KEYS = 512
ROWS = 256
QUERIES = PEERS * SHARE


def attend_kernel(received, message, attended, log_total, pairs_turned, masked_keys, queries, scores):
    gather_keys(received, masked_keys, None, queries)
    for k in range(PEERS):
        pairs_turned[:, 128 * k : 128 * (k + 1)] = jnp.transpose(
            received[k, 0:128, :].astype(F32)
        ).astype(BF)
    chunks = TOKENS // KEYS

    def tile(turn, carry):
        rows = pl.ds(pl.multiple_of(turn * ROWS, ROWS), ROWS)
        query = queries[rows, :]
        top = jnp.full((1, ROWS), -jnp.inf, F32)
        for k in range(chunks):
            part = nt(masked_keys[KEYS * k : KEYS * (k + 1), :], query)
            scores[KEYS * k : KEYS * (k + 1), :] = part
            top = jnp.maximum(top, jnp.max(part, axis=0, keepdims=True))
        total = jnp.zeros((1, ROWS), F32)
        mixed = jnp.zeros((128, ROWS), F32)
        for k in range(chunks):
            chance = jnp.exp(scores[KEYS * k : KEYS * (k + 1), :] - top)
            total = total + jnp.sum(chance, axis=0, keepdims=True)
            mixed = mixed + nn(pairs_turned[:, KEYS * k : KEYS * (k + 1)], chance.astype(BF))
        mixed = mixed / total
        attended[:, rows] = mixed[64:128, :]
        log_total[:, rows] = jnp.broadcast_to(top + jnp.log(total), (8, ROWS))
        turned = jnp.transpose(mixed)
        low = low_lanes(16)
        for k in range(ROWS // SHARE):
            first = turned[SHARE * k : SHARE * k + 16, :]
            second = turned[SHARE * k + 16 : SHARE * (k + 1), :]
            message[turn * (ROWS // SHARE) + k] = jnp.where(low, half_turn(first), second).astype(BF)
        return carry

    lax.fori_loop(0, QUERIES // ROWS, tile, 0)


def pairs_kernel(received, pair_weight, keys, values, keys_turned, values_turned, every, every_turned):
    for k in range(PEERS):
        for j in range(3):
            every[32 * k : 32 * (k + 1), 128 * j : 128 * (j + 1)] = received[
                k, 160 + 32 * j : 192 + 32 * j, :
            ]
    for k in range(PATCHES // 256):
        rows = slice(256 * k, 256 * (k + 1))
        part = every[rows, :]
        every_turned[:, rows] = jnp.transpose(part.astype(F32)).astype(BF)
        both = nn(part, pair_weight[...]).astype(BF)
        keys[rows, :] = both[:, :WIDTH]
        values[rows, :] = both[:, WIDTH:]
        turned = jnp.transpose(both.astype(F32)).astype(BF)
        keys_turned[:, rows] = turned[:WIDTH, :]
        values_turned[:, rows] = turned[WIDTH:, :]


def unpack_heads(received):
    low = low_lanes(16)
    columns = []
    for pair in range(HEADS // 2):
        pieces = []
        for quarter in range(QUARTERS):
            even = received[QUARTERS * (2 * pair) + quarter].astype(F32)
            odd = received[QUARTERS * (2 * pair + 1) + quarter].astype(F32)
            pieces.append(jnp.where(low, even, half_turn(odd)))
            pieces.append(jnp.where(low, half_turn(even), odd))
        columns.append(jnp.concatenate(pieces, axis=0))
    return jnp.concatenate(columns, axis=1)


def pack_heads(values, message):
    low = low_lanes(16)
    for pair in range(HEADS // 2):
        for quarter in range(QUARTERS):
            first = values[SHARE * quarter : SHARE * quarter + 16, 128 * pair : 128 * (pair + 1)]
            second = values[SHARE * quarter + 16 : SHARE * (quarter + 1), 128 * pair : 128 * (pair + 1)]
            message[QUARTERS * (2 * pair) + quarter] = jnp.where(
                low, first, half_turn(second)
            ).astype(BF)
            message[QUARTERS * (2 * pair + 1) + quarter] = jnp.where(
                low, half_turn(first), second
            ).astype(BF)


GELU = 0.7978845608028654
CUBE = 0.044715


def middle_kernel(
    received, tokens, keys, values_turned, self_out, gain_two, offset_two, query_weight, cross_out,
    gain_three, offset_three, up_weight, down_weight, cotangent,
    block_out, after_self, attended, cross_queries, cross_mixed, cross_log, cross_grad, feed_pack, vectors,
):
    attended_low = unpack_heads(received).astype(BF)
    attended[...] = attended_low
    first = tokens[...].astype(F32) + nn(attended_low, self_out[...])
    after_self[...] = first
    normed, _ = norm_parts(first)
    hidden2 = (normed * gain_two[...].astype(F32) + offset_two[...].astype(F32)).astype(BF)
    queries = nn(hidden2, query_weight[...]).astype(BF)
    cross_queries[...] = queries
    low = low_lanes(BLOCK)
    upper = lax.broadcasted_iota(jnp.int32, (128, BLOCK), 0) < 64
    pieces = []
    for pair in range(HEADS // 2):
        at = slice(128 * pair, 128 * (pair + 1))
        key = keys[:, at]
        value = values_turned[at, :]
        query = queries[:, at].astype(F32) * SCALE
        parts = []
        for odd in range(2):
            mine = jnp.where(low if odd == 0 else jnp.logical_not(low), query, 0.0).astype(BF)
            scores = nt(key, mine)
            top = jnp.max(scores, axis=0, keepdims=True)
            chance = jnp.exp(scores - top)
            total = jnp.sum(chance, axis=0, keepdims=True)
            cross_log[2 * pair + odd : 2 * pair + odd + 1, :] = top + jnp.log(total)
            parts.append(nn(value, (chance * (1.0 / total)).astype(BF)))
        pieces.append(jnp.transpose(jnp.where(upper, parts[0], parts[1])))
    mixed = jnp.concatenate(pieces, axis=1).astype(BF)
    cross_mixed[...] = mixed
    second = first + nn(mixed, cross_out[...])
    normed, inverse = norm_parts(second)
    gain = gain_three[...].astype(F32)
    hidden3 = (normed * gain + offset_three[...].astype(F32)).astype(BF)
    grad_low = cotangent[...]
    result = second
    back = jnp.zeros((BLOCK, WIDTH), F32)
    for k in range(4):
        at = slice(512 * k, 512 * (k + 1))
        pre = nn(hidden3, up_weight[:, at])
        square = pre * pre
        turn = jnp.tanh(GELU * (pre + CUBE * (square * pre)))
        half = 0.5 * (1.0 + turn)
        active = (pre * half).astype(BF)
        slope = half + (0.5 * pre) * (1.0 - turn * turn) * (GELU * (1.0 + (3.0 * CUBE) * square))
        result = result + nn(active, down_weight[at, :])
        pre_grad = (nt(grad_low, down_weight[at, :]) * slope).astype(BF)
        back = back + nt(pre_grad, up_weight[:, at])
        feed_pack[at, :] = tn(hidden3, pre_grad).astype(BF)
        feed_pack[2048 + 512 * k : 2048 + 512 * (k + 1), :] = tn(active, grad_low).astype(BF)
    block_out[...] = result
    cross_grad[...] = grad_low.astype(F32) + norm_back(normed, inverse, back * gain)
    vectors[0:1, :] = jnp.sum(back * normed, axis=0, keepdims=True)
    vectors[1:2, :] = jnp.sum(back, axis=0, keepdims=True)
    vectors[2:8, :] = jnp.zeros((6, WIDTH), F32)


def cross_back_kernel(
    after_self, cross_queries, cross_log, cross_grad, keys, keys_turned, values, cross_out,
    query_weight, self_out, gain_two,
    message, self_grad, self_branch, query_grad, key_grad, value_grad, vectors,
):
    grad = cross_grad[...]
    mixed_grad = nt(grad.astype(BF), cross_out[...]).astype(BF)
    low = low_lanes(BLOCK)
    upper = lax.broadcasted_iota(jnp.int32, (128, BLOCK), 0) < 64
    pieces = []
    for pair in range(HEADS // 2):
        at = slice(128 * pair, 128 * (pair + 1))
        key = keys[:, at]
        key_turned = keys_turned[at, :]
        value = values[:, at]
        query = cross_queries[:, at].astype(F32) * SCALE
        outer = mixed_grad[:, at].astype(F32)
        parts = []
        key_sum = None
        value_sum = None
        for odd in range(2):
            here = low if odd == 0 else jnp.logical_not(low)
            mine = jnp.where(here, query, 0.0).astype(BF)
            given = jnp.where(here, outer, 0.0).astype(BF)
            chance = jnp.exp(nt(key, mine) - cross_log[2 * pair + odd : 2 * pair + odd + 1, :])
            chance_grad = nt(value, given)
            inner = jnp.sum(chance * chance_grad, axis=0, keepdims=True)
            score_grad = (chance * (chance_grad - inner)).astype(BF)
            parts.append(nn(key_turned, score_grad))
            key_part = nn(score_grad, mine)
            value_part = nn(chance.astype(BF), given)
            key_sum = key_part if key_sum is None else key_sum + key_part
            value_sum = value_part if value_sum is None else value_sum + value_part
        key_grad[:, at] = key_sum.astype(BF)
        value_grad[:, at] = value_sum.astype(BF)
        pieces.append(jnp.transpose(jnp.where(upper, parts[0], parts[1])) * SCALE)
    low_grad = jnp.concatenate(pieces, axis=1).astype(BF)
    query_grad[...] = low_grad
    back = nt(low_grad, query_weight[...])
    normed, inverse = norm_parts(after_self[...])
    total = grad + norm_back(normed, inverse, back * gain_two[...].astype(F32))
    self_grad[...] = total
    branch = total.astype(BF)
    self_branch[...] = branch
    pack_heads(nt(branch, self_out[...]), message)
    vectors[0:1, :] = jnp.sum(back * normed, axis=0, keepdims=True)
    vectors[1:2, :] = jnp.sum(back, axis=0, keepdims=True)
    vectors[2:8, :] = jnp.zeros((6, WIDTH), F32)


def weights_kernel(
    after_self, attended, cross_mixed, cross_grad, query_grad, self_branch, key_grad, value_grad,
    every_turned, pair_weight, gain_two, offset_two,
    first_pack, second_pack, feature_part,
):
    normed, _ = norm_parts(after_self[...])
    hidden2 = (normed * gain_two[...].astype(F32) + offset_two[...].astype(F32)).astype(BF)
    first_pack[0:512, :] = tn(cross_mixed[...], cross_grad[...].astype(BF)).astype(BF)
    first_pack[512:1024, :] = tn(hidden2, query_grad[...]).astype(BF)
    first_pack[1024:1408, :] = nn(every_turned[...], key_grad[...]).astype(BF)
    first_pack[1408:1792, :] = nn(every_turned[...], value_grad[...]).astype(BF)
    second_pack[...] = tn(attended[...], self_branch[...]).astype(BF)
    for k in range(PATCHES // 256):
        rows = slice(256 * k, 256 * (k + 1))
        feature_part[rows, :] = (
            nt(key_grad[rows, :], pair_weight[:, :WIDTH]) + nt(value_grad[rows, :], pair_weight[:, WIDTH:])
        ).astype(BF)


def attend_back_kernel(
    received, pairs_turned, attended, log_total, given, feature_part, message,
    masked_keys, pairs, queries, outer, outer_row, chances, score_grads, query_sum,
):
    gather_keys(received, masked_keys, pairs, queries)
    low = low_lanes(16)
    for k in range(PEERS):
        piece = given[k].astype(F32)
        outer[SHARE * k : SHARE * k + 16, :] = jnp.where(low, 0.0, half_turn(piece)).astype(BF)
        outer[SHARE * k + 16 : SHARE * (k + 1), :] = jnp.where(low, 0.0, piece).astype(BF)
    for k in range(QUERIES // 256):
        rows = slice(256 * k, 256 * (k + 1))
        turned = jnp.transpose(outer[rows, :].astype(F32))[64:128, :]
        outer_row[:, rows] = jnp.broadcast_to(
            jnp.sum(turned * attended[:, rows], axis=0, keepdims=True), (8, 256)
        )
    query_sum[...] = jnp.zeros_like(query_sum)
    low_q = low_lanes(QUERIES)

    def chunk(turn, carry):
        at = pl.ds(pl.multiple_of(turn * KEYS, KEYS), KEYS)
        key = masked_keys[at, :]
        both = pairs[at, :]
        for k in range(QUERIES // ROWS):
            rows = slice(ROWS * k, ROWS * (k + 1))
            chance = jnp.exp(nt(key, queries[rows, :]) - log_total[0:1, rows])
            chance_grad = nt(both, outer[rows, :])
            chances[:, rows] = chance.astype(BF)
            score_grads[:, rows] = (chance * (chance_grad - outer_row[0:1, rows])).astype(BF)
        sums = nn(score_grads[...], queries[...]) + 0.0
        other = nn(chances[...], outer[...])
        sums = jnp.where(low_lanes(KEYS), sums, other).astype(BF)
        for k in range(KEYS // 128):
            message[turn * (KEYS // 128) + k, 0:128, :] = sums[128 * k : 128 * (k + 1), :]
        query_sum[...] += nn(pairs_turned[:, at], score_grads[...])
        return carry

    lax.fori_loop(0, TOKENS // KEYS, chunk, 0)
    for j in range(QUERIES // 256):
        turned = jnp.transpose(query_sum[:, 256 * j : 256 * (j + 1)]) * SCALE
        for k in range(256 // SHARE):
            first = turned[SHARE * k : SHARE * k + 16, :]
            second = turned[SHARE * k + 16 : SHARE * (k + 1), :]
            message[8 * j + k, 128:144, :] = jnp.where(low, first, half_turn(second)).astype(BF)
    for k in range(PEERS):
        for j in range(3):
            message[k, 144 + 32 * j : 176 + 32 * j, :] = feature_part[
                32 * k : 32 * (k + 1), 128 * j : 128 * (j + 1)
            ]


def finish_kernel(
    place, received, tokens, camera, modulation, self_grad, in_weight, vectors_two, vectors_three,
    token_grad, feature_grad, second_pack, small_pack,
):
    low = low_lanes(BLOCK)
    queries = []
    keys = []
    values = []
    for pair in range(HEADS // 2):
        sums = []
        for odd in range(2):
            head = 2 * pair + odd
            total = received[QUARTERS * head, 0:128, :].astype(F32)
            for quarter in range(1, QUARTERS):
                total = total + received[QUARTERS * head + quarter, 0:128, :].astype(F32)
            sums.append(total)
        keys.append(jnp.where(low, sums[0], half_turn(sums[1])))
        values.append(jnp.where(low, half_turn(sums[0]), sums[1]))
        low_half = low_lanes(16)
        pieces = []
        for quarter in range(QUARTERS):
            even = received[QUARTERS * (2 * pair) + quarter, 128:144, :].astype(F32)
            odd = received[QUARTERS * (2 * pair + 1) + quarter, 128:144, :].astype(F32)
            pieces.append(jnp.where(low_half, even, half_turn(odd)))
            pieces.append(jnp.where(low_half, half_turn(even), odd))
        queries.append(jnp.concatenate(pieces, axis=0))
    total = received[0, 144:240, :].astype(F32)
    for k in range(1, PEERS):
        total = total + received[k, 144:240, :].astype(F32)
    for j in range(3):
        feature_grad[:, 128 * j : 128 * (j + 1)] = total[32 * j : 32 * (j + 1), :]
    parts = [jnp.concatenate(p, axis=1).astype(BF) for p in (queries, keys, values)]
    normed, inverse = norm_parts(tokens[...].astype(F32))
    scale = 1.0 + modulation[0:1, :WIDTH]
    hidden = (normed * scale + modulation[0:1, WIDTH:]).astype(BF)
    back = jnp.zeros((BLOCK, WIDTH), F32)
    for k in range(3):
        at = slice(WIDTH * k, WIDTH * (k + 1))
        back = back + nt(parts[k], in_weight[:, at])
        second_pack[at, :] = tn(hidden, parts[k]).astype(BF)
    token_grad[...] = self_grad[...] + norm_back(normed, inverse, back * scale)
    scale_grad = jnp.sum(back * normed, axis=0, keepdims=True)
    shift_grad = jnp.sum(back, axis=0, keepdims=True)
    cam = camera[...].astype(F32)
    cam_act = cam * jax.nn.sigmoid(cam)
    row = lax.broadcasted_iota(jnp.int32, (32, WIDTH), 0)
    item = place[0]
    first = place[1] == 0
    small = jnp.where(row == 2 * item, scale_grad, 0.0)
    small = small + jnp.where(row == 2 * item + 1, shift_grad, 0.0)
    small = small + jnp.where(jnp.logical_and(first, row == 8 + 2 * item), cam_act[:, :WIDTH], 0.0)
    small = small + jnp.where(jnp.logical_and(first, row == 9 + 2 * item), cam_act[:, WIDTH:], 0.0)
    small = small + jnp.where(row == 16, vectors_two[0:1, :], 0.0)
    small = small + jnp.where(row == 17, vectors_two[1:2, :], 0.0)
    small = small + jnp.where(row == 18, vectors_three[0:1, :], 0.0)
    small = small + jnp.where(row == 19, vectors_three[1:2, :], 0.0)
    small_pack[0:32, :] = small.astype(BF)
    small_pack[32:256, :] = jnp.zeros((224, WIDTH), BF)


def index_of(x, y, z, core):
    return ((z % 2) * 2 + core) * 32 + (y * 4 + x) * 2 + z // 2


CHIPS = [(x, y, z) for x in range(4) for y in range(4) for z in range(4)]
SAME_CORE = [[index_of(*chip, core) for chip in CHIPS] for core in range(2)]
OTHER_CORE = [
    (index_of(*chip, core), index_of(*chip, 1 - core)) for chip in CHIPS for core in range(2)
]


def exchange(message):
    return lax.all_to_all(message, "seq", 0, 0, tiled=True)


def add_everywhere(first, second):
    core = lax.axis_index("batch") % 2
    mine = jnp.where(core == 0, first, second)
    other = lax.ppermute(jnp.where(core == 0, second, first), AXES, OTHER_CORE)
    both = (mine.astype(F32) + other.astype(F32)).astype(BF)
    rows = both.shape[0] // 64
    pieces = lax.all_to_all(
        both.reshape(64, rows, WIDTH), AXES, 0, 0, tiled=True, axis_index_groups=SAME_CORE
    )
    total = jnp.sum(pieces.astype(F32), axis=0).astype(BF)
    pieces = lax.all_to_all(
        jnp.broadcast_to(total[None], (64, rows, WIDTH)),
        AXES, 0, 0, tiled=True, axis_index_groups=SAME_CORE,
    ).reshape(64 * rows, WIDTH)
    other = lax.ppermute(pieces, AXES, OTHER_CORE)
    return jnp.where(core == 0, pieces, other), jnp.where(core == 0, other, pieces)


def body(
    tokens, camera, features, foreground, layout, modulation_weight, modulation_bias,
    self_in_weight, self_out_weight, cross_norm_gain, cross_norm_bias, cross_query_weight,
    cross_pair_weight, cross_out_weight, feed_norm_gain, feed_norm_bias, up_weight, down_weight,
    cotangent,
):
    tokens = tokens[0]
    features = features[0]
    cotangent = cotangent[0]
    row = lambda v: v.reshape(1, -1)
    gain_two, offset_two = row(cross_norm_gain), row(cross_norm_bias)
    gain_three, offset_three = row(feed_norm_gain), row(feed_norm_bias)

    message, modulation = call(
        prepare_kernel,
        (shape((PEERS, 256, 128), BF), shape((8, 1024))),
        (foreground, layout, tokens, features, camera, modulation_weight, row(modulation_bias), self_in_weight),
        flops=1e9, traffic=8e6, smem=(0, 1),
    )
    received = exchange(message)
    message, attended_turned, log_total, pairs_turned = call(
        attend_kernel,
        (shape((PEERS, 16, 128), BF), shape((64, QUERIES)), shape((8, QUERIES)), shape((128, TOKENS), BF)),
        (received,),
        scratch=(
            pltpu.VMEM((TOKENS, 128), BF), pltpu.VMEM((QUERIES, 128), BF), pltpu.VMEM((TOKENS, ROWS), F32),
        ),
        flops=9e9, traffic=4e6,
    )
    back = exchange(message)
    keys, values, keys_turned, values_turned, every, every_turned = call(
        pairs_kernel,
        (
            shape((PATCHES, WIDTH), BF), shape((PATCHES, WIDTH), BF), shape((WIDTH, PATCHES), BF),
            shape((WIDTH, PATCHES), BF), shape((PATCHES, 384), BF), shape((384, PATCHES), BF),
        ),
        (received, cross_pair_weight),
        flops=3e9, traffic=8e6,
    )
    (
        block_out, after_self, attended, cross_queries, cross_mixed, cross_log, cross_grad, feed_pack, vectors_three,
    ) = call(
        middle_kernel,
        (
            shape((BLOCK, WIDTH)), shape((BLOCK, WIDTH)), shape((BLOCK, WIDTH), BF), shape((BLOCK, WIDTH), BF),
            shape((BLOCK, WIDTH), BF), shape((HEADS, BLOCK)), shape((BLOCK, WIDTH)), shape((4096, WIDTH), BF),
            shape((8, WIDTH)),
        ),
        (
            back, tokens, keys, values_turned, self_out_weight, gain_two, offset_two, cross_query_weight,
            cross_out_weight, gain_three, offset_three, up_weight, down_weight, cotangent,
        ),
        flops=1e10, traffic=1.5e7,
    )
    feed_total = lax.psum(feed_pack, AXES)
    message, self_grad, self_branch, query_grad, key_grad, value_grad, vectors_two = call(
        cross_back_kernel,
        (
            shape((PEERS, 16, 128), BF), shape((BLOCK, WIDTH)), shape((BLOCK, WIDTH), BF),
            shape((BLOCK, WIDTH), BF), shape((PATCHES, WIDTH), BF), shape((PATCHES, WIDTH), BF),
            shape((8, WIDTH)),
        ),
        (
            after_self, cross_queries, cross_log, cross_grad, keys, keys_turned, values, cross_out_weight,
            cross_query_weight, self_out_weight, gain_two,
        ),
        flops=6e9, traffic=8e6,
    )
    given = exchange(message)
    first_pack, self_out_pack, feature_part = call(
        weights_kernel,
        (shape((1792, WIDTH), BF), shape((WIDTH, WIDTH), BF), shape((PATCHES, 384), BF)),
        (
            after_self, attended, cross_mixed, cross_grad, query_grad, self_branch, key_grad, value_grad,
            every_turned, cross_pair_weight, gain_two, offset_two,
        ),
        flops=4e9, traffic=8e6,
    )
    message = call(
        attend_back_kernel,
        shape((PEERS, 240, 128), BF),
        (received, pairs_turned, attended_turned, log_total, given, feature_part),
        scratch=(
            pltpu.VMEM((TOKENS, 128), BF), pltpu.VMEM((TOKENS, 128), BF), pltpu.VMEM((QUERIES, 128), BF),
            pltpu.VMEM((QUERIES, 128), BF), pltpu.VMEM((8, QUERIES), F32), pltpu.VMEM((KEYS, QUERIES), BF),
            pltpu.VMEM((KEYS, QUERIES), BF), pltpu.VMEM((128, QUERIES), F32),
        ),
        flops=1.6e10, traffic=8e6,
    )
    received = exchange(message)
    place = jnp.stack([lax.axis_index("batch"), lax.axis_index("seq")]).astype(jnp.int32)
    token_grad, feature_grad, self_in_pack, small_pack = call(
        finish_kernel,
        (
            shape((BLOCK, WIDTH)), shape((32, 384)), shape((3 * WIDTH, WIDTH), BF), shape((256, WIDTH), BF),
        ),
        (
            place, received, tokens, camera, modulation, self_grad, self_in_weight, vectors_two, vectors_three,
        ),
        flops=3e9, traffic=8e6, smem=(0,),
    )
    first, second = add_everywhere(
        jnp.concatenate((first_pack, small_pack), axis=0),
        jnp.concatenate((self_out_pack, self_in_pack), axis=0),
    )
    small = first[1792:1824].astype(F32)
    mod_grad = small[0:8].reshape(4, 1024)
    cam_act = small[8:16].reshape(4, 1024)
    mod_weight_grad = jnp.sum(cam_act[:, :, None] * mod_grad[:, None, :], axis=0)
    wide = lambda pack, count: jnp.concatenate(
        [p for p in jnp.split(pack, count, axis=0)], axis=1
    ).astype(F32)
    return (
        block_out[None],
        token_grad[None],
        feature_grad[None],
        mod_weight_grad,
        jnp.sum(mod_grad, axis=0),
        wide(second[512:], 3),
        second[:512].astype(F32),
        small[16],
        small[17],
        first[512:1024].astype(F32),
        wide(first[1024:1792], 2),
        first[0:512].astype(F32),
        small[18],
        small[19],
        wide(feed_total[:2048], 4),
        feed_total[2048:].astype(F32),
    )


def solution(mesh):
    split = P("batch", "seq", None)
    in_specs = (
        (split, P("batch", None), split, P("batch", None), P("batch", "seq")) + (P(),) * 13 + (split,)
    )
    out_specs = (split,) * 3 + (P(),) * 13
    return jax.shard_map(body, mesh=mesh, in_specs=in_specs, out_specs=out_specs, check_vma=False)
```

```python
import functools

import jax
import jax.numpy as jnp
from jax import lax
from jax.experimental import pallas as pl
from jax.experimental.pallas import tpu as pltpu
from jax.sharding import PartitionSpec as P

HEADS = 8
HEAD_DIM = 64
BLOCK = 128
TRIB = 24
PATCHB = 8
WIDTH = 512
PATCHES = 1024
TOKENS = 4096
EPSILON = 1e-05
MASKED = -1e30
SCALE = HEAD_DIM ** (-0.5)
BF = jnp.bfloat16
F32 = jnp.float32
AXES = ("batch", "seq")
PEERS = 32
QUARTERS = 4
SHARE = BLOCK // QUARTERS
MIB = 1024 * 1024


def nn(a, b):
    return lax.dot_general(a, b, (((1,), (0,)), ((), ())), preferred_element_type=F32)


def nt(a, b):
    return lax.dot_general(a, b, (((1,), (1,)), ((), ())), preferred_element_type=F32)


def tn(a, b):
    return lax.dot_general(a, b, (((0,), (0,)), ((), ())), preferred_element_type=F32)


def half_turn(values):
    return pltpu.roll(values, 64, 1)


def low_lanes(rows):
    return lax.broadcasted_iota(jnp.int32, (rows, 128), 1) < 64


def norm_parts(values):
    centre = jnp.mean(values, axis=-1, keepdims=True)
    centred = values - centre
    spread = jnp.mean(centred * centred, axis=-1, keepdims=True)
    inverse = lax.rsqrt(spread + EPSILON)
    return centred * inverse, inverse


def norm_back(normed, inverse, grad):
    first = jnp.mean(grad, axis=-1, keepdims=True)
    second = jnp.mean(grad * normed, axis=-1, keepdims=True)
    return inverse * (grad - first - normed * second)


class Late:
    def __init__(self, copy, ref):
        self.copy, self.ref, self.here, self.shape = copy, ref, False, ref.shape

    def ready(self):
        if not self.here:
            self.copy.wait()
            self.here = True
        return self.ref

    def __getitem__(self, index):
        return self.ready()[index]


class Away:
    def __init__(self, ref, copy):
        self.ref, self.copy, self.sent, self.shape = ref, copy, False, ref.shape

    def __setitem__(self, index, value):
        self.ref[index] = value

    def send(self):
        if not self.sent:
            self.copy.start()
            self.sent = True


def call(
    kernel, out_shape, inputs, scratch=(), flops=0, traffic=0, limit=32, smem=(), late=(), away=(), far_out=(),
    far_in=(), aliases=None,
):
    vmem = pl.BlockSpec(memory_space=pltpu.VMEM)
    scalar = pl.BlockSpec(memory_space=pltpu.SMEM)
    far = pl.BlockSpec(memory_space=pltpu.HBM)
    single = not isinstance(out_shape, tuple)
    outs = (out_shape,) if single else out_shape
    count, extra = len(inputs), len(scratch)
    def whole(*refs):
        refs = list(refs)
        ins, results = refs[:count], refs[count : count + len(outs)]
        rest = refs[count + len(outs) :]
        mine, buffers = rest[:extra], rest[extra:]
        semaphores = buffers[-1] if late or away else None
        for k, which in enumerate(late):
            copy = pltpu.make_async_copy(ins[which], buffers[k], semaphores.at[k])
            copy.start()
            ins[which] = Late(copy, buffers[k])
        for k, which in enumerate(away):
            buffer = buffers[len(late) + k]
            results[which] = Away(
                buffer, pltpu.make_async_copy(buffer, results[which], semaphores.at[len(late) + k])
            )
        kernel(*ins, *results, *mine)
        for which in late:
            ins[which].ready()
        for which in away:
            results[which].send()
        for which in away:
            results[which].copy.wait()

    buffers = [pltpu.VMEM(inputs[k].shape, inputs[k].dtype) for k in late]
    buffers += [pltpu.VMEM(outs[k].shape, outs[k].dtype) for k in away]
    if buffers:
        buffers.append(pltpu.SemaphoreType.DMA((len(buffers),)))
    out_specs = tuple(far if k in away or k in far_out else vmem for k in range(len(outs)))
    return pl.pallas_call(
        whole,
        out_shape=out_shape,
        in_specs=[scalar if k in smem else far if k in late or k in far_in else vmem for k in range(count)],
        out_specs=out_specs[0] if single else out_specs,
        scratch_shapes=list(scratch) + buffers,
        input_output_aliases=aliases or {},
        compiler_params=pltpu.CompilerParams(vmem_limit_bytes=limit * MIB),
        cost_estimate=pl.CostEstimate(
            flops=int(flops), bytes_accessed=int(traffic), transcendentals=0
        ),
    )(*inputs)


def shape(dims, dtype=F32):
    return jax.ShapeDtypeStruct(dims, dtype)


def prepare_kernel(
    foreground, layout, tokens, features, camera, mod_weight, mod_bias, in_weight,
    far_message, modulation, message, semaphores,
):
    for to in range(PEERS):
        for k in range(3):
            message[to, 160 + 32 * k : 192 + 32 * k, :] = features[:, 128 * k : 128 * (k + 1)]
    cam = camera[...].astype(F32)
    cam_act = (cam * jax.nn.sigmoid(cam)).astype(BF)
    mod = nn(jnp.broadcast_to(cam_act, (16, cam_act.shape[1])), mod_weight[...])[0:8]
    mod = mod + mod_bias[...].astype(F32).reshape(1, 2 * WIDTH)
    modulation[...] = mod
    block = layout[0, 0]
    lit = jnp.int32(0)
    for k in range(PATCHB):
        lit = lit + jnp.where(block - TRIB == k, foreground[0, k], 0)
    kept = jnp.logical_or(block < TRIB, lit > 0)
    bias = jnp.where(kept, jnp.float32(0.0), jnp.float32(MASKED))
    normed, _ = norm_parts(tokens[...].astype(F32))
    hidden = (normed * (1.0 + mod[0:1, :WIDTH]) + mod[0:1, WIDTH:]).astype(BF)
    projected = nn(hidden, in_weight[...]).astype(BF).astype(F32)
    low = low_lanes(BLOCK)
    for pair in range(HEADS // 2):
        at = 128 * pair
        query = projected[:, at : at + 128] * SCALE
        key = projected[:, WIDTH + at : WIDTH + at + 128]
        value = projected[:, 2 * WIDTH + at : 2 * WIDTH + at + 128]
        for odd in range(2):
            head = 2 * pair + odd
            if odd:
                both = jnp.where(low, half_turn(key), value)
                mine = jnp.where(low, half_turn(query), bias)
            else:
                both = jnp.where(low, key, half_turn(value))
                mine = jnp.where(low, query, bias)
            both = both.astype(BF)
            mine = mine.astype(BF)
            for quarter in range(QUARTERS):
                to = QUARTERS * head + quarter
                message[to, 0:128, :] = both
                message[to, 128:160, :] = mine[SHARE * quarter : SHARE * (quarter + 1)]
            some = slice(QUARTERS * head, QUARTERS * (head + 1))
            pltpu.make_async_copy(message.at[some], far_message.at[some], semaphores.at[head]).start()
    for head in range(HEADS):
        some = slice(QUARTERS * head, QUARTERS * (head + 1))
        pltpu.make_async_copy(message.at[some], far_message.at[some], semaphores.at[head]).wait()


def loop(count, work, unroll=1):
    def turn(k, carry):
        work(k)
        return carry

    lax.fori_loop(0, count, turn, 0, unroll=unroll)


def block_of(k, size):
    return pl.ds(pl.multiple_of(k * size, size), size)


def gather_keys(received, masked_keys, pairs, queries, turned):
    low = low_lanes(128)
    lane = lax.broadcasted_iota(jnp.int32, (128, 128), 1)
    lane_q = lax.broadcasted_iota(jnp.int32, (SHARE, 128), 1)

    def gather(k):
        at = block_of(k, 128)
        both = received[k, 0:128, :].astype(F32)
        mine = received[k, 128:160, :].astype(F32)
        masked_keys[at, :] = jnp.where(low, both, jnp.where(lane == 64, mine[0:1, :], 0.0)).astype(BF)
        if pairs is not None:
            pairs[at, :] = received[k, 0:128, :]
        if turned is not None:
            turned[:, at] = jnp.transpose(both).astype(BF)
        queries[block_of(k, SHARE), :] = jnp.where(
            lane_q < 64, mine, jnp.where(lane_q == 64, 1.0, 0.0)
        ).astype(BF)

    loop(PEERS, gather, 4)


KEYS = 512
ROWS = 1024
UNROLL_A = 1
UNROLL_B = 2
UNROLL_C = 1
BACK_KEYS = 1024
BACK_ROWS = 256
QUERIES = PEERS * SHARE


def attend_kernel(
    received, message, attended, log_total, pairs_turned, masked_keys, queries, scores, mixed, turned
):
    gather_keys(received, masked_keys, None, queries, pairs_turned)
    chunks = TOKENS // KEYS
    query = queries[...]

    def score(k, top):
        at = block_of(k, KEYS)
        part = nt(masked_keys[at, :], query)
        scores[at, :] = part
        return jnp.maximum(top, jnp.max(part, axis=0, keepdims=True))

    top = lax.fori_loop(0, chunks, score, jnp.full((1, ROWS), -jnp.inf, F32), unroll=UNROLL_A)
    mixed[...] = jnp.zeros_like(mixed)

    def mix(k, total):
        at = block_of(k, KEYS)
        chance = jnp.exp(scores[at, :] - top)
        mixed[...] += nn(pairs_turned[:, at], chance.astype(BF))
        return total + jnp.sum(chance, axis=0, keepdims=True)

    total = lax.fori_loop(0, chunks, mix, jnp.zeros((1, ROWS), F32), unroll=UNROLL_B)
    result = mixed[...] / total
    attended[...] = result[64:128, :]
    log_total[...] = jnp.broadcast_to(top + jnp.log(total), (8, ROWS))
    turned[...] = jnp.transpose(result)
    low = low_lanes(16)

    def pack(k):
        first = turned[pl.ds(pl.multiple_of(SHARE * k, 16), 16), :]
        second = turned[pl.ds(pl.multiple_of(SHARE * k + 16, 16), 16), :]
        message[k] = jnp.where(low, half_turn(first), second).astype(BF)

    loop(PEERS, pack, 4)


def pairs_kernel(received, pair_weight, keys, values, keys_turned, values_turned, every_turned, every):
    pair_weight = pair_weight.ready()

    def gather(k):
        for j in range(3):
            every[block_of(k, 32), 128 * j : 128 * (j + 1)] = received[k, 160 + 32 * j : 192 + 32 * j, :]

    def project(k):
        rows = block_of(k, 256)
        part = every[rows, :]
        every_turned.ref[:, rows] = jnp.transpose(part.astype(F32)).astype(BF)
        both = nn(part, pair_weight[...]).astype(BF)
        keys.ref[rows, :] = both[:, :WIDTH]
        values.ref[rows, :] = both[:, WIDTH:]
        turned = jnp.transpose(both.astype(F32)).astype(BF)
        keys_turned.ref[:, rows] = turned[:WIDTH, :]
        values_turned.ref[:, rows] = turned[WIDTH:, :]

    loop(PEERS, gather, 4)
    loop(PATCHES // 256, project)


def unpack_heads(received):
    low = low_lanes(16)
    columns = []
    for pair in range(HEADS // 2):
        pieces = []
        for quarter in range(QUARTERS):
            even = received[QUARTERS * (2 * pair) + quarter].astype(F32)
            odd = received[QUARTERS * (2 * pair + 1) + quarter].astype(F32)
            pieces.append(jnp.where(low, even, half_turn(odd)))
            pieces.append(jnp.where(low, half_turn(even), odd))
        columns.append(jnp.concatenate(pieces, axis=0))
    return jnp.concatenate(columns, axis=1)


def pack_heads(values, message):
    low = low_lanes(16)
    for pair in range(HEADS // 2):
        for quarter in range(QUARTERS):
            first = values[SHARE * quarter : SHARE * quarter + 16, 128 * pair : 128 * (pair + 1)]
            second = values[SHARE * quarter + 16 : SHARE * (quarter + 1), 128 * pair : 128 * (pair + 1)]
            message[QUARTERS * (2 * pair) + quarter] = jnp.where(
                low, first, half_turn(second)
            ).astype(BF)
            message[QUARTERS * (2 * pair + 1) + quarter] = jnp.where(
                low, half_turn(first), second
            ).astype(BF)


GELU = 0.7978845608028654
CUBE = 0.044715


def put(place, keep, send, owner, rows, value):
    @pl.when(place[0] == owner)
    def _():
        keep[rows, :] = value

    @pl.when(place[0] != owner)
    def _():
        send[rows, :] = value


def middle_kernel(
    place, received, tokens, keys, keys_turned, values, values_turned, self_out, gain_two, offset_two,
    query_weight, cross_out, gain_three, offset_three, up_weight, down_weight, cotangent, every_turned, pair_weight,
    block_out, feed_keep, feed_send, vectors, message, self_grad, feature_part, pair_value,
    feed_pack, semaphores, key_all, value_all, total_out, total_back,
):
    def move(start, rows, to, slot):
        at = slice(to, to + rows)

        @pl.when(place[0] == 0)
        def _():
            pltpu.make_async_copy(feed_pack.at[0, start : start + rows], feed_keep.at[at], semaphores.at[slot, 0]).start()
            pltpu.make_async_copy(feed_pack.at[1, start : start + rows], feed_send.at[at], semaphores.at[slot, 1]).start()

        @pl.when(place[0] != 0)
        def _():
            pltpu.make_async_copy(feed_pack.at[1, start : start + rows], feed_keep.at[at], semaphores.at[slot, 0]).start()
            pltpu.make_async_copy(feed_pack.at[0, start : start + rows], feed_send.at[at], semaphores.at[slot, 1]).start()

    def put_halves(start, value):
        rows = value.shape[0] // 2
        feed_pack[0, start : start + rows, :] = value[:rows]
        feed_pack[1, start : start + rows, :] = value[rows:]

    attended_low = unpack_heads(received).astype(BF)
    first = tokens[...].astype(F32) + nn(attended_low, self_out[...])
    normed_two, inverse_two = norm_parts(first)
    gain = gain_two[...].astype(F32)
    hidden = (normed_two * gain + offset_two[...].astype(F32)).astype(BF)
    queries = nn(hidden, query_weight[...]).astype(BF).astype(F32) * SCALE
    low = low_lanes(BLOCK)
    upper = lax.broadcasted_iota(jnp.int32, (128, BLOCK), 0) < 64
    masked = []
    chances = []
    pieces = []
    for pair in range(HEADS // 2):
        at = slice(128 * pair, 128 * (pair + 1))
        key = keys[:, at]
        value = values_turned[at, :]
        parts = []
        for odd in range(2):
            mine = jnp.where(low if odd == 0 else jnp.logical_not(low), queries[:, at], 0.0).astype(BF)
            scores = nt(key, mine)
            chance = jnp.exp(scores - jnp.max(scores, axis=0, keepdims=True))
            chance = chance * (1.0 / jnp.sum(chance, axis=0, keepdims=True))
            masked.append(mine)
            chances.append(chance)
            parts.append(nn(value, chance.astype(BF)))
        pieces.append(jnp.transpose(jnp.where(upper, parts[0], parts[1])))
    mixed = jnp.concatenate(pieces, axis=1).astype(BF)
    second = first + nn(mixed, cross_out[...])
    normed, inverse = norm_parts(second)
    gain_out = gain_three[...].astype(F32)
    hidden3 = (normed * gain_out + offset_three[...].astype(F32)).astype(BF)
    grad_low = cotangent[...]
    total_out[...] = second
    total_back[...] = jnp.zeros((BLOCK, WIDTH), F32)
    up_all, down_all = up_weight.ready(), down_weight.ready()

    def feed_block(k, carry):
        at = pl.ds(pl.multiple_of(512 * k, 512), 512)
        up, down = up_all[:, at], down_all[at, :]
        pre = nn(hidden3, up)
        square = pre * pre
        turn = jnp.tanh(GELU * (pre + CUBE * (square * pre)))
        half = 0.5 * (1.0 + turn)
        active = (pre * half).astype(BF)
        slope = half + (0.5 * pre) * (1.0 - turn * turn) * (GELU * (1.0 + (3.0 * CUBE) * square))
        total_out[...] += nn(active, down)
        pre_grad = (nt(grad_low, down) * slope).astype(BF)
        total_back[...] += nt(pre_grad, up)
        grad = tn(hidden3, pre_grad).astype(BF)
        feed_pack[0, pl.ds(pl.multiple_of(256 * k, 256), 256), :] = grad[:256]
        feed_pack[1, pl.ds(pl.multiple_of(256 * k, 256), 256), :] = grad[256:]
        feed_pack[k // 2, pl.ds(pl.multiple_of(1024 + 512 * (k % 2), 512), 512), :] = tn(active, grad_low).astype(BF)
        return carry

    lax.fori_loop(0, 4, feed_block, 0, unroll=1)
    result = total_out[...]
    back = total_back[...]
    move(0, 2048, 0, 0)
    block_out[...] = result
    vectors[2:3, :] = jnp.sum(back * normed, axis=0, keepdims=True)
    vectors[3:4, :] = jnp.sum(back, axis=0, keepdims=True)
    grad = grad_low.astype(F32) + norm_back(normed, inverse, back * gain_out)
    branch = grad.astype(BF)
    put_halves(2048, tn(mixed, branch).astype(BF))
    mixed_grad = nt(branch, cross_out[...]).astype(BF).astype(F32)
    pieces = []
    pair_low = []
    for pair in range(HEADS // 2):
        at = slice(128 * pair, 128 * (pair + 1))
        value = values[:, at]
        key_turned = keys_turned[at, :]
        parts = []
        key_sum = None
        value_sum = None
        for odd in range(2):
            head = 2 * pair + odd
            given = jnp.where(low if odd == 0 else jnp.logical_not(low), mixed_grad[:, at], 0.0).astype(BF)
            chance = chances[head]
            chance_grad = nt(value, given)
            inner = jnp.sum(chance * chance_grad, axis=0, keepdims=True)
            score_grad = (chance * (chance_grad - inner)).astype(BF)
            parts.append(nn(key_turned, score_grad))
            key_part = nn(score_grad, masked[head])
            value_part = nn(chance.astype(BF), given)
            key_sum = key_part if key_sum is None else key_sum + key_part
            value_sum = value_part if value_sum is None else value_sum + value_part
        pair_low.append((key_sum.astype(BF), value_sum.astype(BF)))
        pieces.append(jnp.transpose(jnp.where(upper, parts[0], parts[1])) * SCALE)
    low_grad = jnp.concatenate(pieces, axis=1).astype(BF)
    back = nt(low_grad, query_weight[...])
    vectors[0:1, :] = jnp.sum(back * normed_two, axis=0, keepdims=True)
    vectors[1:2, :] = jnp.sum(back, axis=0, keepdims=True)
    vectors[4:8, :] = jnp.zeros((4, WIDTH), F32)
    grad = grad + norm_back(normed_two, inverse_two, back * gain)
    self_grad[...] = grad
    branch = grad.astype(BF)
    pack_heads(nt(branch, self_out[...]), message)
    put_halves(2304, tn(hidden, low_grad).astype(BF))
    put_halves(2560, tn(attended_low, branch).astype(BF))
    key_grad = jnp.concatenate([p[0] for p in pair_low], axis=1)
    value_grad = jnp.concatenate([p[1] for p in pair_low], axis=1)
    put_halves(2816, nn(every_turned[...], key_grad).astype(BF))
    pair_value[...] = nn(every_turned[...], value_grad).astype(BF)
    feed_pack[0, 3008:3072, :] = jnp.zeros((64, WIDTH), BF)
    feed_pack[1, 3008:3072, :] = jnp.zeros((64, WIDTH), BF)
    move(2048, 1024, 2048, 1)
    def feature_block(k, carry):
        rows = pl.ds(pl.multiple_of(256 * k, 256), 256)
        part = (nt(key_all[rows, :], pair_keys) + nt(value_all[rows, :], pair_values)).astype(BF)
        for i in range(8):
            for j in range(3):
                feature_part[8 * k + i, 32 * j : 32 * (j + 1), :] = part[
                    32 * i : 32 * (i + 1), 128 * j : 128 * (j + 1)
                ]
        return carry

    pair_keys, pair_values = pair_weight[:, :WIDTH], pair_weight[:, WIDTH:]
    key_all[...] = key_grad
    value_all[...] = value_grad
    lax.fori_loop(0, PATCHES // 256, feature_block, 0)
    for slot, rows in enumerate((2048, 1024)):
        for k in range(2):
            pltpu.make_async_copy(
                feed_pack.at[0, 0:rows], feed_keep.at[0:rows], semaphores.at[slot, k]
            ).wait()


def put_halves(place, keep, send, start, value):
    rows = value.shape[0] // 2
    put(place, keep, send, 0, slice(start, start + rows), value[:rows])
    put(place, keep, send, 1, slice(start, start + rows), value[rows:])


def attend_back_kernel(
    received, pairs_turned, attended, log_total, given, feature_part, message,
    masked_keys, pairs, queries, outer, outer_row, chances, score_grads, query_sum, turned,
):
    received = received.ready()
    gather_keys(received, masked_keys, pairs, queries, None)
    low = low_lanes(16)

    def unpack(k):
        piece = given[k].astype(F32)
        outer[pl.ds(pl.multiple_of(SHARE * k, 16), 16), :] = jnp.where(low, 0.0, half_turn(piece)).astype(BF)
        outer[pl.ds(pl.multiple_of(SHARE * k + 16, 16), 16), :] = jnp.where(low, 0.0, piece).astype(BF)
        message[k, 144:240, :] = feature_part[k]

    loop(PEERS, unpack, 4)
    attended = attended.ready()

    def inner(k):
        rows = block_of(k, 256)
        turned = jnp.transpose(outer[rows, :].astype(F32))[64:128, :]
        outer_row[:, rows] = jnp.broadcast_to(
            jnp.sum(turned * attended[:, rows], axis=0, keepdims=True), (8, 256)
        )

    loop(QUERIES // 256, inner)
    query_sum[...] = jnp.zeros_like(query_sum)
    pairs_turned, log_total = pairs_turned.ready(), log_total.ready()

    def chunk(turn, carry):
        at = pl.ds(pl.multiple_of(turn * BACK_KEYS, BACK_KEYS), BACK_KEYS)
        key = masked_keys[at, :]
        both = pairs[at, :]
        for k in range(QUERIES // BACK_ROWS):
            rows = slice(BACK_ROWS * k, BACK_ROWS * (k + 1))
            chance = jnp.exp(nt(key, queries[rows, :]) - log_total[0:1, rows])
            chance_grad = nt(both, outer[rows, :])
            chances[:, rows] = chance.astype(BF)
            score_grads[:, rows] = (chance * (chance_grad - outer_row[0:1, rows])).astype(BF)
        sums = nn(score_grads[...], queries[...])
        other = nn(chances[...], outer[...])
        sums = jnp.where(low_lanes(BACK_KEYS), sums, other).astype(BF)
        for k in range(BACK_KEYS // 128):
            message[turn * (BACK_KEYS // 128) + k, 0:128, :] = sums[128 * k : 128 * (k + 1), :]
        query_sum[...] += nn(pairs_turned[:, at], score_grads[...])
        return carry

    lax.fori_loop(0, TOKENS // BACK_KEYS, chunk, 0, unroll=UNROLL_C)
    turned[...] = jnp.transpose(query_sum[...]) * SCALE

    def pack(k):
        first = turned[pl.ds(pl.multiple_of(SHARE * k, 16), 16), :]
        second = turned[pl.ds(pl.multiple_of(SHARE * k + 16, 16), 16), :]
        message[k, 128:144, :] = jnp.where(low, first, half_turn(second)).astype(BF)

    loop(PEERS, pack, 4)


def finish_kernel(
    place, received, tokens, camera, modulation, self_grad, in_weight, vectors,
    pair_value, token_grad, feature_grad, keep, send,
):
    total = received[0, 144:240, :].astype(F32)
    for k in range(1, PEERS):
        total = total + received[k, 144:240, :].astype(F32)
    for j in range(3):
        feature_grad[:, 128 * j : 128 * (j + 1)] = total[32 * j : 32 * (j + 1), :]
    low = low_lanes(BLOCK)
    queries = []
    keys = []
    values = []
    for pair in range(HEADS // 2):
        sums = []
        for odd in range(2):
            head = 2 * pair + odd
            total = received[QUARTERS * head, 0:128, :].astype(F32)
            for quarter in range(1, QUARTERS):
                total = total + received[QUARTERS * head + quarter, 0:128, :].astype(F32)
            sums.append(total)
        keys.append(jnp.where(low, sums[0], half_turn(sums[1])))
        values.append(jnp.where(low, half_turn(sums[0]), sums[1]))
        low_half = low_lanes(16)
        pieces = []
        for quarter in range(QUARTERS):
            even = received[QUARTERS * (2 * pair) + quarter, 128:144, :].astype(F32)
            odd = received[QUARTERS * (2 * pair + 1) + quarter, 128:144, :].astype(F32)
            pieces.append(jnp.where(low_half, even, half_turn(odd)))
            pieces.append(jnp.where(low_half, half_turn(even), odd))
        queries.append(jnp.concatenate(pieces, axis=0))
    parts = [jnp.concatenate(p, axis=1).astype(BF) for p in (queries, keys, values)]
    normed, inverse = norm_parts(tokens[...].astype(F32))
    scale = 1.0 + modulation[0:1, :WIDTH]
    hidden = (normed * scale + modulation[0:1, WIDTH:]).astype(BF)
    back = jnp.zeros((BLOCK, WIDTH), F32)
    for k in range(3):
        at = slice(WIDTH * k, WIDTH * (k + 1))
        back = back + nt(parts[k], in_weight[:, at])
        put_halves(place, keep, send, 256 * k, tn(hidden, parts[k]).astype(BF))
    token_grad[...] = self_grad[...] + norm_back(normed, inverse, back * scale)
    scale_grad = jnp.sum(back * normed, axis=0, keepdims=True)
    shift_grad = jnp.sum(back, axis=0, keepdims=True)
    cam = camera[...].astype(F32)
    cam_act = cam * jax.nn.sigmoid(cam)
    row = lax.broadcasted_iota(jnp.int32, (32, WIDTH), 0)
    item = place[1]
    first = place[2] == 0
    small = jnp.where(row == item, scale_grad, 0.0)
    small = small + jnp.where(row == 4 + item, shift_grad, 0.0)
    small = small + jnp.where(jnp.logical_and(first, row == 8 + item), cam_act[:, :WIDTH], 0.0)
    small = small + jnp.where(jnp.logical_and(first, row == 12 + item), cam_act[:, WIDTH:], 0.0)
    small = small + jnp.where(row == 16, vectors[0:1, :], 0.0)
    small = small + jnp.where(row == 17, vectors[1:2, :], 0.0)
    small = small + jnp.where(row == 18, vectors[2:3, :], 0.0)
    small = small + jnp.where(row == 19, vectors[3:4, :], 0.0)
    put_halves(place, keep, send, 768, pair_value[...])
    put(place, keep, send, 0, slice(960, 992), small.astype(BF))
    put(place, keep, send, 1, slice(960, 992), jnp.zeros((32, WIDTH), BF))
    keep[992:1024, :] = jnp.zeros((32, WIDTH), BF)
    send[992:1024, :] = jnp.zeros((32, WIDTH), BF)


def sum_split_kernel(which, place, *refs):
    parts, pieces = refs[:-4], refs[-4:]
    rows = pieces[0].shape[0]
    for k in range(4):
        at = pl.ds(pl.multiple_of(lax.rem(place[which] + k, 4) * rows, rows), rows)
        total = parts[0][at, :].astype(F32)
        for part in parts[1:]:
            total = total + part[at, :].astype(F32)
        pieces[k][...] = total.astype(BF)


def halves_kernel(place, value, mine, other):
    rows = mine.shape[0]
    mine[...] = value[pl.ds(pl.multiple_of(place[0] * rows, rows), rows), :]
    other[...] = value[pl.ds(pl.multiple_of((1 - place[0]) * rows, rows), rows), :]


def sum_kernel(*refs):
    total = refs[0][...].astype(F32)
    for part in refs[1:-1]:
        total = total + part[...].astype(F32)
    refs[-1][...] = total.astype(BF)


def sum_pairs_kernel(first, second, third, fourth, out):
    rows = first.shape[0]
    out[0:rows, :] = (first[...].astype(F32) + second[...].astype(F32)).astype(BF)
    out[rows : 2 * rows, :] = (third[...].astype(F32) + fourth[...].astype(F32)).astype(BF)


def arrange_kernel(which, place, *refs):
    pieces, out = refs[:-1], refs[-1]
    rows = pieces[0].shape[0]
    for k in range(4):
        at = pl.ds(pl.multiple_of(lax.rem(place[which] + 4 - k, 4) * rows, rows), rows)
        out[at, :] = pieces[k][...]


def sum_pieces_kernel(pieces, *outs):
    total = pieces[0].astype(F32)
    for k in range(1, pieces.shape[0]):
        total = total + pieces[k].astype(F32)
    total = total.astype(BF)
    for out in outs:
        if len(out.shape) == 2:
            out[...] = total
        else:
            for k in range(out.shape[0]):
                out[k] = total


def write_halves(core, early, late, outs, buffers, semaphores):
    up_grad, down_grad, self_in, pair, self_out, cross_query, cross_out = outs
    up_part, down_part, in_part, pair_part, out_part, query_part, cross_part = buffers
    copies = []

    def send(part, target, slot):
        rows = part.shape[0]
        at = pl.ds(pl.multiple_of(core * rows, rows), rows)
        copies.append(pltpu.make_async_copy(part, target.at[at, :], semaphores.at[slot]))
        copies[-1].start()

    for k in range(4):
        up_part[:, 512 * k : 512 * (k + 1)] = early[256 * k : 256 * (k + 1), :].astype(F32)
    send(up_part, up_grad, 0)
    down_part[...] = early[1024:2048, :].astype(F32)
    send(down_part, down_grad, 1)
    for k in range(3):
        in_part[:, 512 * k : 512 * (k + 1)] = late[256 * k : 256 * (k + 1), :].astype(F32)
    send(in_part, self_in, 2)
    pair_part[:, :WIDTH] = early[2816:3008, :].astype(F32)
    pair_part[:, WIDTH:] = late[768:960, :].astype(F32)
    send(pair_part, pair, 3)
    out_part[...] = early[2560:2816, :].astype(F32)
    send(out_part, self_out, 4)
    query_part[...] = early[2304:2560, :].astype(F32)
    send(query_part, cross_query, 5)
    cross_part[...] = early[2048:2304, :].astype(F32)
    send(cross_part, cross_out, 6)
    return copies


def own_out_kernel(place, early, late, *refs):
    for copy in write_halves(place[0], early, late, refs[:7], refs[7:14], refs[14]):
        copy.wait()


def other_out_kernel(place, early, late, mine, *refs):
    outs, refs = refs[7:14], refs[14:]
    mod_weight, mod_bias, gain_two, offset_two, gain_three, offset_three = refs[:6]
    core = place[0] == 0
    small = jnp.where(core, mine[960:992, :].astype(F32), late[960:992, :].astype(F32))
    grads = small[0:8, :]
    acts = small[8:16, :].astype(BF)
    head = lax.broadcasted_iota(jnp.int32, (8, WIDTH), 0) < 4
    turned = pltpu.roll(grads, 4, 0)
    mod_weight[:WIDTH, :WIDTH] = tn(acts, jnp.where(head, grads, 0.0).astype(BF))
    mod_weight[:WIDTH, WIDTH:] = tn(acts, jnp.where(head, turned, 0.0).astype(BF))
    mod_weight[WIDTH:, :WIDTH] = tn(acts, jnp.where(head, 0.0, turned).astype(BF))
    mod_weight[WIDTH:, WIDTH:] = tn(acts, jnp.where(head, 0.0, grads).astype(BF))
    mod_weight.send()
    copies = write_halves(1 - place[0], early, late, outs, refs[6:13], refs[13])
    gain_two[...] = small[16:17, :]
    offset_two[...] = small[17:18, :]
    gain_three[...] = small[18:19, :]
    offset_three[...] = small[19:20, :]
    mod_bias[:, :WIDTH] = jnp.sum(jnp.where(head, grads, 0.0), axis=0, keepdims=True)
    mod_bias[:, WIDTH:] = jnp.sum(jnp.where(head, 0.0, grads), axis=0, keepdims=True)
    for copy in copies:
        copy.wait()


def index_of(x, y, z, core):
    return ((z % 2) * 2 + core) * 32 + (y * 4 + x) * 2 + z // 2


CHIPS = [(x, y, z) for x in range(4) for y in range(4) for z in range(4)]
SAME_CORE = [[index_of(*chip, core) for chip in CHIPS] for core in range(2)]
SAME_PLANE = [
    [index_of(x, y, z, core) for x in range(4) for y in range(4)] for z in range(4) for core in range(2)
]
OTHER_CORE = [
    (index_of(*chip, core), index_of(*chip, 1 - core)) for chip in CHIPS for core in range(2)
]


def shift_of(axis, step):
    moves = []
    for chip in CHIPS:
        there = list(chip)
        there[axis] = (there[axis] + step) % 4
        moves += [(index_of(*chip, core), index_of(*there, core)) for core in range(2)]
    return moves


SHIFTS = {(axis, step): shift_of(axis, step) for axis in range(3) for step in (1, 2, 3)}


def exchange(message):
    return lax.all_to_all(message, "seq", 0, 0, tiled=True)


def swap_cores(value):
    return lax.ppermute(value, AXES, OTHER_CORE)


def scatter_ring(pieces, axis):
    return (pieces[0],) + tuple(lax.ppermute(pieces[k], AXES, SHIFTS[axis, k]) for k in (1, 3, 2))


def gather_ring(piece, axis):
    came = {k: lax.ppermute(piece, AXES, SHIFTS[axis, k]) for k in (1, 3, 2)}
    return piece, came[1], came[2], came[3]


def sum_split(place, parts, axis):
    rows = parts[0].shape[0] // 4
    return call(
        functools.partial(sum_split_kernel, 3 + axis), (shape((rows, WIDTH), BF),) * 4, (place, *parts),
        traffic=4e5, smem=(0,),
    )


def sum_all(parts):
    return call(sum_kernel, shape(parts[0].shape, BF), parts, traffic=4e5)


def arrange(place, parts, axis):
    return call(
        functools.partial(arrange_kernel, 3 + axis), shape((4 * parts[0].shape[0], WIDTH), BF), (place, *parts),
        traffic=4e5, smem=(0,),
    )


def scatter_chips(value):
    rows = value.shape[0] // 64
    return lax.all_to_all(
        value.reshape(64, rows, WIDTH), AXES, 0, 0, tiled=True, axis_index_groups=SAME_CORE
    )


def in_one_step(always, work, *values):
    def nothing(*values):
        return jax.tree.map(lambda v: jnp.zeros(v.shape, v.dtype), jax.eval_shape(work, *values))

    return lax.cond(always, work, nothing, *values)


def body(
    tokens, camera, features, foreground, layout, modulation_weight, modulation_bias,
    self_in_weight, self_out_weight, cross_norm_gain, cross_norm_bias, cross_query_weight,
    cross_pair_weight, cross_out_weight, feed_norm_gain, feed_norm_bias, up_weight, down_weight,
    cotangent,
):
    tokens = tokens[0]
    features = features[0]
    cotangent = cotangent[0]
    row = lambda v: v.reshape(1, -1)
    step = functools.partial(in_one_step, layout[0, 0] >= 0)
    gain_two, offset_two = row(cross_norm_gain), row(cross_norm_bias)
    gain_three, offset_three = row(feed_norm_gain), row(feed_norm_bias)
    item, spot = lax.axis_index("batch"), lax.axis_index("seq")
    place = jnp.stack(
        [item & 1, item, spot, (spot >> 1) & 3, spot >> 3, (spot & 1) * 2 + (item >> 1)]
    ).astype(jnp.int32)

    message, modulation = call(
        prepare_kernel,
        (shape((PEERS, 256, 128), BF), shape((8, 1024))),
        (foreground, layout, tokens, features, camera, modulation_weight, modulation_bias, self_in_weight),
        flops=1e9, traffic=8e6, smem=(0, 1), late=(4, 5, 2, 7, 3), far_out=(0,), limit=57,
        scratch=(pltpu.VMEM((PEERS, 256, 128), BF), pltpu.SemaphoreType.DMA((HEADS,))),
    )
    received = exchange(message)
    message, attended_turned, log_total, pairs_turned = call(
        attend_kernel,
        (shape((PEERS, 16, 128), BF), shape((64, QUERIES)), shape((8, QUERIES)), shape((128, TOKENS), BF)),
        (received,),
        scratch=(
            pltpu.VMEM((TOKENS, 128), BF), pltpu.VMEM((QUERIES, 128), BF), pltpu.VMEM((TOKENS, ROWS), F32),
            pltpu.VMEM((128, QUERIES), F32), pltpu.VMEM((QUERIES, 128), F32),
        ),
        flops=9e9, traffic=4e6,
    )
    back = exchange(message)
    keys, values, keys_turned, values_turned, every_turned = call(
        pairs_kernel,
        (
            shape((PATCHES, WIDTH), BF), shape((PATCHES, WIDTH), BF), shape((WIDTH, PATCHES), BF),
            shape((WIDTH, PATCHES), BF), shape((384, PATCHES), BF),
        ),
        (received, cross_pair_weight),
        scratch=(pltpu.VMEM((PATCHES, 384), BF),),
        flops=3e9, traffic=8e6, late=(1,), away=(0, 1, 2, 3, 4),
    )
    (
        block_out, early_keep, early_send, vectors, message, self_grad, feature_message, pair_value,
    ) = call(
        middle_kernel,
        (
            shape((BLOCK, WIDTH)), shape((3072, WIDTH), BF), shape((3072, WIDTH), BF), shape((8, WIDTH)),
            shape((PEERS, 16, 128), BF), shape((BLOCK, WIDTH)), shape((PEERS, 96, 128), BF), shape((384, WIDTH), BF),
        ),
        (
            place, back, tokens, keys, keys_turned, values, values_turned, self_out_weight, gain_two, offset_two,
            cross_query_weight, cross_out_weight, gain_three, offset_three, up_weight, down_weight, cotangent,
            every_turned, cross_pair_weight,
        ),
        scratch=(
            pltpu.VMEM((2, 3072, WIDTH), BF), pltpu.SemaphoreType.DMA((2, 2)), pltpu.VMEM((PATCHES, WIDTH), BF),
            pltpu.VMEM((PATCHES, WIDTH), BF), pltpu.VMEM((BLOCK, WIDTH), F32), pltpu.VMEM((BLOCK, WIDTH), F32),
        ),
        flops=1.6e10, traffic=2e7, smem=(0,), late=(7, 2, 10, 3, 6, 11, 14, 16, 15, 5, 4, 17, 18), limit=57,
        far_out=(1, 2),
    )

    def attend_back(message):
        given = exchange(message)
        total = sum_all((early_keep, swap_cores(early_send)))
        given, total = lax.optimization_barrier((given, total))
        pieces = scatter_chips(total)
        message = call(
            attend_back_kernel,
            shape((PEERS, 240, 128), BF),
            (received, pairs_turned, attended_turned, log_total, given, feature_message),
            scratch=(
                pltpu.VMEM((TOKENS, 128), BF), pltpu.VMEM((TOKENS, 128), BF), pltpu.VMEM((QUERIES, 128), BF),
                pltpu.VMEM((QUERIES, 128), BF), pltpu.VMEM((8, QUERIES), F32),
                pltpu.VMEM((BACK_KEYS, QUERIES), BF), pltpu.VMEM((BACK_KEYS, QUERIES), BF),
                pltpu.VMEM((128, QUERIES), F32), pltpu.VMEM((QUERIES, 128), F32),
            ),
            flops=1.6e10, traffic=8e6, late=(0, 2, 1, 3),
        )
        return message, pieces

    message, pieces = step(attend_back, message)
    early = call(sum_pieces_kernel, shape((48, WIDTH), BF), (pieces,), traffic=3e6)
    early = lax.all_gather(early, AXES, axis=0, tiled=True, axis_index_groups=SAME_CORE)

    def finish(message):
        returned = exchange(message)
        token_grad, feature_grad, keep, send = call(
            finish_kernel,
            (shape((BLOCK, WIDTH)), shape((32, 384)), shape((1024, WIDTH), BF), shape((1024, WIDTH), BF)),
            (
                place, returned, tokens, camera, modulation, self_grad, self_in_weight, vectors,
                pair_value,
            ),
            flops=3e9, traffic=8e6, smem=(0,), late=(2, 6, 4, 5),
        )
        pieces = scatter_chips(sum_all((keep, swap_cores(send))))
        total = call(sum_pieces_kernel, shape(pieces.shape, BF), (pieces,), traffic=2e6)
        late = lax.all_to_all(
            total, AXES, 0, 0, tiled=True, axis_index_groups=SAME_CORE
        ).reshape(1024, WIDTH)
        return token_grad, feature_grad, late

    token_grad, feature_grad, late = step(finish, message)
    early, late = lax.optimization_barrier((early, late))
    early_other, late_other = swap_cores(early), swap_cores(late)
    square = shape((WIDTH, WIDTH))
    vector = shape((1, WIDTH))
    grads = (shape((WIDTH, 2048)), shape((2048, WIDTH)), shape((WIDTH, 3 * WIDTH)), shape((384, 1024))) + (square,) * 3
    halves = tuple(pltpu.VMEM((g.shape[0] // 2, g.shape[1]), F32) for g in grads)
    halves += (pltpu.SemaphoreType.DMA((7,)),)
    grads = call(
        own_out_kernel, grads, (place, early, late),
        scratch=halves, traffic=1.4e7, smem=(0,), far_out=tuple(range(7)),
    )
    (
        up_grad, down_grad, self_in_grad, pair_grad, self_out_grad, cross_query_grad, cross_out_grad,
        mod_weight_grad, mod_bias_grad, gain_two_grad, offset_two_grad, gain_three_grad, offset_three_grad,
    ) = call(
        other_out_kernel,
        tuple(shape(g.shape) for g in grads) + (shape((1024, 1024)), shape((1, 1024))) + (vector,) * 4,
        (place, early_other, late_other, late, *grads),
        scratch=halves, traffic=1.4e7, smem=(0,), far_in=tuple(range(4, 11)), far_out=tuple(range(7)),
        away=(7,), aliases={4 + k: k for k in range(7)},
    )
    return (
        block_out[None],
        token_grad[None],
        feature_grad[None],
        mod_weight_grad,
        mod_bias_grad[0],
        self_in_grad,
        self_out_grad,
        gain_two_grad[0],
        offset_two_grad[0],
        cross_query_grad,
        pair_grad,
        cross_out_grad,
        gain_three_grad[0],
        offset_three_grad[0],
        up_grad,
        down_grad,
    )


def solution(mesh):
    split = P("batch", "seq", None)
    in_specs = (
        (split, P("batch", None), split, P("batch", None), P("batch", "seq")) + (P(),) * 13 + (split,)
    )
    out_specs = (split,) * 3 + (P(),) * 13
    return jax.shard_map(body, mesh=mesh, in_specs=in_specs, out_specs=out_specs, check_vma=False)
```

```python
import functools

import jax
import jax.numpy as jnp
from jax import lax
from jax.experimental import pallas as pl
from jax.experimental.pallas import tpu as pltpu
from jax.sharding import PartitionSpec as P

HEADS = 8
HEAD_DIM = 64
BLOCK = 128
TRIB = 24
PATCHB = 8
WIDTH = 512
PATCHES = 1024
TOKENS = 4096
EPSILON = 1e-05
MASKED = -1e30
SCALE = HEAD_DIM ** (-0.5)
BF = jnp.bfloat16
F32 = jnp.float32
AXES = ("batch", "seq")
PEERS = 32
QUARTERS = 4
SHARE = BLOCK // QUARTERS
MIB = 1024 * 1024


def nn(a, b):
    return lax.dot_general(a, b, (((1,), (0,)), ((), ())), preferred_element_type=F32)


def nt(a, b):
    return lax.dot_general(a, b, (((1,), (1,)), ((), ())), preferred_element_type=F32)


def tn(a, b):
    return lax.dot_general(a, b, (((0,), (0,)), ((), ())), preferred_element_type=F32)


def half_turn(values):
    return pltpu.roll(values, 64, 1)


def low_lanes(rows):
    return lax.broadcasted_iota(jnp.int32, (rows, 128), 1) < 64


def norm_parts(values):
    centre = jnp.mean(values, axis=-1, keepdims=True)
    centred = values - centre
    spread = jnp.mean(centred * centred, axis=-1, keepdims=True)
    inverse = lax.rsqrt(spread + EPSILON)
    return centred * inverse, inverse


def norm_back(normed, inverse, grad):
    first = jnp.mean(grad, axis=-1, keepdims=True)
    second = jnp.mean(grad * normed, axis=-1, keepdims=True)
    return inverse * (grad - first - normed * second)


class Late:
    def __init__(self, copy, ref):
        self.copy, self.ref, self.here, self.shape = copy, ref, False, ref.shape

    def ready(self):
        if not self.here:
            self.copy.wait()
            self.here = True
        return self.ref

    def __getitem__(self, index):
        return self.ready()[index]


class Away:
    def __init__(self, ref, copy):
        self.ref, self.copy, self.sent, self.shape = ref, copy, False, ref.shape

    def __setitem__(self, index, value):
        self.ref[index] = value

    def send(self):
        if not self.sent:
            self.copy.start()
            self.sent = True


def call(
    kernel, out_shape, inputs, scratch=(), flops=0, traffic=0, limit=32, smem=(), late=(), away=(), far_out=(),
    far_in=(), aliases=None,
):
    vmem = pl.BlockSpec(memory_space=pltpu.VMEM)
    scalar = pl.BlockSpec(memory_space=pltpu.SMEM)
    far = pl.BlockSpec(memory_space=pltpu.HBM)
    single = not isinstance(out_shape, tuple)
    outs = (out_shape,) if single else out_shape
    count, extra = len(inputs), len(scratch)
    def whole(*refs):
        refs = list(refs)
        ins, results = refs[:count], refs[count : count + len(outs)]
        rest = refs[count + len(outs) :]
        mine, buffers = rest[:extra], rest[extra:]
        semaphores = buffers[-1] if late or away else None
        for k, which in enumerate(late):
            copy = pltpu.make_async_copy(ins[which], buffers[k], semaphores.at[k])
            copy.start()
            ins[which] = Late(copy, buffers[k])
        for k, which in enumerate(away):
            buffer = buffers[len(late) + k]
            results[which] = Away(
                buffer, pltpu.make_async_copy(buffer, results[which], semaphores.at[len(late) + k])
            )
        kernel(*ins, *results, *mine)
        for which in late:
            ins[which].ready()
        for which in away:
            results[which].send()
        for which in away:
            results[which].copy.wait()

    buffers = [pltpu.VMEM(inputs[k].shape, inputs[k].dtype) for k in late]
    buffers += [pltpu.VMEM(outs[k].shape, outs[k].dtype) for k in away]
    if buffers:
        buffers.append(pltpu.SemaphoreType.DMA((len(buffers),)))
    out_specs = tuple(far if k in away or k in far_out else vmem for k in range(len(outs)))
    return pl.pallas_call(
        whole,
        out_shape=out_shape,
        in_specs=[scalar if k in smem else far if k in late or k in far_in else vmem for k in range(count)],
        out_specs=out_specs[0] if single else out_specs,
        scratch_shapes=list(scratch) + buffers,
        input_output_aliases=aliases or {},
        compiler_params=pltpu.CompilerParams(vmem_limit_bytes=limit * MIB),
        cost_estimate=pl.CostEstimate(
            flops=int(flops), bytes_accessed=int(traffic), transcendentals=0
        ),
    )(*inputs)


def shape(dims, dtype=F32):
    return jax.ShapeDtypeStruct(dims, dtype)


def prepare_kernel(
    foreground, layout, tokens, features, camera, mod_weight, mod_bias, in_weight,
    far_message, modulation, message, semaphores,
):
    for to in range(PEERS):
        for k in range(3):
            message[to, 160 + 32 * k : 192 + 32 * k, :] = features[:, 128 * k : 128 * (k + 1)]
    cam = camera[...].astype(F32)
    cam_act = (cam * jax.nn.sigmoid(cam)).astype(BF)
    mod = nn(jnp.broadcast_to(cam_act, (16, cam_act.shape[1])), mod_weight[...])[0:8]
    mod = mod + mod_bias[...].astype(F32).reshape(1, 2 * WIDTH)
    modulation[...] = mod
    block = layout[0, 0]
    lit = jnp.int32(0)
    for k in range(PATCHB):
        lit = lit + jnp.where(block - TRIB == k, foreground[0, k], 0)
    kept = jnp.logical_or(block < TRIB, lit > 0)
    bias = jnp.where(kept, jnp.float32(0.0), jnp.float32(MASKED))
    normed, _ = norm_parts(tokens[...].astype(F32))
    hidden = (normed * (1.0 + mod[0:1, :WIDTH]) + mod[0:1, WIDTH:]).astype(BF)
    projected = nn(hidden, in_weight[...]).astype(BF).astype(F32)
    low = low_lanes(BLOCK)
    for pair in range(HEADS // 2):
        at = 128 * pair
        query = projected[:, at : at + 128] * SCALE
        key = projected[:, WIDTH + at : WIDTH + at + 128]
        value = projected[:, 2 * WIDTH + at : 2 * WIDTH + at + 128]
        for odd in range(2):
            head = 2 * pair + odd
            if odd:
                both = jnp.where(low, half_turn(key), value)
                mine = jnp.where(low, half_turn(query), bias)
            else:
                both = jnp.where(low, key, half_turn(value))
                mine = jnp.where(low, query, bias)
            both = both.astype(BF)
            mine = mine.astype(BF)
            for quarter in range(QUARTERS):
                to = QUARTERS * head + quarter
                message[to, 0:128, :] = both
                message[to, 128:160, :] = mine[SHARE * quarter : SHARE * (quarter + 1)]
            some = slice(QUARTERS * head, QUARTERS * (head + 1))
            pltpu.make_async_copy(message.at[some], far_message.at[some], semaphores.at[head]).start()
    for head in range(HEADS):
        some = slice(QUARTERS * head, QUARTERS * (head + 1))
        pltpu.make_async_copy(message.at[some], far_message.at[some], semaphores.at[head]).wait()


def loop(count, work, unroll=1):
    def turn(k, carry):
        work(k)
        return carry

    lax.fori_loop(0, count, turn, 0, unroll=unroll)


def block_of(k, size):
    return pl.ds(pl.multiple_of(k * size, size), size)


def gather_keys(received, masked_keys, pairs, queries, turned):
    low = low_lanes(128)
    lane = lax.broadcasted_iota(jnp.int32, (128, 128), 1)
    lane_q = lax.broadcasted_iota(jnp.int32, (SHARE, 128), 1)

    def gather(k):
        at = block_of(k, 128)
        both = received[k, 0:128, :].astype(F32)
        mine = received[k, 128:160, :].astype(F32)
        masked_keys[at, :] = jnp.where(low, both, jnp.where(lane == 64, mine[0:1, :], 0.0)).astype(BF)
        if pairs is not None:
            pairs[at, :] = received[k, 0:128, :]
        if turned is not None:
            turned[:, at] = jnp.transpose(both).astype(BF)
        queries[block_of(k, SHARE), :] = jnp.where(
            lane_q < 64, mine, jnp.where(lane_q == 64, 1.0, 0.0)
        ).astype(BF)

    loop(PEERS, gather, 4)


KEYS = 512
ROWS = 1024
UNROLL_A = 2
UNROLL_B = 4
UNROLL_C = 1
BACK_KEYS = 1024
BACK_ROWS = 256
QUERIES = PEERS * SHARE


def attend_kernel(
    received, message, attended, log_total, pairs_turned, masked_keys, queries, scores, mixed, turned
):
    gather_keys(received, masked_keys, None, queries, pairs_turned)
    chunks = TOKENS // KEYS
    query = queries[...]

    def score(k, top):
        at = block_of(k, KEYS)
        part = nt(masked_keys[at, :], query)
        scores[at, :] = part
        return jnp.maximum(top, jnp.max(part, axis=0, keepdims=True))

    top = lax.fori_loop(0, chunks, score, jnp.full((1, ROWS), -jnp.inf, F32), unroll=UNROLL_A)
    mixed[...] = jnp.zeros_like(mixed)

    def mix(k, total):
        at = block_of(k, KEYS)
        chance = jnp.exp(scores[at, :] - top)
        mixed[...] += nn(pairs_turned[:, at], chance.astype(BF))
        return total + jnp.sum(chance, axis=0, keepdims=True)

    total = lax.fori_loop(0, chunks, mix, jnp.zeros((1, ROWS), F32), unroll=UNROLL_B)
    result = mixed[...] / total
    attended[...] = result[64:128, :]
    log_total[...] = jnp.broadcast_to(top + jnp.log(total), (8, ROWS))
    turned[...] = jnp.transpose(result)
    low = low_lanes(16)

    def pack(k):
        first = turned[pl.ds(pl.multiple_of(SHARE * k, 16), 16), :]
        second = turned[pl.ds(pl.multiple_of(SHARE * k + 16, 16), 16), :]
        message[k] = jnp.where(low, half_turn(first), second).astype(BF)

    loop(PEERS, pack, 4)


def pairs_kernel(
    received, pair_weight, keys, values, keys_turned, values_turned, every_turned, kept, every
):
    pair_weight = pair_weight.ready()

    def gather(k):
        for j in range(3):
            every[block_of(k, 32), 128 * j : 128 * (j + 1)] = received[k, 160 + 32 * j : 192 + 32 * j, :]
        kept.ref[k] = received[k, 0:160, :]

    def project(k):
        rows = block_of(k, 256)
        part = every[rows, :]
        every_turned.ref[:, rows] = jnp.transpose(part.astype(F32)).astype(BF)
        both = nn(part, pair_weight[...]).astype(BF)
        keys.ref[rows, :] = both[:, :WIDTH]
        values.ref[rows, :] = both[:, WIDTH:]
        turned = jnp.transpose(both.astype(F32)).astype(BF)
        keys_turned.ref[:, rows] = turned[:WIDTH, :]
        values_turned.ref[:, rows] = turned[WIDTH:, :]

    loop(PEERS, gather, 4)
    kept.send()
    loop(PATCHES // 256, project)


def unpack_heads(received):
    low = low_lanes(16)
    columns = []
    for pair in range(HEADS // 2):
        pieces = []
        for quarter in range(QUARTERS):
            even = received[QUARTERS * (2 * pair) + quarter].astype(F32)
            odd = received[QUARTERS * (2 * pair + 1) + quarter].astype(F32)
            pieces.append(jnp.where(low, even, half_turn(odd)))
            pieces.append(jnp.where(low, half_turn(even), odd))
        columns.append(jnp.concatenate(pieces, axis=0))
    return jnp.concatenate(columns, axis=1)


def pack_heads(values, message):
    low = low_lanes(16)
    for pair in range(HEADS // 2):
        for quarter in range(QUARTERS):
            first = values[SHARE * quarter : SHARE * quarter + 16, 128 * pair : 128 * (pair + 1)]
            second = values[SHARE * quarter + 16 : SHARE * (quarter + 1), 128 * pair : 128 * (pair + 1)]
            message[QUARTERS * (2 * pair) + quarter] = jnp.where(
                low, first, half_turn(second)
            ).astype(BF)
            message[QUARTERS * (2 * pair + 1) + quarter] = jnp.where(
                low, half_turn(first), second
            ).astype(BF)


GELU = 0.7978845608028654
CUBE = 0.044715


def put(place, keep, send, owner, rows, value):
    @pl.when(place[0] == owner)
    def _():
        keep[rows, :] = value

    @pl.when(place[0] != owner)
    def _():
        send[rows, :] = value


def middle_kernel(
    place, received, tokens, keys, keys_turned, values, values_turned, self_out, gain_two, offset_two,
    query_weight, cross_out, gain_three, offset_three, up_weight, down_weight, cotangent, every_turned, pair_weight,
    block_out, feed_keep, feed_send, vectors, message, self_grad, feature_part, pair_value,
    feed_pack, semaphores, key_all, value_all, total_out, total_back,
):
    def move(start, rows, to, slot):
        at = slice(to, to + rows)

        @pl.when(place[0] == 0)
        def _():
            pltpu.make_async_copy(feed_pack.at[0, start : start + rows], feed_keep.at[at], semaphores.at[slot, 0]).start()
            pltpu.make_async_copy(feed_pack.at[1, start : start + rows], feed_send.at[at], semaphores.at[slot, 1]).start()

        @pl.when(place[0] != 0)
        def _():
            pltpu.make_async_copy(feed_pack.at[1, start : start + rows], feed_keep.at[at], semaphores.at[slot, 0]).start()
            pltpu.make_async_copy(feed_pack.at[0, start : start + rows], feed_send.at[at], semaphores.at[slot, 1]).start()

    def put_halves(start, value):
        rows = value.shape[0] // 2
        feed_pack[0, start : start + rows, :] = value[:rows]
        feed_pack[1, start : start + rows, :] = value[rows:]

    attended_low = unpack_heads(received).astype(BF)
    first = tokens[...].astype(F32) + nn(attended_low, self_out[...])
    normed_two, inverse_two = norm_parts(first)
    gain = gain_two[...].astype(F32)
    hidden = (normed_two * gain + offset_two[...].astype(F32)).astype(BF)
    queries = nn(hidden, query_weight[...]).astype(BF).astype(F32) * SCALE
    low = low_lanes(BLOCK)
    upper = lax.broadcasted_iota(jnp.int32, (128, BLOCK), 0) < 64
    masked = []
    chances = []
    pieces = []
    for pair in range(HEADS // 2):
        at = slice(128 * pair, 128 * (pair + 1))
        key = keys[:, at]
        value = values_turned[at, :]
        parts = []
        for odd in range(2):
            mine = jnp.where(low if odd == 0 else jnp.logical_not(low), queries[:, at], 0.0).astype(BF)
            scores = nt(key, mine)
            chance = jnp.exp(scores - jnp.max(scores, axis=0, keepdims=True))
            chance = chance * (1.0 / jnp.sum(chance, axis=0, keepdims=True))
            masked.append(mine)
            chances.append(chance)
            parts.append(nn(value, chance.astype(BF)))
        pieces.append(jnp.transpose(jnp.where(upper, parts[0], parts[1])))
    mixed = jnp.concatenate(pieces, axis=1).astype(BF)
    second = first + nn(mixed, cross_out[...])
    normed, inverse = norm_parts(second)
    gain_out = gain_three[...].astype(F32)
    hidden3 = (normed * gain_out + offset_three[...].astype(F32)).astype(BF)
    grad_low = cotangent[...]
    total_out[...] = second
    total_back[...] = jnp.zeros((BLOCK, WIDTH), F32)
    up_all, down_all = up_weight.ready(), down_weight.ready()

    def feed_block(k, carry):
        at = pl.ds(pl.multiple_of(512 * k, 512), 512)
        up, down = up_all[:, at], down_all[at, :]
        pre = nn(hidden3, up)
        square = pre * pre
        turn = jnp.tanh(GELU * (pre + CUBE * (square * pre)))
        half = 0.5 * (1.0 + turn)
        active = (pre * half).astype(BF)
        slope = half + (0.5 * pre) * (1.0 - turn * turn) * (GELU * (1.0 + (3.0 * CUBE) * square))
        total_out[...] += nn(active, down)
        pre_grad = (nt(grad_low, down) * slope).astype(BF)
        total_back[...] += nt(pre_grad, up)
        grad = tn(hidden3, pre_grad).astype(BF)
        feed_pack[0, pl.ds(pl.multiple_of(256 * k, 256), 256), :] = grad[:256]
        feed_pack[1, pl.ds(pl.multiple_of(256 * k, 256), 256), :] = grad[256:]
        feed_pack[k // 2, pl.ds(pl.multiple_of(1024 + 512 * (k % 2), 512), 512), :] = tn(active, grad_low).astype(BF)
        return carry

    lax.fori_loop(0, 4, feed_block, 0, unroll=1)
    result = total_out[...]
    back = total_back[...]
    move(0, 2048, 0, 0)
    block_out[...] = result
    vectors[2:3, :] = jnp.sum(back * normed, axis=0, keepdims=True)
    vectors[3:4, :] = jnp.sum(back, axis=0, keepdims=True)
    grad = grad_low.astype(F32) + norm_back(normed, inverse, back * gain_out)
    branch = grad.astype(BF)
    put_halves(2048, tn(mixed, branch).astype(BF))
    mixed_grad = nt(branch, cross_out[...]).astype(BF).astype(F32)
    pieces = []
    pair_low = []
    for pair in range(HEADS // 2):
        at = slice(128 * pair, 128 * (pair + 1))
        value = values[:, at]
        key_turned = keys_turned[at, :]
        parts = []
        key_sum = None
        value_sum = None
        for odd in range(2):
            head = 2 * pair + odd
            given = jnp.where(low if odd == 0 else jnp.logical_not(low), mixed_grad[:, at], 0.0).astype(BF)
            chance = chances[head]
            chance_grad = nt(value, given)
            inner = jnp.sum(chance * chance_grad, axis=0, keepdims=True)
            score_grad = (chance * (chance_grad - inner)).astype(BF)
            parts.append(nn(key_turned, score_grad))
            key_part = nn(score_grad, masked[head])
            value_part = nn(chance.astype(BF), given)
            key_sum = key_part if key_sum is None else key_sum + key_part
            value_sum = value_part if value_sum is None else value_sum + value_part
        pair_low.append((key_sum.astype(BF), value_sum.astype(BF)))
        pieces.append(jnp.transpose(jnp.where(upper, parts[0], parts[1])) * SCALE)
    low_grad = jnp.concatenate(pieces, axis=1).astype(BF)
    back = nt(low_grad, query_weight[...])
    vectors[0:1, :] = jnp.sum(back * normed_two, axis=0, keepdims=True)
    vectors[1:2, :] = jnp.sum(back, axis=0, keepdims=True)
    vectors[4:8, :] = jnp.zeros((4, WIDTH), F32)
    grad = grad + norm_back(normed_two, inverse_two, back * gain)
    self_grad[...] = grad
    branch = grad.astype(BF)
    pack_heads(nt(branch, self_out[...]), message)
    put_halves(2304, tn(hidden, low_grad).astype(BF))
    put_halves(2560, tn(attended_low, branch).astype(BF))
    key_grad = jnp.concatenate([p[0] for p in pair_low], axis=1)
    value_grad = jnp.concatenate([p[1] for p in pair_low], axis=1)
    put_halves(2816, nn(every_turned[...], key_grad).astype(BF))
    pair_value[...] = nn(every_turned[...], value_grad).astype(BF)
    feed_pack[0, 3008:3072, :] = jnp.zeros((64, WIDTH), BF)
    feed_pack[1, 3008:3072, :] = jnp.zeros((64, WIDTH), BF)
    move(2048, 1024, 2048, 1)
    def feature_block(k, carry):
        rows = pl.ds(pl.multiple_of(256 * k, 256), 256)
        part = (nt(key_all[rows, :], pair_keys) + nt(value_all[rows, :], pair_values)).astype(BF)
        for i in range(8):
            for j in range(3):
                feature_part[8 * k + i, 32 * j : 32 * (j + 1), :] = part[
                    32 * i : 32 * (i + 1), 128 * j : 128 * (j + 1)
                ]
        return carry

    pair_keys, pair_values = pair_weight[:, :WIDTH], pair_weight[:, WIDTH:]
    key_all[...] = key_grad
    value_all[...] = value_grad
    lax.fori_loop(0, PATCHES // 256, feature_block, 0)
    for slot, rows in enumerate((2048, 1024)):
        for k in range(2):
            pltpu.make_async_copy(
                feed_pack.at[0, 0:rows], feed_keep.at[0:rows], semaphores.at[slot, k]
            ).wait()


def put_halves(place, keep, send, start, value):
    rows = value.shape[0] // 2
    put(place, keep, send, 0, slice(start, start + rows), value[:rows])
    put(place, keep, send, 1, slice(start, start + rows), value[rows:])


def attend_back_kernel(
    received, pairs_turned, attended, log_total, given, feature_part, message,
    masked_keys, pairs, queries, outer, outer_row, chances, score_grads, query_sum, turned,
):
    received = received.ready()
    gather_keys(received, masked_keys, pairs, queries, None)
    low = low_lanes(16)

    def unpack(k):
        piece = given[k].astype(F32)
        outer[pl.ds(pl.multiple_of(SHARE * k, 16), 16), :] = jnp.where(low, 0.0, half_turn(piece)).astype(BF)
        outer[pl.ds(pl.multiple_of(SHARE * k + 16, 16), 16), :] = jnp.where(low, 0.0, piece).astype(BF)
        message[k, 144:240, :] = feature_part[k]

    loop(PEERS, unpack, 4)
    attended = attended.ready()

    def inner(k):
        rows = block_of(k, 256)
        turned = jnp.transpose(outer[rows, :].astype(F32))[64:128, :]
        outer_row[:, rows] = jnp.broadcast_to(
            jnp.sum(turned * attended[:, rows], axis=0, keepdims=True), (8, 256)
        )

    loop(QUERIES // 256, inner)
    query_sum[...] = jnp.zeros_like(query_sum)
    pairs_turned, log_total = pairs_turned.ready(), log_total.ready()

    def chunk(turn, carry):
        at = pl.ds(pl.multiple_of(turn * BACK_KEYS, BACK_KEYS), BACK_KEYS)
        key = masked_keys[at, :]
        both = pairs[at, :]
        for k in range(QUERIES // BACK_ROWS):
            rows = slice(BACK_ROWS * k, BACK_ROWS * (k + 1))
            chance = jnp.exp(nt(key, queries[rows, :]) - log_total[0:1, rows])
            chance_grad = nt(both, outer[rows, :])
            chances[:, rows] = chance.astype(BF)
            score_grads[:, rows] = (chance * (chance_grad - outer_row[0:1, rows])).astype(BF)
        sums = nn(score_grads[...], queries[...])
        other = nn(chances[...], outer[...])
        sums = jnp.where(low_lanes(BACK_KEYS), sums, other).astype(BF)
        for k in range(BACK_KEYS // 128):
            message[turn * (BACK_KEYS // 128) + k, 0:128, :] = sums[128 * k : 128 * (k + 1), :]
        query_sum[...] += nn(pairs_turned[:, at], score_grads[...])
        return carry

    lax.fori_loop(0, TOKENS // BACK_KEYS, chunk, 0, unroll=UNROLL_C)
    turned[...] = jnp.transpose(query_sum[...]) * SCALE

    def pack(k):
        first = turned[pl.ds(pl.multiple_of(SHARE * k, 16), 16), :]
        second = turned[pl.ds(pl.multiple_of(SHARE * k + 16, 16), 16), :]
        message[k, 128:144, :] = jnp.where(low, first, half_turn(second)).astype(BF)

    loop(PEERS, pack, 4)


def finish_kernel(
    place, received, tokens, camera, modulation, self_grad, in_weight, vectors,
    pair_value, token_grad, feature_grad, keep, send,
):
    total = received[0, 144:240, :].astype(F32)
    for k in range(1, PEERS):
        total = total + received[k, 144:240, :].astype(F32)
    for j in range(3):
        feature_grad[:, 128 * j : 128 * (j + 1)] = total[32 * j : 32 * (j + 1), :]
    low = low_lanes(BLOCK)
    queries = []
    keys = []
    values = []
    for pair in range(HEADS // 2):
        sums = []
        for odd in range(2):
            head = 2 * pair + odd
            total = received[QUARTERS * head, 0:128, :].astype(F32)
            for quarter in range(1, QUARTERS):
                total = total + received[QUARTERS * head + quarter, 0:128, :].astype(F32)
            sums.append(total)
        keys.append(jnp.where(low, sums[0], half_turn(sums[1])))
        values.append(jnp.where(low, half_turn(sums[0]), sums[1]))
        low_half = low_lanes(16)
        pieces = []
        for quarter in range(QUARTERS):
            even = received[QUARTERS * (2 * pair) + quarter, 128:144, :].astype(F32)
            odd = received[QUARTERS * (2 * pair + 1) + quarter, 128:144, :].astype(F32)
            pieces.append(jnp.where(low_half, even, half_turn(odd)))
            pieces.append(jnp.where(low_half, half_turn(even), odd))
        queries.append(jnp.concatenate(pieces, axis=0))
    parts = [jnp.concatenate(p, axis=1).astype(BF) for p in (queries, keys, values)]
    normed, inverse = norm_parts(tokens[...].astype(F32))
    scale = 1.0 + modulation[0:1, :WIDTH]
    hidden = (normed * scale + modulation[0:1, WIDTH:]).astype(BF)
    back = jnp.zeros((BLOCK, WIDTH), F32)
    for k in range(3):
        at = slice(WIDTH * k, WIDTH * (k + 1))
        back = back + nt(parts[k], in_weight[:, at])
        put_halves(place, keep, send, 256 * k, tn(hidden, parts[k]).astype(BF))
    token_grad[...] = self_grad[...] + norm_back(normed, inverse, back * scale)
    scale_grad = jnp.sum(back * normed, axis=0, keepdims=True)
    shift_grad = jnp.sum(back, axis=0, keepdims=True)
    cam = camera[...].astype(F32)
    cam_act = cam * jax.nn.sigmoid(cam)
    row = lax.broadcasted_iota(jnp.int32, (32, WIDTH), 0)
    item = place[1]
    first = place[2] == 0
    small = jnp.where(row == item, scale_grad, 0.0)
    small = small + jnp.where(row == 4 + item, shift_grad, 0.0)
    small = small + jnp.where(jnp.logical_and(first, row == 8 + item), cam_act[:, :WIDTH], 0.0)
    small = small + jnp.where(jnp.logical_and(first, row == 12 + item), cam_act[:, WIDTH:], 0.0)
    small = small + jnp.where(row == 16, vectors[0:1, :], 0.0)
    small = small + jnp.where(row == 17, vectors[1:2, :], 0.0)
    small = small + jnp.where(row == 18, vectors[2:3, :], 0.0)
    small = small + jnp.where(row == 19, vectors[3:4, :], 0.0)
    put_halves(place, keep, send, 768, pair_value[...])
    keep[960:992, :] = small.astype(BF)
    send[960:992, :] = small.astype(BF)
    keep[992:1024, :] = jnp.zeros((32, WIDTH), BF)
    send[992:1024, :] = jnp.zeros((32, WIDTH), BF)


def sum_split_kernel(which, place, *refs):
    parts, pieces = refs[:-4], refs[-4:]
    rows = pieces[0].shape[0]
    for k in range(4):
        at = pl.ds(pl.multiple_of(lax.rem(place[which] + k, 4) * rows, rows), rows)
        total = parts[0][at, :].astype(F32)
        for part in parts[1:]:
            total = total + part[at, :].astype(F32)
        pieces[k][...] = total.astype(BF)


def halves_kernel(place, value, mine, other):
    rows = mine.shape[0]
    mine[...] = value[pl.ds(pl.multiple_of(place[0] * rows, rows), rows), :]
    other[...] = value[pl.ds(pl.multiple_of((1 - place[0]) * rows, rows), rows), :]


def sum_kernel(*refs):
    total = refs[0][...].astype(F32)
    for part in refs[1:-1]:
        total = total + part[...].astype(F32)
    refs[-1][...] = total.astype(BF)


def sum_pairs_kernel(first, second, third, fourth, out):
    rows = first.shape[0]
    out[0:rows, :] = (first[...].astype(F32) + second[...].astype(F32)).astype(BF)
    out[rows : 2 * rows, :] = (third[...].astype(F32) + fourth[...].astype(F32)).astype(BF)


def arrange_kernel(which, place, *refs):
    pieces, out = refs[:-1], refs[-1]
    rows = pieces[0].shape[0]
    for k in range(4):
        at = pl.ds(pl.multiple_of(lax.rem(place[which] + 4 - k, 4) * rows, rows), rows)
        out[at, :] = pieces[k][...]


def sum_far_kernel(far_pieces, out, pieces, semaphores):
    count = pieces.shape[0] // 4
    copies = []
    for k in range(4):
        at = slice(count * k, count * (k + 1))
        copies.append(pltpu.make_async_copy(far_pieces.at[at], pieces.at[at], semaphores.at[k]))
        copies[-1].start()
    total = None
    for k in range(4):
        copies[k].wait()
        for j in range(count * k, count * (k + 1)):
            piece = pieces[j].astype(F32)
            total = piece if total is None else total + piece
    out[...] = total.astype(BF)


def sum_pieces_kernel(pieces, *outs):
    total = pieces[0].astype(F32)
    for k in range(1, pieces.shape[0]):
        total = total + pieces[k].astype(F32)
    total = total.astype(BF)
    for out in outs:
        if len(out.shape) == 2:
            out[...] = total
        else:
            for k in range(out.shape[0]):
                out[k] = total


def write_halves(core, early, late, outs, buffers, semaphores):
    up_grad, down_grad, self_in, pair, self_out, cross_query, cross_out = outs
    up_part, down_part, in_part, pair_part, out_part, query_part, cross_part = buffers
    copies = []

    def send(part, target, slot):
        rows = part.shape[0]
        at = pl.ds(pl.multiple_of(core * rows, rows), rows)
        copies.append(pltpu.make_async_copy(part, target.at[at, :], semaphores.at[slot]))
        copies[-1].start()

    for k in range(4):
        up_part[:, 512 * k : 512 * (k + 1)] = early[256 * k : 256 * (k + 1), :].astype(F32)
    send(up_part, up_grad, 0)
    down_part[...] = early[1024:2048, :].astype(F32)
    send(down_part, down_grad, 1)
    for k in range(3):
        in_part[:, 512 * k : 512 * (k + 1)] = late[256 * k : 256 * (k + 1), :].astype(F32)
    send(in_part, self_in, 2)
    pair_part[:, :WIDTH] = early[2816:3008, :].astype(F32)
    pair_part[:, WIDTH:] = late[768:960, :].astype(F32)
    send(pair_part, pair, 3)
    out_part[...] = early[2560:2816, :].astype(F32)
    send(out_part, self_out, 4)
    query_part[...] = early[2304:2560, :].astype(F32)
    send(query_part, cross_query, 5)
    cross_part[...] = early[2048:2304, :].astype(F32)
    send(cross_part, cross_out, 6)
    return copies


def own_out_kernel(place, early, late, *refs):
    mod_weight, mod_bias, gain_two, offset_two, gain_three, offset_three = refs[7:13]
    small = late[960:992, :].astype(F32)
    grads = small[0:8, :]
    acts = small[8:16, :].astype(BF)
    head = lax.broadcasted_iota(jnp.int32, (8, WIDTH), 0) < 4
    turned = pltpu.roll(grads, 4, 0)
    mod_weight[:WIDTH, :WIDTH] = tn(acts, jnp.where(head, grads, 0.0).astype(BF))
    mod_weight[:WIDTH, WIDTH:] = tn(acts, jnp.where(head, turned, 0.0).astype(BF))
    mod_weight[WIDTH:, :WIDTH] = tn(acts, jnp.where(head, 0.0, turned).astype(BF))
    mod_weight[WIDTH:, WIDTH:] = tn(acts, jnp.where(head, 0.0, grads).astype(BF))
    mod_weight.send()
    gain_two[...] = small[16:17, :]
    offset_two[...] = small[17:18, :]
    gain_three[...] = small[18:19, :]
    offset_three[...] = small[19:20, :]
    mod_bias[:, :WIDTH] = jnp.sum(jnp.where(head, grads, 0.0), axis=0, keepdims=True)
    mod_bias[:, WIDTH:] = jnp.sum(jnp.where(head, 0.0, grads), axis=0, keepdims=True)
    for copy in write_halves(place[0], early, late, refs[:7], refs[13:20], refs[20]):
        copy.wait()


def other_out_kernel(place, early, late, *refs):
    for copy in write_halves(1 - place[0], early, late, refs[7:14], refs[14:21], refs[21]):
        copy.wait()


def index_of(x, y, z, core):
    return ((z % 2) * 2 + core) * 32 + (y * 4 + x) * 2 + z // 2


CHIPS = [(x, y, z) for x in range(4) for y in range(4) for z in range(4)]
SAME_CORE = [[index_of(*chip, core) for chip in CHIPS] for core in range(2)]
SAME_PLANE = [
    [index_of(x, y, z, core) for x in range(4) for y in range(4)] for z in range(4) for core in range(2)
]
OTHER_CORE = [
    (index_of(*chip, core), index_of(*chip, 1 - core)) for chip in CHIPS for core in range(2)
]


def shift_of(axis, step):
    moves = []
    for chip in CHIPS:
        there = list(chip)
        there[axis] = (there[axis] + step) % 4
        moves += [(index_of(*chip, core), index_of(*there, core)) for core in range(2)]
    return moves


SHIFTS = {(axis, step): shift_of(axis, step) for axis in range(3) for step in (1, 2, 3)}


def exchange(message):
    return lax.all_to_all(message, "seq", 0, 0, tiled=True)


def swap_cores(value):
    return lax.ppermute(value, AXES, OTHER_CORE)


def scatter_ring(pieces, axis):
    return (pieces[0],) + tuple(lax.ppermute(pieces[k], AXES, SHIFTS[axis, k]) for k in (1, 3, 2))


def gather_ring(piece, axis):
    came = {k: lax.ppermute(piece, AXES, SHIFTS[axis, k]) for k in (1, 3, 2)}
    return piece, came[1], came[2], came[3]


def sum_split(place, parts, axis):
    rows = parts[0].shape[0] // 4
    return call(
        functools.partial(sum_split_kernel, 3 + axis), (shape((rows, WIDTH), BF),) * 4, (place, *parts),
        traffic=4e5, smem=(0,),
    )


def sum_all(parts):
    return call(sum_kernel, shape(parts[0].shape, BF), parts, traffic=4e5)


def arrange(place, parts, axis):
    return call(
        functools.partial(arrange_kernel, 3 + axis), shape((4 * parts[0].shape[0], WIDTH), BF), (place, *parts),
        traffic=4e5, smem=(0,),
    )


def scatter_chips(value):
    rows = value.shape[0] // 64
    return lax.all_to_all(
        value.reshape(64, rows, WIDTH), AXES, 0, 0, tiled=True, axis_index_groups=SAME_CORE
    )


def in_one_step(always, work, *values):
    def nothing(*values):
        return jax.tree.map(lambda v: jnp.zeros(v.shape, v.dtype), jax.eval_shape(work, *values))

    return lax.cond(always, work, nothing, *values)


def body(
    tokens, camera, features, foreground, layout, modulation_weight, modulation_bias,
    self_in_weight, self_out_weight, cross_norm_gain, cross_norm_bias, cross_query_weight,
    cross_pair_weight, cross_out_weight, feed_norm_gain, feed_norm_bias, up_weight, down_weight,
    cotangent,
):
    tokens = tokens[0]
    features = features[0]
    cotangent = cotangent[0]
    row = lambda v: v.reshape(1, -1)
    step = functools.partial(in_one_step, layout[0, 0] >= 0)
    gain_two, offset_two = row(cross_norm_gain), row(cross_norm_bias)
    gain_three, offset_three = row(feed_norm_gain), row(feed_norm_bias)
    item, spot = lax.axis_index("batch"), lax.axis_index("seq")
    place = jnp.stack(
        [item & 1, item, spot, (spot >> 1) & 3, spot >> 3, (spot & 1) * 2 + (item >> 1)]
    ).astype(jnp.int32)

    message, modulation = call(
        prepare_kernel,
        (shape((PEERS, 256, 128), BF), shape((8, 1024))),
        (foreground, layout, tokens, features, camera, modulation_weight, modulation_bias, self_in_weight),
        flops=1e9, traffic=8e6, smem=(0, 1), late=(4, 5, 2, 7, 3), far_out=(0,), limit=57,
        scratch=(pltpu.VMEM((PEERS, 256, 128), BF), pltpu.SemaphoreType.DMA((HEADS,))),
    )
    received = exchange(message)
    message, attended_turned, log_total, pairs_turned = call(
        attend_kernel,
        (shape((PEERS, 16, 128), BF), shape((64, QUERIES)), shape((8, QUERIES)), shape((128, TOKENS), BF)),
        (received,),
        scratch=(
            pltpu.VMEM((TOKENS, 128), BF), pltpu.VMEM((QUERIES, 128), BF), pltpu.VMEM((TOKENS, ROWS), F32),
            pltpu.VMEM((128, QUERIES), F32), pltpu.VMEM((QUERIES, 128), F32),
        ),
        flops=9e9, traffic=4e6,
    )
    back = exchange(message)
    keys, values, keys_turned, values_turned, every_turned, kept = call(
        pairs_kernel,
        (
            shape((PATCHES, WIDTH), BF), shape((PATCHES, WIDTH), BF), shape((WIDTH, PATCHES), BF),
            shape((WIDTH, PATCHES), BF), shape((384, PATCHES), BF),
            shape((PEERS, 160, 128), BF),
        ),
        (received, cross_pair_weight),
        scratch=(pltpu.VMEM((PATCHES, 384), BF),),
        flops=3e9, traffic=8e6, late=(1,), away=(5, 0, 1, 2, 3, 4),
    )
    (
        block_out, early_keep, early_send, vectors, message, self_grad, feature_message, pair_value,
    ) = call(
        middle_kernel,
        (
            shape((BLOCK, WIDTH)), shape((3072, WIDTH), BF), shape((3072, WIDTH), BF), shape((8, WIDTH)),
            shape((PEERS, 16, 128), BF), shape((BLOCK, WIDTH)), shape((PEERS, 96, 128), BF), shape((384, WIDTH), BF),
        ),
        (
            place, back, tokens, keys, keys_turned, values, values_turned, self_out_weight, gain_two, offset_two,
            cross_query_weight, cross_out_weight, gain_three, offset_three, up_weight, down_weight, cotangent,
            every_turned, cross_pair_weight,
        ),
        scratch=(
            pltpu.VMEM((2, 3072, WIDTH), BF), pltpu.SemaphoreType.DMA((2, 2)), pltpu.VMEM((PATCHES, WIDTH), BF),
            pltpu.VMEM((PATCHES, WIDTH), BF), pltpu.VMEM((BLOCK, WIDTH), F32), pltpu.VMEM((BLOCK, WIDTH), F32),
        ),
        flops=1.6e10, traffic=2e7, smem=(0,), late=(7, 2, 10, 3, 6, 11, 14, 16, 15, 5, 4, 17, 18), limit=57,
        far_out=(1, 2),
    )

    def attend_back(message):
        given = exchange(message)
        total = sum_all((early_keep, swap_cores(early_send)))
        given, total = lax.optimization_barrier((given, total))
        pieces = scatter_chips(total)
        message = call(
            attend_back_kernel,
            shape((PEERS, 240, 128), BF),
            (kept, pairs_turned, attended_turned, log_total, given, feature_message),
            scratch=(
                pltpu.VMEM((TOKENS, 128), BF), pltpu.VMEM((TOKENS, 128), BF), pltpu.VMEM((QUERIES, 128), BF),
                pltpu.VMEM((QUERIES, 128), BF), pltpu.VMEM((8, QUERIES), F32),
                pltpu.VMEM((BACK_KEYS, QUERIES), BF), pltpu.VMEM((BACK_KEYS, QUERIES), BF),
                pltpu.VMEM((128, QUERIES), F32), pltpu.VMEM((QUERIES, 128), F32),
            ),
            flops=1.6e10, traffic=8e6, late=(0, 2, 1, 3),
        )
        return message, pieces

    message, pieces = step(attend_back, message)
    early = call(
        sum_far_kernel, shape((48, WIDTH), BF), (pieces,), traffic=3e6, far_in=(0,),
        scratch=(pltpu.VMEM(pieces.shape, BF), pltpu.SemaphoreType.DMA((4,))),
    )
    early = lax.all_gather(early, AXES, axis=0, tiled=True, axis_index_groups=SAME_CORE)

    def finish(message):
        returned = exchange(message)
        token_grad, feature_grad, keep, send = call(
            finish_kernel,
            (shape((BLOCK, WIDTH)), shape((32, 384)), shape((1024, WIDTH), BF), shape((1024, WIDTH), BF)),
            (
                place, returned, tokens, camera, modulation, self_grad, self_in_weight, vectors,
                pair_value,
            ),
            flops=3e9, traffic=8e6, smem=(0,), late=(2, 6, 4, 5),
        )
        pieces = scatter_chips(sum_all((keep, swap_cores(send))))
        total = call(sum_pieces_kernel, shape(pieces.shape, BF), (pieces,), traffic=2e6)
        late = lax.all_to_all(
            total, AXES, 0, 0, tiled=True, axis_index_groups=SAME_CORE
        ).reshape(1024, WIDTH)
        return token_grad, feature_grad, late

    token_grad, feature_grad, late = step(finish, message)
    early, late = lax.optimization_barrier((early, late))
    early_other, late_other = swap_cores(early), swap_cores(late)
    square = shape((WIDTH, WIDTH))
    vector = shape((1, WIDTH))
    grads = (shape((WIDTH, 2048)), shape((2048, WIDTH)), shape((WIDTH, 3 * WIDTH)), shape((384, 1024))) + (square,) * 3
    halves = tuple(pltpu.VMEM((g.shape[0] // 2, g.shape[1]), F32) for g in grads)
    halves += (pltpu.SemaphoreType.DMA((7,)),)
    *grads, mod_weight_grad, mod_bias_grad, gain_two_grad, offset_two_grad, gain_three_grad, offset_three_grad = call(
        own_out_kernel, grads + (shape((1024, 1024)), shape((1, 1024))) + (vector,) * 4, (place, early, late),
        scratch=halves, traffic=1.4e7, smem=(0,), late=(1,), away=(7,), far_out=tuple(range(7)), limit=57,
    )
    up_grad, down_grad, self_in_grad, pair_grad, self_out_grad, cross_query_grad, cross_out_grad = call(
        other_out_kernel,
        tuple(shape(g.shape) for g in grads),
        (place, early_other, late_other, *grads),
        scratch=halves, traffic=1.4e7, smem=(0,), far_in=tuple(range(3, 10)), far_out=tuple(range(7)),
        aliases={3 + k: k for k in range(7)},
    )
    return (
        block_out[None],
        token_grad[None],
        feature_grad[None],
        mod_weight_grad,
        mod_bias_grad[0],
        self_in_grad,
        self_out_grad,
        gain_two_grad[0],
        offset_two_grad[0],
        cross_query_grad,
        pair_grad,
        cross_out_grad,
        gain_three_grad[0],
        offset_three_grad[0],
        up_grad,
        down_grad,
    )


def solution(mesh):
    split = P("batch", "seq", None)
    in_specs = (
        (split, P("batch", None), split, P("batch", None), P("batch", "seq")) + (P(),) * 13 + (split,)
    )
    out_specs = (split,) * 3 + (P(),) * 13
    return jax.shard_map(body, mesh=mesh, in_specs=in_specs, out_specs=out_specs, check_vma=False)
```

```python
import functools

import jax
import jax.numpy as jnp
from jax import lax
from jax.experimental import pallas as pl
from jax.experimental.pallas import tpu as pltpu
from jax.sharding import PartitionSpec as P

HEADS = 8
HEAD_DIM = 64
BLOCK = 128
TRIB = 24
PATCHB = 8
WIDTH = 512
PATCHES = 1024
TOKENS = 4096
EPSILON = 1e-05
MASKED = -1e30
FLAG = 3e38
SCALE = HEAD_DIM ** (-0.5)
BF = jnp.bfloat16
F32 = jnp.float32
AXES = ("batch", "seq")
PEERS = 32
QUARTERS = 4
SHARE = BLOCK // QUARTERS
MIB = 1024 * 1024


def nn(a, b):
    return lax.dot_general(a, b, (((1,), (0,)), ((), ())), preferred_element_type=F32)


def nt(a, b):
    return lax.dot_general(a, b, (((1,), (1,)), ((), ())), preferred_element_type=F32)


def tn(a, b):
    return lax.dot_general(a, b, (((0,), (0,)), ((), ())), preferred_element_type=F32)


def half_turn(values):
    return pltpu.roll(values, 64, 1)


def low_lanes(rows):
    return lax.broadcasted_iota(jnp.int32, (rows, 128), 1) < 64


def norm_parts(values):
    centre = jnp.mean(values, axis=-1, keepdims=True)
    centred = values - centre
    spread = jnp.mean(centred * centred, axis=-1, keepdims=True)
    inverse = lax.rsqrt(spread + EPSILON)
    return centred * inverse, inverse


def norm_back(normed, inverse, grad):
    first = jnp.mean(grad, axis=-1, keepdims=True)
    second = jnp.mean(grad * normed, axis=-1, keepdims=True)
    return inverse * (grad - first - normed * second)


class Late:
    def __init__(self, copy, ref):
        self.copy, self.ref, self.here, self.shape = copy, ref, False, ref.shape

    def ready(self):
        if not self.here:
            self.copy.wait()
            self.here = True
        return self.ref

    def __getitem__(self, index):
        return self.ready()[index]


class Away:
    def __init__(self, ref, copy):
        self.ref, self.copy, self.sent, self.shape = ref, copy, False, ref.shape

    def __setitem__(self, index, value):
        self.ref[index] = value

    def send(self):
        if not self.sent:
            self.copy.start()
            self.sent = True


def call(
    kernel, out_shape, inputs, scratch=(), flops=0, traffic=0, limit=32, smem=(), late=(), away=(), far_out=(),
    far_in=(), aliases=None,
):
    vmem = pl.BlockSpec(memory_space=pltpu.VMEM)
    scalar = pl.BlockSpec(memory_space=pltpu.SMEM)
    far = pl.BlockSpec(memory_space=pltpu.HBM)
    single = not isinstance(out_shape, tuple)
    outs = (out_shape,) if single else out_shape
    count, extra = len(inputs), len(scratch)
    def whole(*refs):
        refs = list(refs)
        ins, results = refs[:count], refs[count : count + len(outs)]
        rest = refs[count + len(outs) :]
        mine, buffers = rest[:extra], rest[extra:]
        semaphores = buffers[-1] if late or away else None
        for k, which in enumerate(late):
            copy = pltpu.make_async_copy(ins[which], buffers[k], semaphores.at[k])
            copy.start()
            ins[which] = Late(copy, buffers[k])
        for k, which in enumerate(away):
            buffer = buffers[len(late) + k]
            results[which] = Away(
                buffer, pltpu.make_async_copy(buffer, results[which], semaphores.at[len(late) + k])
            )
        kernel(*ins, *results, *mine)
        for which in late:
            ins[which].ready()
        for which in away:
            results[which].send()
        for which in away:
            results[which].copy.wait()

    buffers = [pltpu.VMEM(inputs[k].shape, inputs[k].dtype) for k in late]
    buffers += [pltpu.VMEM(outs[k].shape, outs[k].dtype) for k in away]
    if buffers:
        buffers.append(pltpu.SemaphoreType.DMA((len(buffers),)))
    out_specs = tuple(far if k in away or k in far_out else vmem for k in range(len(outs)))
    return pl.pallas_call(
        whole,
        out_shape=out_shape,
        in_specs=[scalar if k in smem else far if k in late or k in far_in else vmem for k in range(count)],
        out_specs=out_specs[0] if single else out_specs,
        scratch_shapes=list(scratch) + buffers,
        input_output_aliases=aliases or {},
        compiler_params=pltpu.CompilerParams(vmem_limit_bytes=limit * MIB),
        cost_estimate=pl.CostEstimate(
            flops=int(flops), bytes_accessed=int(traffic), transcendentals=0
        ),
    )(*inputs)


def shape(dims, dtype=F32):
    return jax.ShapeDtypeStruct(dims, dtype)


def prepare_kernel(
    foreground, layout, tokens, features, camera, mod_weight, mod_bias, in_weight,
    far_message, modulation, message, semaphores,
):
    for to in range(PEERS):
        for k in range(3):
            message[to, 144 + 32 * k : 176 + 32 * k, :] = features[:, 128 * k : 128 * (k + 1)]
    cam = camera[...].astype(F32)
    cam_act = (cam * jax.nn.sigmoid(cam)).astype(BF)
    mod = nn(jnp.broadcast_to(cam_act, (16, cam_act.shape[1])), mod_weight[...])[0:8]
    mod = mod + mod_bias[...].astype(F32).reshape(1, 2 * WIDTH)
    modulation[...] = mod
    block = layout[0, 0]
    lit = jnp.int32(0)
    for k in range(PATCHB):
        lit = lit + jnp.where(block - TRIB == k, foreground[0, k], 0)
    kept = jnp.logical_or(block < TRIB, lit > 0)
    normed, _ = norm_parts(tokens[...].astype(F32))
    hidden = (normed * (1.0 + mod[0:1, :WIDTH]) + mod[0:1, WIDTH:]).astype(BF)
    projected = nn(hidden, in_weight[...]).astype(BF).astype(F32)
    low = low_lanes(BLOCK)
    low_half = low_lanes(16)
    corner = jnp.logical_and(
        lax.broadcasted_iota(jnp.int32, (BLOCK, 128), 0) == 0, lax.broadcasted_iota(jnp.int32, (BLOCK, 128), 1) == 0
    )
    flagged = jnp.logical_and(corner, jnp.logical_not(kept))
    for pair in range(HEADS // 2):
        at = 128 * pair
        query = projected[:, at : at + 128] * SCALE
        key = projected[:, WIDTH + at : WIDTH + at + 128]
        value = projected[:, 2 * WIDTH + at : 2 * WIDTH + at + 128]
        query_turned = half_turn(query)
        for odd in range(2):
            head = 2 * pair + odd
            if odd:
                both = jnp.where(low, half_turn(key), value)
                first, second = query_turned, query
            else:
                both = jnp.where(low, key, half_turn(value))
                first, second = query, query_turned
            both = jnp.where(flagged, FLAG, both).astype(BF)
            for quarter in range(QUARTERS):
                to = QUARTERS * head + quarter
                message[to, 0:128, :] = both
                top = SHARE * quarter
                message[to, 128:144, :] = jnp.where(
                    low_half, first[top : top + 16], second[top + 16 : top + 32]
                ).astype(BF)
            some = slice(QUARTERS * head, QUARTERS * (head + 1))
            pltpu.make_async_copy(message.at[some], far_message.at[some], semaphores.at[head]).start()
    for head in range(HEADS):
        some = slice(QUARTERS * head, QUARTERS * (head + 1))
        pltpu.make_async_copy(message.at[some], far_message.at[some], semaphores.at[head]).wait()


def loop(count, work, unroll=1):
    def turn(k, carry):
        work(k)
        return carry

    lax.fori_loop(0, count, turn, 0, unroll=unroll)


def block_of(k, size):
    return pl.ds(pl.multiple_of(k * size, size), size)


def gather_keys(received, masked_keys, pairs, queries, turned):
    low = low_lanes(128)
    lane = lax.broadcasted_iota(jnp.int32, (128, 128), 1)
    lane_q = lax.broadcasted_iota(jnp.int32, (16, 128), 1)
    extra = jnp.where(lane_q == 64, 1.0, 0.0)

    def gather(k):
        at = block_of(k, 128)
        both = received[k, 0:128, :].astype(F32)
        mine = received[k, 128:144, :].astype(F32)
        masked = both[0:1, 0:1] > 1e38
        masked_keys[at, :] = jnp.where(
            low, jnp.where(masked, 0.0, both), jnp.where(jnp.logical_and(masked, lane == 64), MASKED, 0.0)
        ).astype(BF)
        if pairs is not None:
            pairs[at, :] = received[k, 0:128, :]
        if turned is not None:
            turned[:, at] = jnp.transpose(both).astype(BF)
        first = pl.ds(pl.multiple_of(SHARE * k, 16), 16)
        second = pl.ds(pl.multiple_of(SHARE * k + 16, 16), 16)
        queries[first, :] = jnp.where(lane_q < 64, mine, extra).astype(BF)
        queries[second, :] = jnp.where(lane_q < 64, half_turn(mine), extra).astype(BF)

    loop(PEERS, gather, 4)


KEYS = 512
ROWS = 1024
UNROLL_A = 2
UNROLL_B = 4
UNROLL_C = 1
BACK_KEYS = 1024
BACK_ROWS = 256
QUERIES = PEERS * SHARE


def attend_kernel(
    received, message, attended, log_total, pairs_turned, masked_keys, queries, scores, mixed, turned
):
    gather_keys(received, masked_keys, None, queries, pairs_turned)
    chunks = TOKENS // KEYS
    query = queries[...]

    def score(k, top):
        at = block_of(k, KEYS)
        part = nt(masked_keys[at, :], query)
        scores[at, :] = part
        return jnp.maximum(top, jnp.max(part, axis=0, keepdims=True))

    top = lax.fori_loop(0, chunks, score, jnp.full((1, ROWS), -jnp.inf, F32), unroll=UNROLL_A)
    mixed[...] = jnp.zeros_like(mixed)

    def mix(k, total):
        at = block_of(k, KEYS)
        chance = jnp.exp(scores[at, :] - top)
        mixed[...] += nn(pairs_turned[:, at], chance.astype(BF))
        return total + jnp.sum(chance, axis=0, keepdims=True)

    total = lax.fori_loop(0, chunks, mix, jnp.zeros((1, ROWS), F32), unroll=UNROLL_B)
    result = mixed[...] / total
    attended[...] = result[64:128, :]
    log_total[...] = jnp.broadcast_to(top + jnp.log(total), (8, ROWS))
    turned[...] = jnp.transpose(result)
    low = low_lanes(16)

    def pack(k):
        first = turned[pl.ds(pl.multiple_of(SHARE * k, 16), 16), :]
        second = turned[pl.ds(pl.multiple_of(SHARE * k + 16, 16), 16), :]
        message[k] = jnp.where(low, half_turn(first), second).astype(BF)

    loop(PEERS, pack, 4)


def pairs_kernel(
    received, pair_weight, keys, values, keys_turned, values_turned, every_turned, kept, every
):
    pair_weight = pair_weight.ready()

    def gather(k):
        for j in range(3):
            every[block_of(k, 32), 128 * j : 128 * (j + 1)] = received[k, 144 + 32 * j : 176 + 32 * j, :]
        kept.ref[k] = received[k, 0:144, :]

    def project(k):
        rows = block_of(k, 256)
        part = every[rows, :]
        every_turned.ref[:, rows] = jnp.transpose(part.astype(F32)).astype(BF)
        both = nn(part, pair_weight[...]).astype(BF)
        keys.ref[rows, :] = both[:, :WIDTH]
        values.ref[rows, :] = both[:, WIDTH:]
        turned = jnp.transpose(both.astype(F32)).astype(BF)
        keys_turned.ref[:, rows] = turned[:WIDTH, :]
        values_turned.ref[:, rows] = turned[WIDTH:, :]

    loop(PEERS, gather, 4)
    kept.send()
    loop(PATCHES // 256, project)


def unpack_heads(received):
    low = low_lanes(16)
    columns = []
    for pair in range(HEADS // 2):
        pieces = []
        for quarter in range(QUARTERS):
            even = received[QUARTERS * (2 * pair) + quarter].astype(F32)
            odd = received[QUARTERS * (2 * pair + 1) + quarter].astype(F32)
            pieces.append(jnp.where(low, even, half_turn(odd)))
            pieces.append(jnp.where(low, half_turn(even), odd))
        columns.append(jnp.concatenate(pieces, axis=0))
    return jnp.concatenate(columns, axis=1)


def pack_heads(values, message):
    low = low_lanes(16)
    for pair in range(HEADS // 2):
        for quarter in range(QUARTERS):
            first = values[SHARE * quarter : SHARE * quarter + 16, 128 * pair : 128 * (pair + 1)]
            second = values[SHARE * quarter + 16 : SHARE * (quarter + 1), 128 * pair : 128 * (pair + 1)]
            message[QUARTERS * (2 * pair) + quarter] = jnp.where(
                low, first, half_turn(second)
            ).astype(BF)
            message[QUARTERS * (2 * pair + 1) + quarter] = jnp.where(
                low, half_turn(first), second
            ).astype(BF)


GELU = 0.7978845608028654
CUBE = 0.044715


def put(place, keep, send, owner, rows, value):
    @pl.when(place[0] == owner)
    def _():
        keep[rows, :] = value

    @pl.when(place[0] != owner)
    def _():
        send[rows, :] = value


def middle_kernel(
    place, received, tokens, keys, keys_turned, values, values_turned, self_out, gain_two, offset_two,
    query_weight, cross_out, gain_three, offset_three, up_weight, down_weight, cotangent, every_turned, pair_weight,
    block_out, feed_keep, feed_send, vectors, message, self_grad, feature_part, pair_value,
    feed_pack, semaphores, key_all, value_all, total_out, total_back,
):
    def move(start, rows, to, slot):
        at = slice(to, to + rows)

        @pl.when(place[0] == 0)
        def _():
            pltpu.make_async_copy(feed_pack.at[0, start : start + rows], feed_keep.at[at], semaphores.at[slot, 0]).start()
            pltpu.make_async_copy(feed_pack.at[1, start : start + rows], feed_send.at[at], semaphores.at[slot, 1]).start()

        @pl.when(place[0] != 0)
        def _():
            pltpu.make_async_copy(feed_pack.at[1, start : start + rows], feed_keep.at[at], semaphores.at[slot, 0]).start()
            pltpu.make_async_copy(feed_pack.at[0, start : start + rows], feed_send.at[at], semaphores.at[slot, 1]).start()

    def put_halves(start, value):
        rows = value.shape[0] // 2
        feed_pack[0, start : start + rows, :] = value[:rows]
        feed_pack[1, start : start + rows, :] = value[rows:]

    attended_low = unpack_heads(received).astype(BF)
    first = tokens[...].astype(F32) + nn(attended_low, self_out[...])
    normed_two, inverse_two = norm_parts(first)
    gain = gain_two[...].astype(F32)
    hidden = (normed_two * gain + offset_two[...].astype(F32)).astype(BF)
    queries = nn(hidden, query_weight[...]).astype(BF).astype(F32) * SCALE
    low = low_lanes(BLOCK)
    upper = lax.broadcasted_iota(jnp.int32, (128, BLOCK), 0) < 64
    masked = []
    chances = []
    pieces = []
    for pair in range(HEADS // 2):
        at = slice(128 * pair, 128 * (pair + 1))
        key = keys[:, at]
        value = values_turned[at, :]
        parts = []
        for odd in range(2):
            mine = jnp.where(low if odd == 0 else jnp.logical_not(low), queries[:, at], 0.0).astype(BF)
            scores = nt(key, mine)
            chance = jnp.exp(scores - jnp.max(scores, axis=0, keepdims=True))
            chance = chance * (1.0 / jnp.sum(chance, axis=0, keepdims=True))
            masked.append(mine)
            chances.append(chance)
            parts.append(nn(value, chance.astype(BF)))
        pieces.append(jnp.transpose(jnp.where(upper, parts[0], parts[1])))
    mixed = jnp.concatenate(pieces, axis=1).astype(BF)
    second = first + nn(mixed, cross_out[...])
    normed, inverse = norm_parts(second)
    gain_out = gain_three[...].astype(F32)
    hidden3 = (normed * gain_out + offset_three[...].astype(F32)).astype(BF)
    grad_low = cotangent[...]
    total_out[...] = second
    total_back[...] = jnp.zeros((BLOCK, WIDTH), F32)
    up_all, down_all = up_weight.ready(), down_weight.ready()

    def feed_block(k, carry):
        at = pl.ds(pl.multiple_of(512 * k, 512), 512)
        up, down = up_all[:, at], down_all[at, :]
        pre = nn(hidden3, up)
        square = pre * pre
        turn = jnp.tanh(GELU * (pre + CUBE * (square * pre)))
        half = 0.5 * (1.0 + turn)
        active = (pre * half).astype(BF)
        slope = half + (0.5 * pre) * (1.0 - turn * turn) * (GELU * (1.0 + (3.0 * CUBE) * square))
        total_out[...] += nn(active, down)
        pre_grad = (nt(grad_low, down) * slope).astype(BF)
        total_back[...] += nt(pre_grad, up)
        grad = tn(hidden3, pre_grad).astype(BF)
        feed_pack[0, pl.ds(pl.multiple_of(256 * k, 256), 256), :] = grad[:256]
        feed_pack[1, pl.ds(pl.multiple_of(256 * k, 256), 256), :] = grad[256:]
        feed_pack[k // 2, pl.ds(pl.multiple_of(1024 + 512 * (k % 2), 512), 512), :] = tn(active, grad_low).astype(BF)
        return carry

    lax.fori_loop(0, 4, feed_block, 0, unroll=1)
    result = total_out[...]
    back = total_back[...]
    move(0, 2048, 0, 0)
    block_out[...] = result
    vectors[2:3, :] = jnp.sum(back * normed, axis=0, keepdims=True)
    vectors[3:4, :] = jnp.sum(back, axis=0, keepdims=True)
    grad = grad_low.astype(F32) + norm_back(normed, inverse, back * gain_out)
    branch = grad.astype(BF)
    put_halves(2048, tn(mixed, branch).astype(BF))
    mixed_grad = nt(branch, cross_out[...]).astype(BF).astype(F32)
    pieces = []
    pair_low = []
    for pair in range(HEADS // 2):
        at = slice(128 * pair, 128 * (pair + 1))
        value = values[:, at]
        key_turned = keys_turned[at, :]
        parts = []
        key_sum = None
        value_sum = None
        for odd in range(2):
            head = 2 * pair + odd
            given = jnp.where(low if odd == 0 else jnp.logical_not(low), mixed_grad[:, at], 0.0).astype(BF)
            chance = chances[head]
            chance_grad = nt(value, given)
            inner = jnp.sum(chance * chance_grad, axis=0, keepdims=True)
            score_grad = (chance * (chance_grad - inner)).astype(BF)
            parts.append(nn(key_turned, score_grad))
            key_part = nn(score_grad, masked[head])
            value_part = nn(chance.astype(BF), given)
            key_sum = key_part if key_sum is None else key_sum + key_part
            value_sum = value_part if value_sum is None else value_sum + value_part
        pair_low.append((key_sum.astype(BF), value_sum.astype(BF)))
        pieces.append(jnp.transpose(jnp.where(upper, parts[0], parts[1])) * SCALE)
    low_grad = jnp.concatenate(pieces, axis=1).astype(BF)
    back = nt(low_grad, query_weight[...])
    vectors[0:1, :] = jnp.sum(back * normed_two, axis=0, keepdims=True)
    vectors[1:2, :] = jnp.sum(back, axis=0, keepdims=True)
    vectors[4:8, :] = jnp.zeros((4, WIDTH), F32)
    grad = grad + norm_back(normed_two, inverse_two, back * gain)
    self_grad[...] = grad
    branch = grad.astype(BF)
    pack_heads(nt(branch, self_out[...]), message)
    put_halves(2304, tn(hidden, low_grad).astype(BF))
    put_halves(2560, tn(attended_low, branch).astype(BF))
    key_grad = jnp.concatenate([p[0] for p in pair_low], axis=1)
    value_grad = jnp.concatenate([p[1] for p in pair_low], axis=1)
    put_halves(2816, nn(every_turned[...], key_grad).astype(BF))
    pair_value[...] = nn(every_turned[...], value_grad).astype(BF)
    feed_pack[0, 3008:3072, :] = jnp.zeros((64, WIDTH), BF)
    feed_pack[1, 3008:3072, :] = jnp.zeros((64, WIDTH), BF)
    move(2048, 1024, 2048, 1)
    def feature_block(k, carry):
        rows = pl.ds(pl.multiple_of(256 * k, 256), 256)
        part = (nt(key_all[rows, :], pair_keys) + nt(value_all[rows, :], pair_values)).astype(BF)
        for i in range(8):
            for j in range(3):
                feature_part[8 * k + i, 32 * j : 32 * (j + 1), :] = part[
                    32 * i : 32 * (i + 1), 128 * j : 128 * (j + 1)
                ]
        return carry

    pair_keys, pair_values = pair_weight[:, :WIDTH], pair_weight[:, WIDTH:]
    key_all[...] = key_grad
    value_all[...] = value_grad
    lax.fori_loop(0, PATCHES // 256, feature_block, 0)
    for slot, rows in enumerate((2048, 1024)):
        for k in range(2):
            pltpu.make_async_copy(
                feed_pack.at[0, 0:rows], feed_keep.at[0:rows], semaphores.at[slot, k]
            ).wait()


def put_halves(place, keep, send, start, value):
    rows = value.shape[0] // 2
    put(place, keep, send, 0, slice(start, start + rows), value[:rows])
    put(place, keep, send, 1, slice(start, start + rows), value[rows:])


def attend_back_kernel(
    received, pairs_turned, attended, log_total, given, feature_part, message,
    masked_keys, pairs, queries, outer, outer_row, chances, score_grads, query_sum, turned,
):
    received = received.ready()
    gather_keys(received, masked_keys, pairs, queries, None)
    low = low_lanes(16)

    def unpack(k):
        piece = given[k].astype(F32)
        outer[pl.ds(pl.multiple_of(SHARE * k, 16), 16), :] = jnp.where(low, 0.0, half_turn(piece)).astype(BF)
        outer[pl.ds(pl.multiple_of(SHARE * k + 16, 16), 16), :] = jnp.where(low, 0.0, piece).astype(BF)
        message[k, 144:240, :] = feature_part[k]

    loop(PEERS, unpack, 4)
    attended = attended.ready()

    def inner(k):
        rows = block_of(k, 256)
        turned = jnp.transpose(outer[rows, :].astype(F32))[64:128, :]
        outer_row[:, rows] = jnp.broadcast_to(
            jnp.sum(turned * attended[:, rows], axis=0, keepdims=True), (8, 256)
        )

    loop(QUERIES // 256, inner)
    query_sum[...] = jnp.zeros_like(query_sum)
    pairs_turned, log_total = pairs_turned.ready(), log_total.ready()

    def chunk(turn, carry):
        at = pl.ds(pl.multiple_of(turn * BACK_KEYS, BACK_KEYS), BACK_KEYS)
        key = masked_keys[at, :]
        both = pairs[at, :]
        for k in range(QUERIES // BACK_ROWS):
            rows = slice(BACK_ROWS * k, BACK_ROWS * (k + 1))
            chance = jnp.exp(nt(key, queries[rows, :]) - log_total[0:1, rows])
            chance_grad = nt(both, outer[rows, :])
            chances[:, rows] = chance.astype(BF)
            score_grads[:, rows] = (chance * (chance_grad - outer_row[0:1, rows])).astype(BF)
        sums = nn(score_grads[...], queries[...])
        other = nn(chances[...], outer[...])
        sums = jnp.where(low_lanes(BACK_KEYS), sums, other).astype(BF)
        for k in range(BACK_KEYS // 128):
            message[turn * (BACK_KEYS // 128) + k, 0:128, :] = sums[128 * k : 128 * (k + 1), :]
        query_sum[...] += nn(pairs_turned[:, at], score_grads[...])
        return carry

    lax.fori_loop(0, TOKENS // BACK_KEYS, chunk, 0, unroll=UNROLL_C)
    turned[...] = jnp.transpose(query_sum[...]) * SCALE

    def pack(k):
        first = turned[pl.ds(pl.multiple_of(SHARE * k, 16), 16), :]
        second = turned[pl.ds(pl.multiple_of(SHARE * k + 16, 16), 16), :]
        message[k, 128:144, :] = jnp.where(low, first, half_turn(second)).astype(BF)

    loop(PEERS, pack, 4)


def finish_kernel(
    place, received, tokens, camera, modulation, self_grad, in_weight, vectors,
    pair_value, token_grad, feature_grad, keep, send,
):
    total = received[0, 144:240, :].astype(F32)
    for k in range(1, PEERS):
        total = total + received[k, 144:240, :].astype(F32)
    for j in range(3):
        feature_grad[:, 128 * j : 128 * (j + 1)] = total[32 * j : 32 * (j + 1), :]
    low = low_lanes(BLOCK)
    queries = []
    keys = []
    values = []
    for pair in range(HEADS // 2):
        sums = []
        for odd in range(2):
            head = 2 * pair + odd
            total = received[QUARTERS * head, 0:128, :].astype(F32)
            for quarter in range(1, QUARTERS):
                total = total + received[QUARTERS * head + quarter, 0:128, :].astype(F32)
            sums.append(total)
        keys.append(jnp.where(low, sums[0], half_turn(sums[1])))
        values.append(jnp.where(low, half_turn(sums[0]), sums[1]))
        low_half = low_lanes(16)
        pieces = []
        for quarter in range(QUARTERS):
            even = received[QUARTERS * (2 * pair) + quarter, 128:144, :].astype(F32)
            odd = received[QUARTERS * (2 * pair + 1) + quarter, 128:144, :].astype(F32)
            pieces.append(jnp.where(low_half, even, half_turn(odd)))
            pieces.append(jnp.where(low_half, half_turn(even), odd))
        queries.append(jnp.concatenate(pieces, axis=0))
    parts = [jnp.concatenate(p, axis=1).astype(BF) for p in (queries, keys, values)]
    normed, inverse = norm_parts(tokens[...].astype(F32))
    scale = 1.0 + modulation[0:1, :WIDTH]
    hidden = (normed * scale + modulation[0:1, WIDTH:]).astype(BF)
    back = jnp.zeros((BLOCK, WIDTH), F32)
    for k in range(3):
        at = slice(WIDTH * k, WIDTH * (k + 1))
        back = back + nt(parts[k], in_weight[:, at])
        put_halves(place, keep, send, 256 * k, tn(hidden, parts[k]).astype(BF))
    token_grad[...] = self_grad[...] + norm_back(normed, inverse, back * scale)
    scale_grad = jnp.sum(back * normed, axis=0, keepdims=True)
    shift_grad = jnp.sum(back, axis=0, keepdims=True)
    cam = camera[...].astype(F32)
    cam_act = cam * jax.nn.sigmoid(cam)
    row = lax.broadcasted_iota(jnp.int32, (32, WIDTH), 0)
    item = place[1]
    first = place[2] == 0
    small = jnp.where(row == item, scale_grad, 0.0)
    small = small + jnp.where(row == 4 + item, shift_grad, 0.0)
    small = small + jnp.where(jnp.logical_and(first, row == 8 + item), cam_act[:, :WIDTH], 0.0)
    small = small + jnp.where(jnp.logical_and(first, row == 12 + item), cam_act[:, WIDTH:], 0.0)
    small = small + jnp.where(row == 16, vectors[0:1, :], 0.0)
    small = small + jnp.where(row == 17, vectors[1:2, :], 0.0)
    small = small + jnp.where(row == 18, vectors[2:3, :], 0.0)
    small = small + jnp.where(row == 19, vectors[3:4, :], 0.0)
    put_halves(place, keep, send, 768, pair_value[...])
    keep[960:992, :] = small.astype(BF)
    send[960:992, :] = small.astype(BF)
    keep[992:1024, :] = jnp.zeros((32, WIDTH), BF)
    send[992:1024, :] = jnp.zeros((32, WIDTH), BF)


def sum_split_kernel(which, place, *refs):
    parts, pieces = refs[:-4], refs[-4:]
    rows = pieces[0].shape[0]
    for k in range(4):
        at = pl.ds(pl.multiple_of(lax.rem(place[which] + k, 4) * rows, rows), rows)
        total = parts[0][at, :].astype(F32)
        for part in parts[1:]:
            total = total + part[at, :].astype(F32)
        pieces[k][...] = total.astype(BF)


def halves_kernel(place, value, mine, other):
    rows = mine.shape[0]
    mine[...] = value[pl.ds(pl.multiple_of(place[0] * rows, rows), rows), :]
    other[...] = value[pl.ds(pl.multiple_of((1 - place[0]) * rows, rows), rows), :]


def sum_kernel(*refs):
    total = refs[0][...].astype(F32)
    for part in refs[1:-1]:
        total = total + part[...].astype(F32)
    refs[-1][...] = total.astype(BF)


def sum_pairs_kernel(first, second, third, fourth, out):
    rows = first.shape[0]
    out[0:rows, :] = (first[...].astype(F32) + second[...].astype(F32)).astype(BF)
    out[rows : 2 * rows, :] = (third[...].astype(F32) + fourth[...].astype(F32)).astype(BF)


def arrange_kernel(which, place, *refs):
    pieces, out = refs[:-1], refs[-1]
    rows = pieces[0].shape[0]
    for k in range(4):
        at = pl.ds(pl.multiple_of(lax.rem(place[which] + 4 - k, 4) * rows, rows), rows)
        out[at, :] = pieces[k][...]


def sum_far_kernel(far_pieces, out, pieces, semaphores):
    count = pieces.shape[0] // 4
    copies = []
    for k in range(4):
        at = slice(count * k, count * (k + 1))
        copies.append(pltpu.make_async_copy(far_pieces.at[at], pieces.at[at], semaphores.at[k]))
        copies[-1].start()
    total = None
    for k in range(4):
        copies[k].wait()
        for j in range(count * k, count * (k + 1)):
            piece = pieces[j].astype(F32)
            total = piece if total is None else total + piece
    out[...] = total.astype(BF)


def sum_pieces_kernel(pieces, *outs):
    total = pieces[0].astype(F32)
    for k in range(1, pieces.shape[0]):
        total = total + pieces[k].astype(F32)
    total = total.astype(BF)
    for out in outs:
        if len(out.shape) == 2:
            out[...] = total
        else:
            for k in range(out.shape[0]):
                out[k] = total


def write_halves(core, early, late, outs, buffers, semaphores):
    up_grad, down_grad, self_in, pair, self_out, cross_query, cross_out = outs
    up_part, down_part, in_part, pair_part, out_part, query_part, cross_part = buffers
    copies = []

    def send(part, target, slot):
        rows = part.shape[0]
        at = pl.ds(pl.multiple_of(core * rows, rows), rows)
        copies.append(pltpu.make_async_copy(part, target.at[at, :], semaphores.at[slot]))
        copies[-1].start()

    for k in range(4):
        up_part[:, 512 * k : 512 * (k + 1)] = early[256 * k : 256 * (k + 1), :].astype(F32)
    send(up_part, up_grad, 0)
    down_part[...] = early[1024:2048, :].astype(F32)
    send(down_part, down_grad, 1)
    for k in range(3):
        in_part[:, 512 * k : 512 * (k + 1)] = late[256 * k : 256 * (k + 1), :].astype(F32)
    send(in_part, self_in, 2)
    pair_part[:, :WIDTH] = early[2816:3008, :].astype(F32)
    pair_part[:, WIDTH:] = late[768:960, :].astype(F32)
    send(pair_part, pair, 3)
    out_part[...] = early[2560:2816, :].astype(F32)
    send(out_part, self_out, 4)
    query_part[...] = early[2304:2560, :].astype(F32)
    send(query_part, cross_query, 5)
    cross_part[...] = early[2048:2304, :].astype(F32)
    send(cross_part, cross_out, 6)
    return copies


def own_out_kernel(place, early, late, *refs):
    mod_weight, mod_bias, gain_two, offset_two, gain_three, offset_three = refs[7:13]
    small = late[960:992, :].astype(F32)
    grads = small[0:8, :]
    acts = small[8:16, :].astype(BF)
    head = lax.broadcasted_iota(jnp.int32, (8, WIDTH), 0) < 4
    turned = pltpu.roll(grads, 4, 0)
    mod_weight[:WIDTH, :WIDTH] = tn(acts, jnp.where(head, grads, 0.0).astype(BF))
    mod_weight[:WIDTH, WIDTH:] = tn(acts, jnp.where(head, turned, 0.0).astype(BF))
    mod_weight[WIDTH:, :WIDTH] = tn(acts, jnp.where(head, 0.0, turned).astype(BF))
    mod_weight[WIDTH:, WIDTH:] = tn(acts, jnp.where(head, 0.0, grads).astype(BF))
    mod_weight.send()
    gain_two[...] = small[16:17, :]
    offset_two[...] = small[17:18, :]
    gain_three[...] = small[18:19, :]
    offset_three[...] = small[19:20, :]
    mod_bias[:, :WIDTH] = jnp.sum(jnp.where(head, grads, 0.0), axis=0, keepdims=True)
    mod_bias[:, WIDTH:] = jnp.sum(jnp.where(head, 0.0, grads), axis=0, keepdims=True)
    for copy in write_halves(place[0], early, late, refs[:7], refs[13:20], refs[20]):
        copy.wait()


def other_out_kernel(place, early, late, *refs):
    for copy in write_halves(1 - place[0], early, late, refs[7:14], refs[14:21], refs[21]):
        copy.wait()


def index_of(x, y, z, core):
    return ((z % 2) * 2 + core) * 32 + (y * 4 + x) * 2 + z // 2


CHIPS = [(x, y, z) for x in range(4) for y in range(4) for z in range(4)]
SAME_CORE = [[index_of(*chip, core) for chip in CHIPS] for core in range(2)]
SAME_PLANE = [
    [index_of(x, y, z, core) for x in range(4) for y in range(4)] for z in range(4) for core in range(2)
]
OTHER_CORE = [
    (index_of(*chip, core), index_of(*chip, 1 - core)) for chip in CHIPS for core in range(2)
]


def shift_of(axis, step):
    moves = []
    for chip in CHIPS:
        there = list(chip)
        there[axis] = (there[axis] + step) % 4
        moves += [(index_of(*chip, core), index_of(*there, core)) for core in range(2)]
    return moves


SHIFTS = {(axis, step): shift_of(axis, step) for axis in range(3) for step in (1, 2, 3)}


def exchange(message):
    return lax.all_to_all(message, "seq", 0, 0, tiled=True)


def swap_cores(value):
    return lax.ppermute(value, AXES, OTHER_CORE)


def scatter_ring(pieces, axis):
    return (pieces[0],) + tuple(lax.ppermute(pieces[k], AXES, SHIFTS[axis, k]) for k in (1, 3, 2))


def gather_ring(piece, axis):
    came = {k: lax.ppermute(piece, AXES, SHIFTS[axis, k]) for k in (1, 3, 2)}
    return piece, came[1], came[2], came[3]


def sum_split(place, parts, axis):
    rows = parts[0].shape[0] // 4
    return call(
        functools.partial(sum_split_kernel, 3 + axis), (shape((rows, WIDTH), BF),) * 4, (place, *parts),
        traffic=4e5, smem=(0,),
    )


def sum_all(parts):
    return call(sum_kernel, shape(parts[0].shape, BF), parts, traffic=4e5)


def arrange(place, parts, axis):
    return call(
        functools.partial(arrange_kernel, 3 + axis), shape((4 * parts[0].shape[0], WIDTH), BF), (place, *parts),
        traffic=4e5, smem=(0,),
    )


def scatter_chips(value):
    rows = value.shape[0] // 64
    return lax.all_to_all(
        value.reshape(64, rows, WIDTH), AXES, 0, 0, tiled=True, axis_index_groups=SAME_CORE
    )


def in_one_step(always, work, *values):
    def nothing(*values):
        return jax.tree.map(lambda v: jnp.zeros(v.shape, v.dtype), jax.eval_shape(work, *values))

    return lax.cond(always, work, nothing, *values)


def body(
    tokens, camera, features, foreground, layout, modulation_weight, modulation_bias,
    self_in_weight, self_out_weight, cross_norm_gain, cross_norm_bias, cross_query_weight,
    cross_pair_weight, cross_out_weight, feed_norm_gain, feed_norm_bias, up_weight, down_weight,
    cotangent,
):
    tokens = tokens[0]
    features = features[0]
    cotangent = cotangent[0]
    row = lambda v: v.reshape(1, -1)
    step = functools.partial(in_one_step, layout[0, 0] >= 0)
    gain_two, offset_two = row(cross_norm_gain), row(cross_norm_bias)
    gain_three, offset_three = row(feed_norm_gain), row(feed_norm_bias)
    item, spot = lax.axis_index("batch"), lax.axis_index("seq")
    place = jnp.stack(
        [item & 1, item, spot, (spot >> 1) & 3, spot >> 3, (spot & 1) * 2 + (item >> 1)]
    ).astype(jnp.int32)

    message, modulation = call(
        prepare_kernel,
        (shape((PEERS, 240, 128), BF), shape((8, 1024))),
        (foreground, layout, tokens, features, camera, modulation_weight, modulation_bias, self_in_weight),
        flops=1e9, traffic=8e6, smem=(0, 1), late=(4, 5, 2, 7, 3), far_out=(0,), limit=57,
        scratch=(pltpu.VMEM((PEERS, 240, 128), BF), pltpu.SemaphoreType.DMA((HEADS,))),
    )
    received = exchange(message)
    message, attended_turned, log_total, pairs_turned = call(
        attend_kernel,
        (shape((PEERS, 16, 128), BF), shape((64, QUERIES)), shape((8, QUERIES)), shape((128, TOKENS), BF)),
        (received,),
        scratch=(
            pltpu.VMEM((TOKENS, 128), BF), pltpu.VMEM((QUERIES, 128), BF), pltpu.VMEM((TOKENS, ROWS), F32),
            pltpu.VMEM((128, QUERIES), F32), pltpu.VMEM((QUERIES, 128), F32),
        ),
        flops=9e9, traffic=4e6,
    )
    back = exchange(message)
    keys, values, keys_turned, values_turned, every_turned, kept = call(
        pairs_kernel,
        (
            shape((PATCHES, WIDTH), BF), shape((PATCHES, WIDTH), BF), shape((WIDTH, PATCHES), BF),
            shape((WIDTH, PATCHES), BF), shape((384, PATCHES), BF),
            shape((PEERS, 144, 128), BF),
        ),
        (received, cross_pair_weight),
        scratch=(pltpu.VMEM((PATCHES, 384), BF),),
        flops=3e9, traffic=8e6, late=(1,), away=(5, 0, 1, 2, 3, 4),
    )
    (
        block_out, early_keep, early_send, vectors, message, self_grad, feature_message, pair_value,
    ) = call(
        middle_kernel,
        (
            shape((BLOCK, WIDTH)), shape((3072, WIDTH), BF), shape((3072, WIDTH), BF), shape((8, WIDTH)),
            shape((PEERS, 16, 128), BF), shape((BLOCK, WIDTH)), shape((PEERS, 96, 128), BF), shape((384, WIDTH), BF),
        ),
        (
            place, back, tokens, keys, keys_turned, values, values_turned, self_out_weight, gain_two, offset_two,
            cross_query_weight, cross_out_weight, gain_three, offset_three, up_weight, down_weight, cotangent,
            every_turned, cross_pair_weight,
        ),
        scratch=(
            pltpu.VMEM((2, 3072, WIDTH), BF), pltpu.SemaphoreType.DMA((2, 2)), pltpu.VMEM((PATCHES, WIDTH), BF),
            pltpu.VMEM((PATCHES, WIDTH), BF), pltpu.VMEM((BLOCK, WIDTH), F32), pltpu.VMEM((BLOCK, WIDTH), F32),
        ),
        flops=1.6e10, traffic=2e7, smem=(0,), late=(7, 2, 10, 3, 6, 11, 14, 16, 15, 5, 4, 17, 18), limit=57,
        far_out=(1, 2),
    )

    def attend_back(message):
        given = exchange(message)
        total = sum_all((early_keep, swap_cores(early_send)))
        given, total = lax.optimization_barrier((given, total))
        pieces = scatter_chips(total)
        message = call(
            attend_back_kernel,
            shape((PEERS, 240, 128), BF),
            (kept, pairs_turned, attended_turned, log_total, given, feature_message),
            scratch=(
                pltpu.VMEM((TOKENS, 128), BF), pltpu.VMEM((TOKENS, 128), BF), pltpu.VMEM((QUERIES, 128), BF),
                pltpu.VMEM((QUERIES, 128), BF), pltpu.VMEM((8, QUERIES), F32),
                pltpu.VMEM((BACK_KEYS, QUERIES), BF), pltpu.VMEM((BACK_KEYS, QUERIES), BF),
                pltpu.VMEM((128, QUERIES), F32), pltpu.VMEM((QUERIES, 128), F32),
            ),
            flops=1.6e10, traffic=8e6, late=(0, 2, 1, 3),
        )
        return message, pieces

    message, pieces = step(attend_back, message)
    early = call(
        sum_far_kernel, shape((48, WIDTH), BF), (pieces,), traffic=3e6, far_in=(0,),
        scratch=(pltpu.VMEM(pieces.shape, BF), pltpu.SemaphoreType.DMA((4,))),
    )
    early = lax.all_gather(early, AXES, axis=0, tiled=True, axis_index_groups=SAME_CORE)

    def finish(message):
        returned = exchange(message)
        token_grad, feature_grad, keep, send = call(
            finish_kernel,
            (shape((BLOCK, WIDTH)), shape((32, 384)), shape((1024, WIDTH), BF), shape((1024, WIDTH), BF)),
            (
                place, returned, tokens, camera, modulation, self_grad, self_in_weight, vectors,
                pair_value,
            ),
            flops=3e9, traffic=8e6, smem=(0,), late=(2, 6, 4, 5),
        )
        pieces = scatter_chips(sum_all((keep, swap_cores(send))))
        total = call(sum_pieces_kernel, shape(pieces.shape, BF), (pieces,), traffic=2e6)
        late = lax.all_to_all(
            total, AXES, 0, 0, tiled=True, axis_index_groups=SAME_CORE
        ).reshape(1024, WIDTH)
        return token_grad, feature_grad, late

    token_grad, feature_grad, late = step(finish, message)
    early, late = lax.optimization_barrier((early, late))
    early_other, late_other = swap_cores(early), swap_cores(late)
    square = shape((WIDTH, WIDTH))
    vector = shape((1, WIDTH))
    grads = (shape((WIDTH, 2048)), shape((2048, WIDTH)), shape((WIDTH, 3 * WIDTH)), shape((384, 1024))) + (square,) * 3
    halves = tuple(pltpu.VMEM((g.shape[0] // 2, g.shape[1]), F32) for g in grads)
    halves += (pltpu.SemaphoreType.DMA((7,)),)
    *grads, mod_weight_grad, mod_bias_grad, gain_two_grad, offset_two_grad, gain_three_grad, offset_three_grad = call(
        own_out_kernel, grads + (shape((1024, 1024)), shape((1, 1024))) + (vector,) * 4, (place, early, late),
        scratch=halves, traffic=1.4e7, smem=(0,), late=(1,), away=(7,), far_out=tuple(range(7)), limit=57,
    )
    up_grad, down_grad, self_in_grad, pair_grad, self_out_grad, cross_query_grad, cross_out_grad = call(
        other_out_kernel,
        tuple(shape(g.shape) for g in grads),
        (place, early_other, late_other, *grads),
        scratch=halves, traffic=1.4e7, smem=(0,), far_in=tuple(range(3, 10)), far_out=tuple(range(7)),
        aliases={3 + k: k for k in range(7)},
    )
    return (
        block_out[None],
        token_grad[None],
        feature_grad[None],
        mod_weight_grad,
        mod_bias_grad[0],
        self_in_grad,
        self_out_grad,
        gain_two_grad[0],
        offset_two_grad[0],
        cross_query_grad,
        pair_grad,
        cross_out_grad,
        gain_three_grad[0],
        offset_three_grad[0],
        up_grad,
        down_grad,
    )


def solution(mesh):
    split = P("batch", "seq", None)
    in_specs = (
        (split, P("batch", None), split, P("batch", None), P("batch", "seq")) + (P(),) * 13 + (split,)
    )
    out_specs = (split,) * 3 + (P(),) * 13
    return jax.shard_map(body, mesh=mesh, in_specs=in_specs, out_specs=out_specs, check_vma=False)
```

```python
import functools

import jax
import jax.numpy as jnp
from jax import lax
from jax.experimental import pallas as pl
from jax.experimental.pallas import tpu as pltpu
from jax.sharding import PartitionSpec as P

HEADS = 8
HEAD_DIM = 64
BLOCK = 128
TRIB = 24
PATCHB = 8
WIDTH = 512
PATCHES = 1024
TOKENS = 4096
EPSILON = 1e-05
MASKED = -1e30
FLAG = 3e38
SCALE = HEAD_DIM ** (-0.5)
BF = jnp.bfloat16
F32 = jnp.float32
AXES = ("batch", "seq")
PEERS = 32
QUARTERS = 4
SHARE = BLOCK // QUARTERS
MIB = 1024 * 1024


def nn(a, b):
    return lax.dot_general(a, b, (((1,), (0,)), ((), ())), preferred_element_type=F32)


def nt(a, b):
    return lax.dot_general(a, b, (((1,), (1,)), ((), ())), preferred_element_type=F32)


def tn(a, b):
    return lax.dot_general(a, b, (((0,), (0,)), ((), ())), preferred_element_type=F32)


def half_turn(values):
    return pltpu.roll(values, 64, 1)


def low_lanes(rows):
    return lax.broadcasted_iota(jnp.int32, (rows, 128), 1) < 64


def norm_parts(values):
    centre = jnp.mean(values, axis=-1, keepdims=True)
    centred = values - centre
    spread = jnp.mean(centred * centred, axis=-1, keepdims=True)
    inverse = lax.rsqrt(spread + EPSILON)
    return centred * inverse, inverse


def norm_back(normed, inverse, grad):
    first = jnp.mean(grad, axis=-1, keepdims=True)
    second = jnp.mean(grad * normed, axis=-1, keepdims=True)
    return inverse * (grad - first - normed * second)


class Late:
    def __init__(self, copy, ref):
        self.copy, self.ref, self.here, self.shape = copy, ref, False, ref.shape

    def ready(self):
        if not self.here:
            self.copy.wait()
            self.here = True
        return self.ref

    def __getitem__(self, index):
        return self.ready()[index]


class Away:
    def __init__(self, ref, copy):
        self.ref, self.copy, self.sent, self.shape = ref, copy, False, ref.shape

    def __setitem__(self, index, value):
        self.ref[index] = value

    def send(self):
        if not self.sent:
            self.copy.start()
            self.sent = True


def call(
    kernel, out_shape, inputs, scratch=(), flops=0, traffic=0, limit=32, smem=(), late=(), away=(), far_out=(),
    far_in=(), aliases=None,
):
    vmem = pl.BlockSpec(memory_space=pltpu.VMEM)
    scalar = pl.BlockSpec(memory_space=pltpu.SMEM)
    far = pl.BlockSpec(memory_space=pltpu.HBM)
    single = not isinstance(out_shape, tuple)
    outs = (out_shape,) if single else out_shape
    count, extra = len(inputs), len(scratch)
    def whole(*refs):
        refs = list(refs)
        ins, results = refs[:count], refs[count : count + len(outs)]
        rest = refs[count + len(outs) :]
        mine, buffers = rest[:extra], rest[extra:]
        semaphores = buffers[-1] if late or away else None
        for k, which in enumerate(late):
            copy = pltpu.make_async_copy(ins[which], buffers[k], semaphores.at[k])
            copy.start()
            ins[which] = Late(copy, buffers[k])
        for k, which in enumerate(away):
            buffer = buffers[len(late) + k]
            results[which] = Away(
                buffer, pltpu.make_async_copy(buffer, results[which], semaphores.at[len(late) + k])
            )
        kernel(*ins, *results, *mine)
        for which in late:
            ins[which].ready()
        for which in away:
            results[which].send()
        for which in away:
            results[which].copy.wait()

    buffers = [pltpu.VMEM(inputs[k].shape, inputs[k].dtype) for k in late]
    buffers += [pltpu.VMEM(outs[k].shape, outs[k].dtype) for k in away]
    if buffers:
        buffers.append(pltpu.SemaphoreType.DMA((len(buffers),)))
    out_specs = tuple(far if k in away or k in far_out else vmem for k in range(len(outs)))
    return pl.pallas_call(
        whole,
        out_shape=out_shape,
        in_specs=[scalar if k in smem else far if k in late or k in far_in else vmem for k in range(count)],
        out_specs=out_specs[0] if single else out_specs,
        scratch_shapes=list(scratch) + buffers,
        input_output_aliases=aliases or {},
        compiler_params=pltpu.CompilerParams(vmem_limit_bytes=limit * MIB),
        cost_estimate=pl.CostEstimate(
            flops=int(flops), bytes_accessed=int(traffic), transcendentals=0
        ),
    )(*inputs)


def shape(dims, dtype=F32):
    return jax.ShapeDtypeStruct(dims, dtype)


def prepare_kernel(
    foreground, layout, tokens, features, camera, mod_weight, mod_bias, in_weight,
    far_message, modulation, message, semaphores,
):
    cam = camera[...].astype(F32)
    cam_act = (cam * jax.nn.sigmoid(cam)).astype(BF)
    mod = nn(jnp.broadcast_to(cam_act, (16, cam_act.shape[1])), mod_weight[...])[0:8]
    mod = mod + mod_bias[...].astype(F32).reshape(1, 2 * WIDTH)
    modulation[...] = mod
    block = layout[0, 0]
    lit = jnp.int32(0)
    for k in range(PATCHB):
        lit = lit + jnp.where(block - TRIB == k, foreground[0, k], 0)
    kept = jnp.logical_or(block < TRIB, lit > 0)
    normed, _ = norm_parts(tokens[...].astype(F32))
    hidden = (normed * (1.0 + mod[0:1, :WIDTH]) + mod[0:1, WIDTH:]).astype(BF)
    projected = nn(hidden, in_weight[...]).astype(BF).astype(F32)
    low = low_lanes(BLOCK)
    low_half = low_lanes(16)
    corner = jnp.logical_and(
        lax.broadcasted_iota(jnp.int32, (BLOCK, 128), 0) == 0, lax.broadcasted_iota(jnp.int32, (BLOCK, 128), 1) == 0
    )
    flagged = jnp.logical_and(corner, jnp.logical_not(kept))
    for pair in range(HEADS // 2):
        at = 128 * pair
        query = projected[:, at : at + 128] * SCALE
        key = projected[:, WIDTH + at : WIDTH + at + 128]
        value = projected[:, 2 * WIDTH + at : 2 * WIDTH + at + 128]
        query_turned = half_turn(query)
        for odd in range(2):
            head = 2 * pair + odd
            if odd:
                both = jnp.where(low, half_turn(key), value)
                first, second = query_turned, query
            else:
                both = jnp.where(low, key, half_turn(value))
                first, second = query, query_turned
            both = jnp.where(flagged, FLAG, both).astype(BF)
            for quarter in range(QUARTERS):
                to = QUARTERS * head + quarter
                message[to, 0:128, :] = both
                top = SHARE * quarter
                for k in range(3):
                    message[to, 144 + 32 * k : 176 + 32 * k, :] = features[:, 128 * k : 128 * (k + 1)]
                message[to, 128:144, :] = jnp.where(
                    low_half, first[top : top + 16], second[top + 16 : top + 32]
                ).astype(BF)
            some = slice(QUARTERS * head, QUARTERS * (head + 1))
            pltpu.make_async_copy(message.at[some], far_message.at[some], semaphores.at[head]).start()
    for head in range(HEADS):
        some = slice(QUARTERS * head, QUARTERS * (head + 1))
        pltpu.make_async_copy(message.at[some], far_message.at[some], semaphores.at[head]).wait()


def loop(count, work, unroll=1):
    def turn(k, carry):
        work(k)
        return carry

    lax.fori_loop(0, count, turn, 0, unroll=unroll)


def block_of(k, size):
    return pl.ds(pl.multiple_of(k * size, size), size)


def gather_keys(received, masked_keys, pairs, queries, turned):
    low = low_lanes(128)
    lane = lax.broadcasted_iota(jnp.int32, (128, 128), 1)
    lane_q = lax.broadcasted_iota(jnp.int32, (16, 128), 1)
    extra = jnp.where(lane_q == 64, 1.0, 0.0)

    def gather(k):
        at = block_of(k, 128)
        both = received[k, 0:128, :].astype(F32)
        mine = received[k, 128:144, :].astype(F32)
        masked = both[0:1, 0:1] > 1e38
        masked_keys[at, :] = jnp.where(
            low, jnp.where(masked, 0.0, both), jnp.where(jnp.logical_and(masked, lane == 64), MASKED, 0.0)
        ).astype(BF)
        if pairs is not None:
            pairs[at, :] = received[k, 0:128, :]
        if turned is not None:
            turned[:, at] = jnp.transpose(both).astype(BF)
        first = pl.ds(pl.multiple_of(SHARE * k, 16), 16)
        second = pl.ds(pl.multiple_of(SHARE * k + 16, 16), 16)
        queries[first, :] = jnp.where(lane_q < 64, mine, extra).astype(BF)
        queries[second, :] = jnp.where(lane_q < 64, half_turn(mine), extra).astype(BF)

    loop(PEERS, gather, 4)


KEYS = 512
ROWS = 1024
UNROLL_A = 2
UNROLL_B = 4
UNROLL_C = 1
BACK_KEYS = 1024
BACK_ROWS = 256
QUERIES = PEERS * SHARE


def attend_kernel(
    received, message, attended, log_total, pairs_turned, masked_keys, queries, scores, mixed, turned
):
    gather_keys(received, masked_keys, None, queries, pairs_turned)
    chunks = TOKENS // KEYS
    query = queries[...]

    def score(k, top):
        at = block_of(k, KEYS)
        part = nt(masked_keys[at, :], query)
        scores[at, :] = part
        return jnp.maximum(top, jnp.max(part, axis=0, keepdims=True))

    top = lax.fori_loop(0, chunks, score, jnp.full((1, ROWS), -jnp.inf, F32), unroll=UNROLL_A)
    mixed[...] = jnp.zeros_like(mixed)

    def mix(k, total):
        at = block_of(k, KEYS)
        chance = jnp.exp(scores[at, :] - top)
        mixed[...] += nn(pairs_turned[:, at], chance.astype(BF))
        return total + jnp.sum(chance, axis=0, keepdims=True)

    total = lax.fori_loop(0, chunks, mix, jnp.zeros((1, ROWS), F32), unroll=UNROLL_B)
    result = mixed[...] / total
    attended[...] = result[64:128, :]
    log_total[...] = jnp.broadcast_to(top + jnp.log(total), (8, ROWS))
    turned[...] = jnp.transpose(result)
    low = low_lanes(16)

    def pack(k):
        first = turned[pl.ds(pl.multiple_of(SHARE * k, 16), 16), :]
        second = turned[pl.ds(pl.multiple_of(SHARE * k + 16, 16), 16), :]
        message[k] = jnp.where(low, half_turn(first), second).astype(BF)

    loop(PEERS, pack, 4)


def pairs_kernel(
    received, pair_weight, keys, values, keys_turned, values_turned, every_turned, kept, every
):
    pair_weight = pair_weight.ready()

    def gather(k):
        for j in range(3):
            every[block_of(k, 32), 128 * j : 128 * (j + 1)] = received[k, 144 + 32 * j : 176 + 32 * j, :]
        kept.ref[k] = received[k, 0:144, :]

    def project(k):
        rows = block_of(k, 256)
        part = every[rows, :]
        every_turned.ref[:, rows] = jnp.transpose(part.astype(F32)).astype(BF)
        both = nn(part, pair_weight[...]).astype(BF)
        keys.ref[rows, :] = both[:, :WIDTH]
        values.ref[rows, :] = both[:, WIDTH:]
        turned = jnp.transpose(both.astype(F32)).astype(BF)
        keys_turned.ref[:, rows] = turned[:WIDTH, :]
        values_turned.ref[:, rows] = turned[WIDTH:, :]

    loop(PEERS, gather, 4)
    kept.send()
    loop(PATCHES // 256, project)


def unpack_heads(received):
    low = low_lanes(16)
    columns = []
    for pair in range(HEADS // 2):
        pieces = []
        for quarter in range(QUARTERS):
            even = received[QUARTERS * (2 * pair) + quarter].astype(F32)
            odd = received[QUARTERS * (2 * pair + 1) + quarter].astype(F32)
            pieces.append(jnp.where(low, even, half_turn(odd)))
            pieces.append(jnp.where(low, half_turn(even), odd))
        columns.append(jnp.concatenate(pieces, axis=0))
    return jnp.concatenate(columns, axis=1)


def pack_heads(values, message):
    low = low_lanes(16)
    for pair in range(HEADS // 2):
        for quarter in range(QUARTERS):
            first = values[SHARE * quarter : SHARE * quarter + 16, 128 * pair : 128 * (pair + 1)]
            second = values[SHARE * quarter + 16 : SHARE * (quarter + 1), 128 * pair : 128 * (pair + 1)]
            message[QUARTERS * (2 * pair) + quarter] = jnp.where(
                low, first, half_turn(second)
            ).astype(BF)
            message[QUARTERS * (2 * pair + 1) + quarter] = jnp.where(
                low, half_turn(first), second
            ).astype(BF)


GELU = 0.7978845608028654
CUBE = 0.044715


def put(place, keep, send, owner, rows, value):
    @pl.when(place[0] == owner)
    def _():
        keep[rows, :] = value

    @pl.when(place[0] != owner)
    def _():
        send[rows, :] = value


def middle_kernel(
    place, received, tokens, keys, keys_turned, values, values_turned, self_out, gain_two, offset_two,
    query_weight, cross_out, gain_three, offset_three, up_weight, down_weight, cotangent, every_turned, pair_weight,
    block_out, feed_keep, feed_send, vectors, message, self_grad, feature_part, pair_value,
    feed_pack, semaphores, key_all, value_all, total_out, total_back,
):
    def move(start, rows, to, slot):
        at = slice(to, to + rows)

        @pl.when(place[0] == 0)
        def _():
            pltpu.make_async_copy(feed_pack.at[0, start : start + rows], feed_keep.at[at], semaphores.at[slot, 0]).start()
            pltpu.make_async_copy(feed_pack.at[1, start : start + rows], feed_send.at[at], semaphores.at[slot, 1]).start()

        @pl.when(place[0] != 0)
        def _():
            pltpu.make_async_copy(feed_pack.at[1, start : start + rows], feed_keep.at[at], semaphores.at[slot, 0]).start()
            pltpu.make_async_copy(feed_pack.at[0, start : start + rows], feed_send.at[at], semaphores.at[slot, 1]).start()

    def put_halves(start, value):
        rows = value.shape[0] // 2
        feed_pack[0, start : start + rows, :] = value[:rows]
        feed_pack[1, start : start + rows, :] = value[rows:]

    attended_low = unpack_heads(received).astype(BF)
    first = tokens[...].astype(F32) + nn(attended_low, self_out[...])
    normed_two, inverse_two = norm_parts(first)
    gain = gain_two[...].astype(F32)
    hidden = (normed_two * gain + offset_two[...].astype(F32)).astype(BF)
    queries = nn(hidden, query_weight[...]).astype(BF).astype(F32) * SCALE
    low = low_lanes(BLOCK)
    upper = lax.broadcasted_iota(jnp.int32, (128, BLOCK), 0) < 64
    masked = []
    chances = []
    pieces = []
    for pair in range(HEADS // 2):
        at = slice(128 * pair, 128 * (pair + 1))
        key = keys[:, at]
        value = values_turned[at, :]
        parts = []
        for odd in range(2):
            mine = jnp.where(low if odd == 0 else jnp.logical_not(low), queries[:, at], 0.0).astype(BF)
            scores = nt(key, mine)
            chance = jnp.exp(scores - jnp.max(scores, axis=0, keepdims=True))
            chance = chance * (1.0 / jnp.sum(chance, axis=0, keepdims=True))
            masked.append(mine)
            chances.append(chance)
            parts.append(nn(value, chance.astype(BF)))
        pieces.append(jnp.transpose(jnp.where(upper, parts[0], parts[1])))
    mixed = jnp.concatenate(pieces, axis=1).astype(BF)
    second = first + nn(mixed, cross_out[...])
    normed, inverse = norm_parts(second)
    gain_out = gain_three[...].astype(F32)
    hidden3 = (normed * gain_out + offset_three[...].astype(F32)).astype(BF)
    grad_low = cotangent[...]
    total_out[...] = second
    total_back[...] = jnp.zeros((BLOCK, WIDTH), F32)
    up_all, down_all = up_weight.ready(), down_weight.ready()

    def feed_block(k, carry):
        at = pl.ds(pl.multiple_of(512 * k, 512), 512)
        up, down = up_all[:, at], down_all[at, :]
        pre = nn(hidden3, up)
        square = pre * pre
        turn = jnp.tanh(GELU * (pre + CUBE * (square * pre)))
        half = 0.5 * (1.0 + turn)
        active = (pre * half).astype(BF)
        slope = half + (0.5 * pre) * (1.0 - turn * turn) * (GELU * (1.0 + (3.0 * CUBE) * square))
        total_out[...] += nn(active, down)
        pre_grad = (nt(grad_low, down) * slope).astype(BF)
        total_back[...] += nt(pre_grad, up)
        grad = tn(hidden3, pre_grad).astype(BF)
        feed_pack[0, pl.ds(pl.multiple_of(256 * k, 256), 256), :] = grad[:256]
        feed_pack[1, pl.ds(pl.multiple_of(256 * k, 256), 256), :] = grad[256:]
        feed_pack[k // 2, pl.ds(pl.multiple_of(1024 + 512 * (k % 2), 512), 512), :] = tn(active, grad_low).astype(BF)
        return carry

    lax.fori_loop(0, 4, feed_block, 0, unroll=1)
    result = total_out[...]
    back = total_back[...]
    move(0, 2048, 0, 0)
    block_out[...] = result
    vectors[2:3, :] = jnp.sum(back * normed, axis=0, keepdims=True)
    vectors[3:4, :] = jnp.sum(back, axis=0, keepdims=True)
    grad = grad_low.astype(F32) + norm_back(normed, inverse, back * gain_out)
    branch = grad.astype(BF)
    put_halves(2048, tn(mixed, branch).astype(BF))
    mixed_grad = nt(branch, cross_out[...]).astype(BF).astype(F32)
    pieces = []
    pair_low = []
    for pair in range(HEADS // 2):
        at = slice(128 * pair, 128 * (pair + 1))
        value = values[:, at]
        key_turned = keys_turned[at, :]
        parts = []
        key_sum = None
        value_sum = None
        for odd in range(2):
            head = 2 * pair + odd
            given = jnp.where(low if odd == 0 else jnp.logical_not(low), mixed_grad[:, at], 0.0).astype(BF)
            chance = chances[head]
            chance_grad = nt(value, given)
            inner = jnp.sum(chance * chance_grad, axis=0, keepdims=True)
            score_grad = (chance * (chance_grad - inner)).astype(BF)
            parts.append(nn(key_turned, score_grad))
            key_part = nn(score_grad, masked[head])
            value_part = nn(chance.astype(BF), given)
            key_sum = key_part if key_sum is None else key_sum + key_part
            value_sum = value_part if value_sum is None else value_sum + value_part
        pair_low.append((key_sum.astype(BF), value_sum.astype(BF)))
        pieces.append(jnp.transpose(jnp.where(upper, parts[0], parts[1])) * SCALE)
    low_grad = jnp.concatenate(pieces, axis=1).astype(BF)
    back = nt(low_grad, query_weight[...])
    vectors[0:1, :] = jnp.sum(back * normed_two, axis=0, keepdims=True)
    vectors[1:2, :] = jnp.sum(back, axis=0, keepdims=True)
    vectors[4:8, :] = jnp.zeros((4, WIDTH), F32)
    grad = grad + norm_back(normed_two, inverse_two, back * gain)
    self_grad[...] = grad
    branch = grad.astype(BF)
    pack_heads(nt(branch, self_out[...]), message)
    put_halves(2304, tn(hidden, low_grad).astype(BF))
    put_halves(2560, tn(attended_low, branch).astype(BF))
    key_grad = jnp.concatenate([p[0] for p in pair_low], axis=1)
    value_grad = jnp.concatenate([p[1] for p in pair_low], axis=1)
    put_halves(2816, nn(every_turned[...], key_grad).astype(BF))
    pair_value[...] = nn(every_turned[...], value_grad).astype(BF)
    feed_pack[0, 3008:3072, :] = jnp.zeros((64, WIDTH), BF)
    feed_pack[1, 3008:3072, :] = jnp.zeros((64, WIDTH), BF)
    move(2048, 1024, 2048, 1)
    def feature_block(k, carry):
        rows = pl.ds(pl.multiple_of(256 * k, 256), 256)
        part = (nt(key_all[rows, :], pair_keys) + nt(value_all[rows, :], pair_values)).astype(BF)
        for i in range(8):
            for j in range(3):
                feature_part[8 * k + i, 32 * j : 32 * (j + 1), :] = part[
                    32 * i : 32 * (i + 1), 128 * j : 128 * (j + 1)
                ]
        return carry

    pair_keys, pair_values = pair_weight[:, :WIDTH], pair_weight[:, WIDTH:]
    key_all[...] = key_grad
    value_all[...] = value_grad
    lax.fori_loop(0, PATCHES // 256, feature_block, 0)
    for slot, rows in enumerate((2048, 1024)):
        for k in range(2):
            pltpu.make_async_copy(
                feed_pack.at[0, 0:rows], feed_keep.at[0:rows], semaphores.at[slot, k]
            ).wait()


def put_halves(place, keep, send, start, value):
    rows = value.shape[0] // 2
    put(place, keep, send, 0, slice(start, start + rows), value[:rows])
    put(place, keep, send, 1, slice(start, start + rows), value[rows:])


def attend_back_kernel(
    received, pairs_turned, attended, log_total, given, feature_part, message,
    masked_keys, pairs, queries, outer, outer_row, chances, score_grads, query_sum, turned,
):
    received = received.ready()
    gather_keys(received, masked_keys, pairs, queries, None)
    low = low_lanes(16)

    def unpack(k):
        piece = given[k].astype(F32)
        outer[pl.ds(pl.multiple_of(SHARE * k, 16), 16), :] = jnp.where(low, 0.0, half_turn(piece)).astype(BF)
        outer[pl.ds(pl.multiple_of(SHARE * k + 16, 16), 16), :] = jnp.where(low, 0.0, piece).astype(BF)
        message[k, 144:240, :] = feature_part[k]

    loop(PEERS, unpack, 4)
    attended = attended.ready()

    def inner(k):
        rows = block_of(k, 256)
        turned = jnp.transpose(outer[rows, :].astype(F32))[64:128, :]
        outer_row[:, rows] = jnp.broadcast_to(
            jnp.sum(turned * attended[:, rows], axis=0, keepdims=True), (8, 256)
        )

    loop(QUERIES // 256, inner)
    query_sum[...] = jnp.zeros_like(query_sum)
    pairs_turned, log_total = pairs_turned.ready(), log_total.ready()

    def chunk(turn, carry):
        at = pl.ds(pl.multiple_of(turn * BACK_KEYS, BACK_KEYS), BACK_KEYS)
        key = masked_keys[at, :]
        both = pairs[at, :]
        for k in range(QUERIES // BACK_ROWS):
            rows = slice(BACK_ROWS * k, BACK_ROWS * (k + 1))
            chance = jnp.exp(nt(key, queries[rows, :]) - log_total[0:1, rows])
            chance_grad = nt(both, outer[rows, :])
            chances[:, rows] = chance.astype(BF)
            score_grads[:, rows] = (chance * (chance_grad - outer_row[0:1, rows])).astype(BF)
        sums = nn(score_grads[...], queries[...])
        other = nn(chances[...], outer[...])
        sums = jnp.where(low_lanes(BACK_KEYS), sums, other).astype(BF)
        for k in range(BACK_KEYS // 128):
            message[turn * (BACK_KEYS // 128) + k, 0:128, :] = sums[128 * k : 128 * (k + 1), :]
        query_sum[...] += nn(pairs_turned[:, at], score_grads[...])
        return carry

    lax.fori_loop(0, TOKENS // BACK_KEYS, chunk, 0, unroll=UNROLL_C)
    turned[...] = jnp.transpose(query_sum[...]) * SCALE

    def pack(k):
        first = turned[pl.ds(pl.multiple_of(SHARE * k, 16), 16), :]
        second = turned[pl.ds(pl.multiple_of(SHARE * k + 16, 16), 16), :]
        message[k, 128:144, :] = jnp.where(low, first, half_turn(second)).astype(BF)

    loop(PEERS, pack, 4)


def finish_kernel(
    place, received, tokens, camera, modulation, self_grad, in_weight, vectors,
    pair_value, token_grad, feature_grad, keep, send,
):
    total = received[0, 144:240, :].astype(F32)
    for k in range(1, PEERS):
        total = total + received[k, 144:240, :].astype(F32)
    for j in range(3):
        feature_grad[:, 128 * j : 128 * (j + 1)] = total[32 * j : 32 * (j + 1), :]
    low = low_lanes(BLOCK)
    queries = []
    keys = []
    values = []
    for pair in range(HEADS // 2):
        sums = []
        for odd in range(2):
            head = 2 * pair + odd
            total = received[QUARTERS * head, 0:128, :].astype(F32)
            for quarter in range(1, QUARTERS):
                total = total + received[QUARTERS * head + quarter, 0:128, :].astype(F32)
            sums.append(total)
        keys.append(jnp.where(low, sums[0], half_turn(sums[1])))
        values.append(jnp.where(low, half_turn(sums[0]), sums[1]))
        low_half = low_lanes(16)
        pieces = []
        for quarter in range(QUARTERS):
            even = received[QUARTERS * (2 * pair) + quarter, 128:144, :].astype(F32)
            odd = received[QUARTERS * (2 * pair + 1) + quarter, 128:144, :].astype(F32)
            pieces.append(jnp.where(low_half, even, half_turn(odd)))
            pieces.append(jnp.where(low_half, half_turn(even), odd))
        queries.append(jnp.concatenate(pieces, axis=0))
    parts = [jnp.concatenate(p, axis=1).astype(BF) for p in (queries, keys, values)]
    normed, inverse = norm_parts(tokens[...].astype(F32))
    scale = 1.0 + modulation[0:1, :WIDTH]
    hidden = (normed * scale + modulation[0:1, WIDTH:]).astype(BF)
    back = jnp.zeros((BLOCK, WIDTH), F32)
    for k in range(3):
        at = slice(WIDTH * k, WIDTH * (k + 1))
        back = back + nt(parts[k], in_weight[:, at])
        put_halves(place, keep, send, 256 * k, tn(hidden, parts[k]).astype(BF))
    token_grad[...] = self_grad[...] + norm_back(normed, inverse, back * scale)
    scale_grad = jnp.sum(back * normed, axis=0, keepdims=True)
    shift_grad = jnp.sum(back, axis=0, keepdims=True)
    cam = camera[...].astype(F32)
    cam_act = cam * jax.nn.sigmoid(cam)
    row = lax.broadcasted_iota(jnp.int32, (32, WIDTH), 0)
    item = place[1]
    first = place[2] == 0
    small = jnp.where(row == item, scale_grad, 0.0)
    small = small + jnp.where(row == 4 + item, shift_grad, 0.0)
    small = small + jnp.where(jnp.logical_and(first, row == 8 + item), cam_act[:, :WIDTH], 0.0)
    small = small + jnp.where(jnp.logical_and(first, row == 12 + item), cam_act[:, WIDTH:], 0.0)
    small = small + jnp.where(row == 16, vectors[0:1, :], 0.0)
    small = small + jnp.where(row == 17, vectors[1:2, :], 0.0)
    small = small + jnp.where(row == 18, vectors[2:3, :], 0.0)
    small = small + jnp.where(row == 19, vectors[3:4, :], 0.0)
    put_halves(place, keep, send, 768, pair_value[...])
    keep[960:992, :] = small.astype(BF)
    send[960:992, :] = small.astype(BF)
    keep[992:1024, :] = jnp.zeros((32, WIDTH), BF)
    send[992:1024, :] = jnp.zeros((32, WIDTH), BF)


def sum_split_kernel(which, place, *refs):
    parts, pieces = refs[:-4], refs[-4:]
    rows = pieces[0].shape[0]
    for k in range(4):
        at = pl.ds(pl.multiple_of(lax.rem(place[which] + k, 4) * rows, rows), rows)
        total = parts[0][at, :].astype(F32)
        for part in parts[1:]:
            total = total + part[at, :].astype(F32)
        pieces[k][...] = total.astype(BF)


def halves_kernel(place, value, mine, other):
    rows = mine.shape[0]
    mine[...] = value[pl.ds(pl.multiple_of(place[0] * rows, rows), rows), :]
    other[...] = value[pl.ds(pl.multiple_of((1 - place[0]) * rows, rows), rows), :]


def sum_kernel(*refs):
    total = refs[0][...].astype(F32)
    for part in refs[1:-1]:
        total = total + part[...].astype(F32)
    refs[-1][...] = total.astype(BF)


def sum_pairs_kernel(first, second, third, fourth, out):
    rows = first.shape[0]
    out[0:rows, :] = (first[...].astype(F32) + second[...].astype(F32)).astype(BF)
    out[rows : 2 * rows, :] = (third[...].astype(F32) + fourth[...].astype(F32)).astype(BF)


def arrange_kernel(which, place, *refs):
    pieces, out = refs[:-1], refs[-1]
    rows = pieces[0].shape[0]
    for k in range(4):
        at = pl.ds(pl.multiple_of(lax.rem(place[which] + 4 - k, 4) * rows, rows), rows)
        out[at, :] = pieces[k][...]


def sum_pieces_kernel(pieces, *outs):
    total = pieces[0].astype(F32)
    for k in range(1, pieces.shape[0]):
        total = total + pieces[k].astype(F32)
    total = total.astype(BF)
    for out in outs:
        if len(out.shape) == 2:
            out[...] = total
        else:
            for k in range(out.shape[0]):
                out[k] = total


def write_halves(core, early, late, outs, buffers, semaphores):
    up_grad, down_grad, self_in, pair, self_out, cross_query, cross_out = outs
    up_part, down_part, in_part, pair_part, out_part, query_part, cross_part = buffers
    copies = []

    def send(part, target, slot):
        rows = part.shape[0]
        at = pl.ds(pl.multiple_of(core * rows, rows), rows)
        copies.append(pltpu.make_async_copy(part, target.at[at, :], semaphores.at[slot]))
        copies[-1].start()

    for k in range(4):
        up_part[:, 512 * k : 512 * (k + 1)] = early[256 * k : 256 * (k + 1), :].astype(F32)
    send(up_part, up_grad, 0)
    down_part[...] = early[1024:2048, :].astype(F32)
    send(down_part, down_grad, 1)
    for k in range(3):
        in_part[:, 512 * k : 512 * (k + 1)] = late[256 * k : 256 * (k + 1), :].astype(F32)
    send(in_part, self_in, 2)
    pair_part[:, :WIDTH] = early[2816:3008, :].astype(F32)
    pair_part[:, WIDTH:] = late[768:960, :].astype(F32)
    send(pair_part, pair, 3)
    out_part[...] = early[2560:2816, :].astype(F32)
    send(out_part, self_out, 4)
    query_part[...] = early[2304:2560, :].astype(F32)
    send(query_part, cross_query, 5)
    cross_part[...] = early[2048:2304, :].astype(F32)
    send(cross_part, cross_out, 6)
    return copies


def own_out_kernel(place, early, late, *refs):
    mod_weight, mod_bias, gain_two, offset_two, gain_three, offset_three = refs[7:13]
    small = late[960:992, :].astype(F32)
    grads = small[0:8, :]
    acts = small[8:16, :].astype(BF)
    head = lax.broadcasted_iota(jnp.int32, (8, WIDTH), 0) < 4
    turned = pltpu.roll(grads, 4, 0)
    mod_weight[:WIDTH, :WIDTH] = tn(acts, jnp.where(head, grads, 0.0).astype(BF))
    mod_weight[:WIDTH, WIDTH:] = tn(acts, jnp.where(head, turned, 0.0).astype(BF))
    mod_weight[WIDTH:, :WIDTH] = tn(acts, jnp.where(head, 0.0, turned).astype(BF))
    mod_weight[WIDTH:, WIDTH:] = tn(acts, jnp.where(head, 0.0, grads).astype(BF))
    mod_weight.send()
    gain_two[...] = small[16:17, :]
    offset_two[...] = small[17:18, :]
    gain_three[...] = small[18:19, :]
    offset_three[...] = small[19:20, :]
    mod_bias[:, :WIDTH] = jnp.sum(jnp.where(head, grads, 0.0), axis=0, keepdims=True)
    mod_bias[:, WIDTH:] = jnp.sum(jnp.where(head, 0.0, grads), axis=0, keepdims=True)
    for copy in write_halves(place[0], early, late, refs[:7], refs[13:20], refs[20]):
        copy.wait()


def other_out_kernel(place, early, late, *refs):
    for copy in write_halves(1 - place[0], early, late, refs[7:14], refs[14:21], refs[21]):
        copy.wait()


def index_of(x, y, z, core):
    return ((z % 2) * 2 + core) * 32 + (y * 4 + x) * 2 + z // 2


CHIPS = [(x, y, z) for x in range(4) for y in range(4) for z in range(4)]
SAME_CORE = [[index_of(*chip, core) for chip in CHIPS] for core in range(2)]
SAME_PLANE = [
    [index_of(x, y, z, core) for x in range(4) for y in range(4)] for z in range(4) for core in range(2)
]
OTHER_CORE = [
    (index_of(*chip, core), index_of(*chip, 1 - core)) for chip in CHIPS for core in range(2)
]


def shift_of(axis, step):
    moves = []
    for chip in CHIPS:
        there = list(chip)
        there[axis] = (there[axis] + step) % 4
        moves += [(index_of(*chip, core), index_of(*there, core)) for core in range(2)]
    return moves


SHIFTS = {(axis, step): shift_of(axis, step) for axis in range(3) for step in (1, 2, 3)}


def exchange(message):
    return lax.all_to_all(message, "seq", 0, 0, tiled=True)


def swap_cores(value):
    return lax.ppermute(value, AXES, OTHER_CORE)


def scatter_ring(pieces, axis):
    return (pieces[0],) + tuple(lax.ppermute(pieces[k], AXES, SHIFTS[axis, k]) for k in (1, 3, 2))


def gather_ring(piece, axis):
    came = {k: lax.ppermute(piece, AXES, SHIFTS[axis, k]) for k in (1, 3, 2)}
    return piece, came[1], came[2], came[3]


def sum_split(place, parts, axis):
    rows = parts[0].shape[0] // 4
    return call(
        functools.partial(sum_split_kernel, 3 + axis), (shape((rows, WIDTH), BF),) * 4, (place, *parts),
        traffic=4e5, smem=(0,),
    )


def sum_all(parts):
    return call(sum_kernel, shape(parts[0].shape, BF), parts, traffic=4e5)


def arrange(place, parts, axis):
    return call(
        functools.partial(arrange_kernel, 3 + axis), shape((4 * parts[0].shape[0], WIDTH), BF), (place, *parts),
        traffic=4e5, smem=(0,),
    )


def scatter_chips(value):
    rows = value.shape[0] // 64
    return lax.all_to_all(
        value.reshape(64, rows, WIDTH), AXES, 0, 0, tiled=True, axis_index_groups=SAME_CORE
    )


def in_one_step(always, work, *values):
    def nothing(*values):
        return jax.tree.map(lambda v: jnp.zeros(v.shape, v.dtype), jax.eval_shape(work, *values))

    return lax.cond(always, work, nothing, *values)


def body(
    tokens, camera, features, foreground, layout, modulation_weight, modulation_bias,
    self_in_weight, self_out_weight, cross_norm_gain, cross_norm_bias, cross_query_weight,
    cross_pair_weight, cross_out_weight, feed_norm_gain, feed_norm_bias, up_weight, down_weight,
    cotangent,
):
    tokens = tokens[0]
    features = features[0]
    cotangent = cotangent[0]
    row = lambda v: v.reshape(1, -1)
    step = functools.partial(in_one_step, layout[0, 0] >= 0)
    gain_two, offset_two = row(cross_norm_gain), row(cross_norm_bias)
    gain_three, offset_three = row(feed_norm_gain), row(feed_norm_bias)
    item, spot = lax.axis_index("batch"), lax.axis_index("seq")
    place = jnp.stack(
        [item & 1, item, spot, (spot >> 1) & 3, spot >> 3, (spot & 1) * 2 + (item >> 1)]
    ).astype(jnp.int32)

    message, modulation = call(
        prepare_kernel,
        (shape((PEERS, 240, 128), BF), shape((8, 1024))),
        (foreground, layout, tokens, features, camera, modulation_weight, modulation_bias, self_in_weight),
        flops=1e9, traffic=8e6, smem=(0, 1), late=(4, 5, 2, 7, 3, 6), far_out=(0,), limit=57,
        scratch=(pltpu.VMEM((PEERS, 240, 128), BF), pltpu.SemaphoreType.DMA((HEADS,))),
    )
    received = exchange(message)
    message, attended_turned, log_total, pairs_turned = call(
        attend_kernel,
        (shape((PEERS, 16, 128), BF), shape((64, QUERIES)), shape((8, QUERIES)), shape((128, TOKENS), BF)),
        (received,),
        scratch=(
            pltpu.VMEM((TOKENS, 128), BF), pltpu.VMEM((QUERIES, 128), BF), pltpu.VMEM((TOKENS, ROWS), F32),
            pltpu.VMEM((128, QUERIES), F32), pltpu.VMEM((QUERIES, 128), F32),
        ),
        flops=9e9, traffic=4e6,
    )
    back = exchange(message)
    keys, values, keys_turned, values_turned, every_turned, kept = call(
        pairs_kernel,
        (
            shape((PATCHES, WIDTH), BF), shape((PATCHES, WIDTH), BF), shape((WIDTH, PATCHES), BF),
            shape((WIDTH, PATCHES), BF), shape((384, PATCHES), BF),
            shape((PEERS, 144, 128), BF),
        ),
        (received, cross_pair_weight),
        scratch=(pltpu.VMEM((PATCHES, 384), BF),),
        flops=3e9, traffic=8e6, late=(1,), away=(5, 0, 1, 2, 3, 4),
    )
    (
        block_out, early_keep, early_send, vectors, message, self_grad, feature_message, pair_value,
    ) = call(
        middle_kernel,
        (
            shape((BLOCK, WIDTH)), shape((3072, WIDTH), BF), shape((3072, WIDTH), BF), shape((8, WIDTH)),
            shape((PEERS, 16, 128), BF), shape((BLOCK, WIDTH)), shape((PEERS, 96, 128), BF), shape((384, WIDTH), BF),
        ),
        (
            place, back, tokens, keys, keys_turned, values, values_turned, self_out_weight, gain_two, offset_two,
            cross_query_weight, cross_out_weight, gain_three, offset_three, up_weight, down_weight, cotangent,
            every_turned, cross_pair_weight,
        ),
        scratch=(
            pltpu.VMEM((2, 3072, WIDTH), BF), pltpu.SemaphoreType.DMA((2, 2)), pltpu.VMEM((PATCHES, WIDTH), BF),
            pltpu.VMEM((PATCHES, WIDTH), BF), pltpu.VMEM((BLOCK, WIDTH), F32), pltpu.VMEM((BLOCK, WIDTH), F32),
        ),
        flops=1.6e10, traffic=2e7, smem=(0,), late=(1, 7, 2, 8, 9, 10, 3, 6, 11, 12, 13, 14, 16, 15, 5, 4, 17, 18),
        limit=57,
        far_out=(1, 2),
    )

    def attend_back(message):
        given = exchange(message)
        total = sum_all((early_keep, swap_cores(early_send)))
        given, total = lax.optimization_barrier((given, total))
        pieces = scatter_chips(total)
        message = call(
            attend_back_kernel,
            shape((PEERS, 240, 128), BF),
            (kept, pairs_turned, attended_turned, log_total, given, feature_message),
            scratch=(
                pltpu.VMEM((TOKENS, 128), BF), pltpu.VMEM((TOKENS, 128), BF), pltpu.VMEM((QUERIES, 128), BF),
                pltpu.VMEM((QUERIES, 128), BF), pltpu.VMEM((8, QUERIES), F32),
                pltpu.VMEM((BACK_KEYS, QUERIES), BF), pltpu.VMEM((BACK_KEYS, QUERIES), BF),
                pltpu.VMEM((128, QUERIES), F32), pltpu.VMEM((QUERIES, 128), F32),
            ),
            flops=1.6e10, traffic=8e6, late=(0, 2, 1, 3),
        )
        message, pieces = lax.optimization_barrier((message, pieces))
        return message, call(sum_pieces_kernel, shape((48, WIDTH), BF), (pieces,), traffic=3e6)

    message, early = step(attend_back, message)
    early = lax.all_gather(early, AXES, axis=0, tiled=True, axis_index_groups=SAME_CORE)

    def finish(message):
        returned = exchange(message)
        token_grad, feature_grad, keep, send = call(
            finish_kernel,
            (shape((BLOCK, WIDTH)), shape((32, 384)), shape((1024, WIDTH), BF), shape((1024, WIDTH), BF)),
            (
                place, returned, tokens, camera, modulation, self_grad, self_in_weight, vectors,
                pair_value,
            ),
            flops=3e9, traffic=8e6, smem=(0,), late=(2, 6, 4, 5),
        )
        pieces = scatter_chips(sum_all((keep, swap_cores(send))))
        total = call(sum_pieces_kernel, shape(pieces.shape, BF), (pieces,), traffic=2e6)
        late = lax.all_to_all(
            total, AXES, 0, 0, tiled=True, axis_index_groups=SAME_CORE
        ).reshape(1024, WIDTH)
        return token_grad, feature_grad, late

    token_grad, feature_grad, late = step(finish, message)
    early, late = lax.optimization_barrier((early, late))
    early_other, late_other = swap_cores(early), swap_cores(late)
    square = shape((WIDTH, WIDTH))
    vector = shape((1, WIDTH))
    grads = (shape((WIDTH, 2048)), shape((2048, WIDTH)), shape((WIDTH, 3 * WIDTH)), shape((384, 1024))) + (square,) * 3
    halves = tuple(pltpu.VMEM((g.shape[0] // 2, g.shape[1]), F32) for g in grads)
    halves += (pltpu.SemaphoreType.DMA((7,)),)
    *grads, mod_weight_grad, mod_bias_grad, gain_two_grad, offset_two_grad, gain_three_grad, offset_three_grad = call(
        own_out_kernel, grads + (shape((1024, 1024)), shape((1, 1024))) + (vector,) * 4, (place, early, late),
        scratch=halves, traffic=1.4e7, smem=(0,), late=(1,), away=(7,), far_out=tuple(range(7)), limit=57,
    )
    up_grad, down_grad, self_in_grad, pair_grad, self_out_grad, cross_query_grad, cross_out_grad = call(
        other_out_kernel,
        tuple(shape(g.shape) for g in grads),
        (place, early_other, late_other, *grads),
        scratch=halves, traffic=1.4e7, smem=(0,), far_in=tuple(range(3, 10)), far_out=tuple(range(7)),
        aliases={3 + k: k for k in range(7)},
    )
    return (
        block_out[None],
        token_grad[None],
        feature_grad[None],
        mod_weight_grad,
        mod_bias_grad[0],
        self_in_grad,
        self_out_grad,
        gain_two_grad[0],
        offset_two_grad[0],
        cross_query_grad,
        pair_grad,
        cross_out_grad,
        gain_three_grad[0],
        offset_three_grad[0],
        up_grad,
        down_grad,
    )


def solution(mesh):
    split = P("batch", "seq", None)
    in_specs = (
        (split, P("batch", None), split, P("batch", None), P("batch", "seq")) + (P(),) * 13 + (split,)
    )
    out_specs = (split,) * 3 + (P(),) * 13
    return jax.shard_map(body, mesh=mesh, in_specs=in_specs, out_specs=out_specs, check_vma=False)
```

```python
import functools

import jax
import jax.numpy as jnp
from jax import lax
from jax.experimental import pallas as pl
from jax.experimental.pallas import tpu as pltpu
from jax.sharding import PartitionSpec as P

HEADS = 8
HEAD_DIM = 64
BLOCK = 128
TRIB = 24
PATCHB = 8
WIDTH = 512
PATCHES = 1024
TOKENS = 4096
EPSILON = 1e-05
MASKED = -1e30
FLAG = 3e38
SCALE = HEAD_DIM ** (-0.5)
BF = jnp.bfloat16
F32 = jnp.float32
AXES = ("batch", "seq")
PEERS = 32
QUARTERS = 4
SHARE = BLOCK // QUARTERS
MIB = 1024 * 1024


def nn(a, b):
    return lax.dot_general(a, b, (((1,), (0,)), ((), ())), preferred_element_type=F32)


def nt(a, b):
    return lax.dot_general(a, b, (((1,), (1,)), ((), ())), preferred_element_type=F32)


def tn(a, b):
    return lax.dot_general(a, b, (((0,), (0,)), ((), ())), preferred_element_type=F32)


def half_turn(values):
    return pltpu.roll(values, 64, 1)


def low_lanes(rows):
    return lax.broadcasted_iota(jnp.int32, (rows, 128), 1) < 64


def norm_parts(values):
    centre = jnp.mean(values, axis=-1, keepdims=True)
    centred = values - centre
    spread = jnp.mean(centred * centred, axis=-1, keepdims=True)
    inverse = lax.rsqrt(spread + EPSILON)
    return centred * inverse, inverse


def norm_back(normed, inverse, grad):
    first = jnp.mean(grad, axis=-1, keepdims=True)
    second = jnp.mean(grad * normed, axis=-1, keepdims=True)
    return inverse * (grad - first - normed * second)


class Late:
    def __init__(self, copy, ref):
        self.copy, self.ref, self.here, self.shape = copy, ref, False, ref.shape

    def ready(self):
        if not self.here:
            self.copy.wait()
            self.here = True
        return self.ref

    def __getitem__(self, index):
        return self.ready()[index]


class Away:
    def __init__(self, ref, copy):
        self.ref, self.copy, self.sent, self.shape = ref, copy, False, ref.shape

    def __setitem__(self, index, value):
        self.ref[index] = value

    def send(self):
        if not self.sent:
            self.copy.start()
            self.sent = True


def call(
    kernel, out_shape, inputs, scratch=(), flops=0, traffic=0, limit=32, smem=(), late=(), away=(), far_out=(),
    far_in=(), aliases=None,
):
    vmem = pl.BlockSpec(memory_space=pltpu.VMEM)
    scalar = pl.BlockSpec(memory_space=pltpu.SMEM)
    far = pl.BlockSpec(memory_space=pltpu.HBM)
    single = not isinstance(out_shape, tuple)
    outs = (out_shape,) if single else out_shape
    count, extra = len(inputs), len(scratch)
    def whole(*refs):
        refs = list(refs)
        ins, results = refs[:count], refs[count : count + len(outs)]
        rest = refs[count + len(outs) :]
        mine, buffers = rest[:extra], rest[extra:]
        semaphores = buffers[-1] if late or away else None
        for k, which in enumerate(late):
            copy = pltpu.make_async_copy(ins[which], buffers[k], semaphores.at[k])
            copy.start()
            ins[which] = Late(copy, buffers[k])
        for k, which in enumerate(away):
            buffer = buffers[len(late) + k]
            results[which] = Away(
                buffer, pltpu.make_async_copy(buffer, results[which], semaphores.at[len(late) + k])
            )
        kernel(*ins, *results, *mine)
        for which in late:
            ins[which].ready()
        for which in away:
            results[which].send()
        for which in away:
            results[which].copy.wait()

    buffers = [pltpu.VMEM(inputs[k].shape, inputs[k].dtype) for k in late]
    buffers += [pltpu.VMEM(outs[k].shape, outs[k].dtype) for k in away]
    if buffers:
        buffers.append(pltpu.SemaphoreType.DMA((len(buffers),)))
    out_specs = tuple(far if k in away or k in far_out else vmem for k in range(len(outs)))
    return pl.pallas_call(
        whole,
        out_shape=out_shape,
        in_specs=[scalar if k in smem else far if k in late or k in far_in else vmem for k in range(count)],
        out_specs=out_specs[0] if single else out_specs,
        scratch_shapes=list(scratch) + buffers,
        input_output_aliases=aliases or {},
        compiler_params=pltpu.CompilerParams(vmem_limit_bytes=limit * MIB),
        cost_estimate=pl.CostEstimate(
            flops=int(flops), bytes_accessed=int(traffic), transcendentals=0
        ),
    )(*inputs)


def shape(dims, dtype=F32):
    return jax.ShapeDtypeStruct(dims, dtype)


def prepare_kernel(
    foreground, layout, tokens, features, camera, mod_weight, mod_bias, in_weight,
    far_message, modulation, message, semaphores,
):
    cam = camera[...].astype(F32)
    cam_act = (cam * jax.nn.sigmoid(cam)).astype(BF)
    mod = nn(jnp.broadcast_to(cam_act, (16, cam_act.shape[1])), mod_weight[...])[0:8]
    mod = mod + mod_bias[...].astype(F32).reshape(1, 2 * WIDTH)
    modulation[...] = mod
    block = layout[0, 0]
    lit = jnp.int32(0)
    for k in range(PATCHB):
        lit = lit + jnp.where(block - TRIB == k, foreground[0, k], 0)
    kept = jnp.logical_or(block < TRIB, lit > 0)
    normed, _ = norm_parts(tokens[...].astype(F32))
    hidden = (normed * (1.0 + mod[0:1, :WIDTH]) + mod[0:1, WIDTH:]).astype(BF)
    projected = nn(hidden, in_weight[...]).astype(BF).astype(F32)
    low = low_lanes(BLOCK)
    low_half = low_lanes(16)
    corner = jnp.logical_and(
        lax.broadcasted_iota(jnp.int32, (BLOCK, 128), 0) == 0, lax.broadcasted_iota(jnp.int32, (BLOCK, 128), 1) == 0
    )
    flagged = jnp.logical_and(corner, jnp.logical_not(kept))
    for pair in range(HEADS // 2):
        at = 128 * pair
        query = projected[:, at : at + 128] * SCALE
        key = projected[:, WIDTH + at : WIDTH + at + 128]
        value = projected[:, 2 * WIDTH + at : 2 * WIDTH + at + 128]
        query_turned = half_turn(query)
        for odd in range(2):
            head = 2 * pair + odd
            if odd:
                both = jnp.where(low, half_turn(key), value)
                first, second = query_turned, query
            else:
                both = jnp.where(low, key, half_turn(value))
                first, second = query, query_turned
            both = jnp.where(flagged, FLAG, both).astype(BF)
            for quarter in range(QUARTERS):
                to = QUARTERS * head + quarter
                message[to, 0:128, :] = both
                top = SHARE * quarter
                for k in range(3):
                    message[to, 144 + 32 * k : 176 + 32 * k, :] = features[:, 128 * k : 128 * (k + 1)]
                message[to, 128:144, :] = jnp.where(
                    low_half, first[top : top + 16], second[top + 16 : top + 32]
                ).astype(BF)
            some = slice(QUARTERS * head, QUARTERS * (head + 1))
            pltpu.make_async_copy(message.at[some], far_message.at[some], semaphores.at[head]).start()
    for head in range(HEADS):
        some = slice(QUARTERS * head, QUARTERS * (head + 1))
        pltpu.make_async_copy(message.at[some], far_message.at[some], semaphores.at[head]).wait()


def loop(count, work, unroll=1):
    def turn(k, carry):
        work(k)
        return carry

    lax.fori_loop(0, count, turn, 0, unroll=unroll)


def block_of(k, size):
    return pl.ds(pl.multiple_of(k * size, size), size)


def gather_keys(received, masked_keys, pairs, queries, turned):
    low = low_lanes(128)
    lane = lax.broadcasted_iota(jnp.int32, (128, 128), 1)
    lane_q = lax.broadcasted_iota(jnp.int32, (16, 128), 1)
    extra = jnp.where(lane_q == 64, 1.0, 0.0)

    def gather(k):
        at = block_of(k, 128)
        both = received[k, 0:128, :].astype(F32)
        mine = received[k, 128:144, :].astype(F32)
        masked = both[0:1, 0:1] > 1e38
        masked_keys[at, :] = jnp.where(
            low, jnp.where(masked, 0.0, both), jnp.where(jnp.logical_and(masked, lane == 64), MASKED, 0.0)
        ).astype(BF)
        if pairs is not None:
            pairs[at, :] = received[k, 0:128, :]
        if turned is not None:
            turned[:, at] = jnp.transpose(both).astype(BF)
        first = pl.ds(pl.multiple_of(SHARE * k, 16), 16)
        second = pl.ds(pl.multiple_of(SHARE * k + 16, 16), 16)
        queries[first, :] = jnp.where(lane_q < 64, mine, extra).astype(BF)
        queries[second, :] = jnp.where(lane_q < 64, half_turn(mine), extra).astype(BF)

    loop(PEERS, gather, 4)


KEYS = 512
ROWS = 1024
UNROLL_A = 4
UNROLL_B = 4
UNROLL_C = 1
BACK_KEYS = 1024
BACK_ROWS = 256
QUERIES = PEERS * SHARE


def attend_kernel(
    received, message, attended, log_total, pairs_turned, masked_keys, queries, scores, mixed, turned
):
    gather_keys(received, masked_keys, None, queries, pairs_turned)
    chunks = TOKENS // KEYS
    query = queries[...]

    def score(k, top):
        at = block_of(k, KEYS)
        part = nt(masked_keys[at, :], query)
        scores[at, :] = part
        return jnp.maximum(top, jnp.max(part, axis=0, keepdims=True))

    top = lax.fori_loop(0, chunks, score, jnp.full((1, ROWS), -jnp.inf, F32), unroll=UNROLL_A)
    mixed[...] = jnp.zeros_like(mixed)

    def mix(k, total):
        at = block_of(k, KEYS)
        chance = jnp.exp(scores[at, :] - top)
        mixed[...] += nn(pairs_turned[:, at], chance.astype(BF))
        return total + jnp.sum(chance, axis=0, keepdims=True)

    total = lax.fori_loop(0, chunks, mix, jnp.zeros((1, ROWS), F32), unroll=UNROLL_B)
    result = mixed[...] / total
    attended[...] = result[64:128, :]
    log_total[...] = jnp.broadcast_to(top + jnp.log(total), (8, ROWS))
    turned[...] = jnp.transpose(result)
    low = low_lanes(16)

    def pack(k):
        first = turned[pl.ds(pl.multiple_of(SHARE * k, 16), 16), :]
        second = turned[pl.ds(pl.multiple_of(SHARE * k + 16, 16), 16), :]
        message[k] = jnp.where(low, half_turn(first), second).astype(BF)

    loop(PEERS, pack, 4)


def pairs_kernel(
    received, pair_weight, keys, values, keys_turned, values_turned, every_turned, kept, every
):
    pair_weight = pair_weight.ready()

    def gather(k):
        for j in range(3):
            every[block_of(k, 32), 128 * j : 128 * (j + 1)] = received[k, 144 + 32 * j : 176 + 32 * j, :]
        kept.ref[k] = received[k, 0:144, :]

    def project(k):
        rows = block_of(k, 256)
        part = every[rows, :]
        every_turned.ref[:, rows] = jnp.transpose(part.astype(F32)).astype(BF)
        both = nn(part, pair_weight[...]).astype(BF)
        keys.ref[rows, :] = both[:, :WIDTH]
        values.ref[rows, :] = both[:, WIDTH:]
        turned = jnp.transpose(both.astype(F32)).astype(BF)
        keys_turned.ref[:, rows] = turned[:WIDTH, :]
        values_turned.ref[:, rows] = turned[WIDTH:, :]

    loop(PEERS, gather, 4)
    kept.send()
    loop(PATCHES // 256, project)


def unpack_heads(received):
    low = low_lanes(16)
    columns = []
    for pair in range(HEADS // 2):
        pieces = []
        for quarter in range(QUARTERS):
            even = received[QUARTERS * (2 * pair) + quarter].astype(F32)
            odd = received[QUARTERS * (2 * pair + 1) + quarter].astype(F32)
            pieces.append(jnp.where(low, even, half_turn(odd)))
            pieces.append(jnp.where(low, half_turn(even), odd))
        columns.append(jnp.concatenate(pieces, axis=0))
    return jnp.concatenate(columns, axis=1)


def pack_heads(values, message):
    low = low_lanes(16)
    for pair in range(HEADS // 2):
        for quarter in range(QUARTERS):
            first = values[SHARE * quarter : SHARE * quarter + 16, 128 * pair : 128 * (pair + 1)]
            second = values[SHARE * quarter + 16 : SHARE * (quarter + 1), 128 * pair : 128 * (pair + 1)]
            message[QUARTERS * (2 * pair) + quarter] = jnp.where(
                low, first, half_turn(second)
            ).astype(BF)
            message[QUARTERS * (2 * pair + 1) + quarter] = jnp.where(
                low, half_turn(first), second
            ).astype(BF)


GELU = 0.7978845608028654
CUBE = 0.044715


def put(place, keep, send, owner, rows, value):
    @pl.when(place[0] == owner)
    def _():
        keep[rows, :] = value

    @pl.when(place[0] != owner)
    def _():
        send[rows, :] = value


def middle_kernel(
    place, received, tokens, keys, keys_turned, values, values_turned, self_out, gain_two, offset_two,
    query_weight, cross_out, gain_three, offset_three, up_weight, down_weight, cotangent, every_turned, pair_weight,
    block_out, feed_keep, feed_send, vectors, message, self_grad, feature_part, pair_value,
    feed_pack, semaphores, key_all, value_all, total_out, total_back,
):
    def move(start, rows, to, slot):
        at = slice(to, to + rows)

        @pl.when(place[0] == 0)
        def _():
            pltpu.make_async_copy(feed_pack.at[0, start : start + rows], feed_keep.at[at], semaphores.at[slot, 0]).start()
            pltpu.make_async_copy(feed_pack.at[1, start : start + rows], feed_send.at[at], semaphores.at[slot, 1]).start()

        @pl.when(place[0] != 0)
        def _():
            pltpu.make_async_copy(feed_pack.at[1, start : start + rows], feed_keep.at[at], semaphores.at[slot, 0]).start()
            pltpu.make_async_copy(feed_pack.at[0, start : start + rows], feed_send.at[at], semaphores.at[slot, 1]).start()

    def put_halves(start, value):
        rows = value.shape[0] // 2
        feed_pack[0, start : start + rows, :] = value[:rows]
        feed_pack[1, start : start + rows, :] = value[rows:]

    attended_low = unpack_heads(received).astype(BF)
    first = tokens[...].astype(F32) + nn(attended_low, self_out[...])
    normed_two, inverse_two = norm_parts(first)
    gain = gain_two[...].astype(F32)
    hidden = (normed_two * gain + offset_two[...].astype(F32)).astype(BF)
    queries = nn(hidden, query_weight[...]).astype(BF).astype(F32) * SCALE
    low = low_lanes(BLOCK)
    upper = lax.broadcasted_iota(jnp.int32, (128, BLOCK), 0) < 64
    masked = []
    chances = []
    pieces = []
    for pair in range(HEADS // 2):
        at = slice(128 * pair, 128 * (pair + 1))
        key = keys[:, at]
        value = values_turned[at, :]
        parts = []
        for odd in range(2):
            mine = jnp.where(low if odd == 0 else jnp.logical_not(low), queries[:, at], 0.0).astype(BF)
            scores = nt(key, mine)
            chance = jnp.exp(scores - jnp.max(scores, axis=0, keepdims=True))
            chance = chance * (1.0 / jnp.sum(chance, axis=0, keepdims=True))
            masked.append(mine)
            chances.append(chance)
            parts.append(nn(value, chance.astype(BF)))
        pieces.append(jnp.transpose(jnp.where(upper, parts[0], parts[1])))
    mixed = jnp.concatenate(pieces, axis=1).astype(BF)
    second = first + nn(mixed, cross_out[...])
    normed, inverse = norm_parts(second)
    gain_out = gain_three[...].astype(F32)
    hidden3 = (normed * gain_out + offset_three[...].astype(F32)).astype(BF)
    grad_low = cotangent[...]
    total_out[...] = second
    total_back[...] = jnp.zeros((BLOCK, WIDTH), F32)
    up_all, down_all = up_weight.ready(), down_weight.ready()

    def feed_block(k, carry):
        at = pl.ds(pl.multiple_of(512 * k, 512), 512)
        up, down = up_all[:, at], down_all[at, :]
        pre = nn(hidden3, up)
        square = pre * pre
        turn = jnp.tanh(GELU * (pre + CUBE * (square * pre)))
        half = 0.5 * (1.0 + turn)
        active = (pre * half).astype(BF)
        slope = half + (0.5 * pre) * (1.0 - turn * turn) * (GELU * (1.0 + (3.0 * CUBE) * square))
        total_out[...] += nn(active, down)
        pre_grad = (nt(grad_low, down) * slope).astype(BF)
        total_back[...] += nt(pre_grad, up)
        grad = tn(hidden3, pre_grad).astype(BF)
        feed_pack[0, pl.ds(pl.multiple_of(256 * k, 256), 256), :] = grad[:256]
        feed_pack[1, pl.ds(pl.multiple_of(256 * k, 256), 256), :] = grad[256:]
        feed_pack[k // 2, pl.ds(pl.multiple_of(1024 + 512 * (k % 2), 512), 512), :] = tn(active, grad_low).astype(BF)
        return carry

    lax.fori_loop(0, 4, feed_block, 0, unroll=1)
    result = total_out[...]
    back = total_back[...]
    move(0, 2048, 0, 0)
    block_out[...] = result
    vectors[2:3, :] = jnp.sum(back * normed, axis=0, keepdims=True)
    vectors[3:4, :] = jnp.sum(back, axis=0, keepdims=True)
    grad = grad_low.astype(F32) + norm_back(normed, inverse, back * gain_out)
    branch = grad.astype(BF)
    put_halves(2048, tn(mixed, branch).astype(BF))
    mixed_grad = nt(branch, cross_out[...]).astype(BF).astype(F32)
    pieces = []
    pair_low = []
    for pair in range(HEADS // 2):
        at = slice(128 * pair, 128 * (pair + 1))
        value = values[:, at]
        key_turned = keys_turned[at, :]
        parts = []
        key_sum = None
        value_sum = None
        for odd in range(2):
            head = 2 * pair + odd
            given = jnp.where(low if odd == 0 else jnp.logical_not(low), mixed_grad[:, at], 0.0).astype(BF)
            chance = chances[head]
            chance_grad = nt(value, given)
            inner = jnp.sum(chance * chance_grad, axis=0, keepdims=True)
            score_grad = (chance * (chance_grad - inner)).astype(BF)
            parts.append(nn(key_turned, score_grad))
            key_part = nn(score_grad, masked[head])
            value_part = nn(chance.astype(BF), given)
            key_sum = key_part if key_sum is None else key_sum + key_part
            value_sum = value_part if value_sum is None else value_sum + value_part
        pair_low.append((key_sum.astype(BF), value_sum.astype(BF)))
        pieces.append(jnp.transpose(jnp.where(upper, parts[0], parts[1])) * SCALE)
    low_grad = jnp.concatenate(pieces, axis=1).astype(BF)
    back = nt(low_grad, query_weight[...])
    vectors[0:1, :] = jnp.sum(back * normed_two, axis=0, keepdims=True)
    vectors[1:2, :] = jnp.sum(back, axis=0, keepdims=True)
    vectors[4:8, :] = jnp.zeros((4, WIDTH), F32)
    grad = grad + norm_back(normed_two, inverse_two, back * gain)
    self_grad[...] = grad
    branch = grad.astype(BF)
    pack_heads(nt(branch, self_out[...]), message)
    put_halves(2304, tn(hidden, low_grad).astype(BF))
    put_halves(2560, tn(attended_low, branch).astype(BF))
    key_grad = jnp.concatenate([p[0] for p in pair_low], axis=1)
    value_grad = jnp.concatenate([p[1] for p in pair_low], axis=1)
    put_halves(2816, nn(every_turned[...], key_grad).astype(BF))
    pair_value[...] = nn(every_turned[...], value_grad).astype(BF)
    feed_pack[0, 3008:3072, :] = jnp.zeros((64, WIDTH), BF)
    feed_pack[1, 3008:3072, :] = jnp.zeros((64, WIDTH), BF)
    move(2048, 1024, 2048, 1)
    def feature_block(k, carry):
        rows = pl.ds(pl.multiple_of(256 * k, 256), 256)
        part = (nt(key_all[rows, :], pair_keys) + nt(value_all[rows, :], pair_values)).astype(BF)
        for i in range(8):
            for j in range(3):
                feature_part[8 * k + i, 32 * j : 32 * (j + 1), :] = part[
                    32 * i : 32 * (i + 1), 128 * j : 128 * (j + 1)
                ]
        return carry

    pair_keys, pair_values = pair_weight[:, :WIDTH], pair_weight[:, WIDTH:]
    key_all[...] = key_grad
    value_all[...] = value_grad
    lax.fori_loop(0, PATCHES // 256, feature_block, 0)
    for slot, rows in enumerate((2048, 1024)):
        for k in range(2):
            pltpu.make_async_copy(
                feed_pack.at[0, 0:rows], feed_keep.at[0:rows], semaphores.at[slot, k]
            ).wait()


def put_halves(place, keep, send, start, value):
    rows = value.shape[0] // 2
    put(place, keep, send, 0, slice(start, start + rows), value[:rows])
    put(place, keep, send, 1, slice(start, start + rows), value[rows:])


def attend_back_kernel(
    received, pairs_turned, attended, log_total, given, feature_part, message,
    masked_keys, pairs, queries, outer, outer_row, chances, score_grads, query_sum, turned,
):
    received = received.ready()
    gather_keys(received, masked_keys, pairs, queries, None)
    low = low_lanes(16)

    def unpack(k):
        piece = given[k].astype(F32)
        outer[pl.ds(pl.multiple_of(SHARE * k, 16), 16), :] = jnp.where(low, 0.0, half_turn(piece)).astype(BF)
        outer[pl.ds(pl.multiple_of(SHARE * k + 16, 16), 16), :] = jnp.where(low, 0.0, piece).astype(BF)
        message[k, 144:240, :] = feature_part[k]

    loop(PEERS, unpack, 4)
    attended = attended.ready()

    def inner(k):
        rows = block_of(k, 256)
        turned = jnp.transpose(outer[rows, :].astype(F32))[64:128, :]
        outer_row[:, rows] = jnp.broadcast_to(
            jnp.sum(turned * attended[:, rows], axis=0, keepdims=True), (8, 256)
        )

    loop(QUERIES // 256, inner)
    query_sum[...] = jnp.zeros_like(query_sum)
    pairs_turned, log_total = pairs_turned.ready(), log_total.ready()

    def chunk(turn, carry):
        at = pl.ds(pl.multiple_of(turn * BACK_KEYS, BACK_KEYS), BACK_KEYS)
        key = masked_keys[at, :]
        both = pairs[at, :]
        for k in range(QUERIES // BACK_ROWS):
            rows = slice(BACK_ROWS * k, BACK_ROWS * (k + 1))
            chance = jnp.exp(nt(key, queries[rows, :]) - log_total[0:1, rows])
            chance_grad = nt(both, outer[rows, :])
            chances[:, rows] = chance.astype(BF)
            score_grads[:, rows] = (chance * (chance_grad - outer_row[0:1, rows])).astype(BF)
        sums = nn(score_grads[...], queries[...])
        other = nn(chances[...], outer[...])
        sums = jnp.where(low_lanes(BACK_KEYS), sums, other).astype(BF)
        for k in range(BACK_KEYS // 128):
            message[turn * (BACK_KEYS // 128) + k, 0:128, :] = sums[128 * k : 128 * (k + 1), :]
        query_sum[...] += nn(pairs_turned[:, at], score_grads[...])
        return carry

    lax.fori_loop(0, TOKENS // BACK_KEYS, chunk, 0, unroll=UNROLL_C)
    turned[...] = jnp.transpose(query_sum[...]) * SCALE

    def pack(k):
        first = turned[pl.ds(pl.multiple_of(SHARE * k, 16), 16), :]
        second = turned[pl.ds(pl.multiple_of(SHARE * k + 16, 16), 16), :]
        message[k, 128:144, :] = jnp.where(low, first, half_turn(second)).astype(BF)

    loop(PEERS, pack, 4)


def finish_kernel(
    place, received, tokens, camera, modulation, self_grad, in_weight, vectors,
    pair_value, token_grad, feature_grad, keep, send,
):
    total = received[0, 144:240, :].astype(F32)
    for k in range(1, PEERS):
        total = total + received[k, 144:240, :].astype(F32)
    for j in range(3):
        feature_grad[:, 128 * j : 128 * (j + 1)] = total[32 * j : 32 * (j + 1), :]
    low = low_lanes(BLOCK)
    queries = []
    keys = []
    values = []
    for pair in range(HEADS // 2):
        sums = []
        for odd in range(2):
            head = 2 * pair + odd
            total = received[QUARTERS * head, 0:128, :].astype(F32)
            for quarter in range(1, QUARTERS):
                total = total + received[QUARTERS * head + quarter, 0:128, :].astype(F32)
            sums.append(total)
        keys.append(jnp.where(low, sums[0], half_turn(sums[1])))
        values.append(jnp.where(low, half_turn(sums[0]), sums[1]))
        low_half = low_lanes(16)
        pieces = []
        for quarter in range(QUARTERS):
            even = received[QUARTERS * (2 * pair) + quarter, 128:144, :].astype(F32)
            odd = received[QUARTERS * (2 * pair + 1) + quarter, 128:144, :].astype(F32)
            pieces.append(jnp.where(low_half, even, half_turn(odd)))
            pieces.append(jnp.where(low_half, half_turn(even), odd))
        queries.append(jnp.concatenate(pieces, axis=0))
    parts = [jnp.concatenate(p, axis=1).astype(BF) for p in (queries, keys, values)]
    normed, inverse = norm_parts(tokens[...].astype(F32))
    scale = 1.0 + modulation[0:1, :WIDTH]
    hidden = (normed * scale + modulation[0:1, WIDTH:]).astype(BF)
    back = jnp.zeros((BLOCK, WIDTH), F32)
    for k in range(3):
        at = slice(WIDTH * k, WIDTH * (k + 1))
        back = back + nt(parts[k], in_weight[:, at])
        put_halves(place, keep, send, 256 * k, tn(hidden, parts[k]).astype(BF))
    token_grad[...] = self_grad[...] + norm_back(normed, inverse, back * scale)
    scale_grad = jnp.sum(back * normed, axis=0, keepdims=True)
    shift_grad = jnp.sum(back, axis=0, keepdims=True)
    cam = camera[...].astype(F32)
    cam_act = cam * jax.nn.sigmoid(cam)
    row = lax.broadcasted_iota(jnp.int32, (32, WIDTH), 0)
    item = place[1]
    first = place[2] == 0
    small = jnp.where(row == item, scale_grad, 0.0)
    small = small + jnp.where(row == 4 + item, shift_grad, 0.0)
    small = small + jnp.where(jnp.logical_and(first, row == 8 + item), cam_act[:, :WIDTH], 0.0)
    small = small + jnp.where(jnp.logical_and(first, row == 12 + item), cam_act[:, WIDTH:], 0.0)
    small = small + jnp.where(row == 16, vectors[0:1, :], 0.0)
    small = small + jnp.where(row == 17, vectors[1:2, :], 0.0)
    small = small + jnp.where(row == 18, vectors[2:3, :], 0.0)
    small = small + jnp.where(row == 19, vectors[3:4, :], 0.0)
    put_halves(place, keep, send, 768, pair_value[...])
    keep[960:992, :] = small.astype(BF)
    send[960:992, :] = small.astype(BF)
    keep[992:1024, :] = jnp.zeros((32, WIDTH), BF)
    send[992:1024, :] = jnp.zeros((32, WIDTH), BF)


def sum_split_kernel(which, place, *refs):
    parts, pieces = refs[:-4], refs[-4:]
    rows = pieces[0].shape[0]
    for k in range(4):
        at = pl.ds(pl.multiple_of(lax.rem(place[which] + k, 4) * rows, rows), rows)
        total = parts[0][at, :].astype(F32)
        for part in parts[1:]:
            total = total + part[at, :].astype(F32)
        pieces[k][...] = total.astype(BF)


def halves_kernel(place, value, mine, other):
    rows = mine.shape[0]
    mine[...] = value[pl.ds(pl.multiple_of(place[0] * rows, rows), rows), :]
    other[...] = value[pl.ds(pl.multiple_of((1 - place[0]) * rows, rows), rows), :]


def sum_kernel(*refs):
    total = refs[0][...].astype(F32)
    for part in refs[1:-1]:
        total = total + part[...].astype(F32)
    refs[-1][...] = total.astype(BF)


def sum_pairs_kernel(first, second, third, fourth, out):
    rows = first.shape[0]
    out[0:rows, :] = (first[...].astype(F32) + second[...].astype(F32)).astype(BF)
    out[rows : 2 * rows, :] = (third[...].astype(F32) + fourth[...].astype(F32)).astype(BF)


def arrange_kernel(which, place, *refs):
    pieces, out = refs[:-1], refs[-1]
    rows = pieces[0].shape[0]
    for k in range(4):
        at = pl.ds(pl.multiple_of(lax.rem(place[which] + 4 - k, 4) * rows, rows), rows)
        out[at, :] = pieces[k][...]


def sum_pieces_kernel(pieces, *outs):
    total = pieces[0].astype(F32)
    for k in range(1, pieces.shape[0]):
        total = total + pieces[k].astype(F32)
    total = total.astype(BF)
    for out in outs:
        if len(out.shape) == 2:
            out[...] = total
        else:
            for k in range(out.shape[0]):
                out[k] = total


def write_halves(core, early, late, outs, buffers, semaphores):
    up_grad, down_grad, self_in, pair, self_out, cross_query, cross_out = outs
    up_part, down_part, in_part, pair_part, out_part, query_part, cross_part = buffers
    copies = []

    def send(part, target, slot):
        rows = part.shape[0]
        at = pl.ds(pl.multiple_of(core * rows, rows), rows)
        copies.append(pltpu.make_async_copy(part, target.at[at, :], semaphores.at[slot]))
        copies[-1].start()

    for k in range(4):
        up_part[:, 512 * k : 512 * (k + 1)] = early[256 * k : 256 * (k + 1), :].astype(F32)
    send(up_part, up_grad, 0)
    down_part[...] = early[1024:2048, :].astype(F32)
    send(down_part, down_grad, 1)
    for k in range(3):
        in_part[:, 512 * k : 512 * (k + 1)] = late[256 * k : 256 * (k + 1), :].astype(F32)
    send(in_part, self_in, 2)
    pair_part[:, :WIDTH] = early[2816:3008, :].astype(F32)
    pair_part[:, WIDTH:] = late[768:960, :].astype(F32)
    send(pair_part, pair, 3)
    out_part[...] = early[2560:2816, :].astype(F32)
    send(out_part, self_out, 4)
    query_part[...] = early[2304:2560, :].astype(F32)
    send(query_part, cross_query, 5)
    cross_part[...] = early[2048:2304, :].astype(F32)
    send(cross_part, cross_out, 6)
    return copies


def own_out_kernel(place, early, late, *refs):
    mod_weight, mod_bias, gain_two, offset_two, gain_three, offset_three = refs[7:13]
    small = late[960:992, :].astype(F32)
    grads = small[0:8, :]
    acts = small[8:16, :].astype(BF)
    head = lax.broadcasted_iota(jnp.int32, (8, WIDTH), 0) < 4
    turned = pltpu.roll(grads, 4, 0)
    mod_weight[:WIDTH, :WIDTH] = tn(acts, jnp.where(head, grads, 0.0).astype(BF))
    mod_weight[:WIDTH, WIDTH:] = tn(acts, jnp.where(head, turned, 0.0).astype(BF))
    mod_weight[WIDTH:, :WIDTH] = tn(acts, jnp.where(head, 0.0, turned).astype(BF))
    mod_weight[WIDTH:, WIDTH:] = tn(acts, jnp.where(head, 0.0, grads).astype(BF))
    mod_weight.send()
    gain_two[...] = small[16:17, :]
    offset_two[...] = small[17:18, :]
    gain_three[...] = small[18:19, :]
    offset_three[...] = small[19:20, :]
    mod_bias[:, :WIDTH] = jnp.sum(jnp.where(head, grads, 0.0), axis=0, keepdims=True)
    mod_bias[:, WIDTH:] = jnp.sum(jnp.where(head, 0.0, grads), axis=0, keepdims=True)
    for copy in write_halves(place[0], early, late, refs[:7], refs[13:20], refs[20]):
        copy.wait()


def other_out_kernel(place, early, late, *refs):
    for copy in write_halves(1 - place[0], early, late, refs[7:14], refs[14:21], refs[21]):
        copy.wait()


def index_of(x, y, z, core):
    return ((z % 2) * 2 + core) * 32 + (y * 4 + x) * 2 + z // 2


CHIPS = [(x, y, z) for x in range(4) for y in range(4) for z in range(4)]
SAME_CORE = [[index_of(*chip, core) for chip in CHIPS] for core in range(2)]
SAME_PLANE = [
    [index_of(x, y, z, core) for x in range(4) for y in range(4)] for z in range(4) for core in range(2)
]
OTHER_CORE = [
    (index_of(*chip, core), index_of(*chip, 1 - core)) for chip in CHIPS for core in range(2)
]


def shift_of(axis, step):
    moves = []
    for chip in CHIPS:
        there = list(chip)
        there[axis] = (there[axis] + step) % 4
        moves += [(index_of(*chip, core), index_of(*there, core)) for core in range(2)]
    return moves


SHIFTS = {(axis, step): shift_of(axis, step) for axis in range(3) for step in (1, 2, 3)}


def exchange(message):
    return lax.all_to_all(message, "seq", 0, 0, tiled=True)


def swap_cores(value):
    return lax.ppermute(value, AXES, OTHER_CORE)


def scatter_ring(pieces, axis):
    return (pieces[0],) + tuple(lax.ppermute(pieces[k], AXES, SHIFTS[axis, k]) for k in (1, 3, 2))


def gather_ring(piece, axis):
    came = {k: lax.ppermute(piece, AXES, SHIFTS[axis, k]) for k in (1, 3, 2)}
    return piece, came[1], came[2], came[3]


def sum_split(place, parts, axis):
    rows = parts[0].shape[0] // 4
    return call(
        functools.partial(sum_split_kernel, 3 + axis), (shape((rows, WIDTH), BF),) * 4, (place, *parts),
        traffic=4e5, smem=(0,),
    )


def sum_all(parts):
    return call(sum_kernel, shape(parts[0].shape, BF), parts, traffic=4e5)


def arrange(place, parts, axis):
    return call(
        functools.partial(arrange_kernel, 3 + axis), shape((4 * parts[0].shape[0], WIDTH), BF), (place, *parts),
        traffic=4e5, smem=(0,),
    )


def scatter_chips(value):
    rows = value.shape[0] // 64
    return lax.all_to_all(
        value.reshape(64, rows, WIDTH), AXES, 0, 0, tiled=True, axis_index_groups=SAME_CORE
    )


def in_one_step(always, work, *values):
    def nothing(*values):
        return jax.tree.map(lambda v: jnp.zeros(v.shape, v.dtype), jax.eval_shape(work, *values))

    return lax.cond(always, work, nothing, *values)


def body(
    tokens, camera, features, foreground, layout, modulation_weight, modulation_bias,
    self_in_weight, self_out_weight, cross_norm_gain, cross_norm_bias, cross_query_weight,
    cross_pair_weight, cross_out_weight, feed_norm_gain, feed_norm_bias, up_weight, down_weight,
    cotangent,
):
    tokens = tokens[0]
    features = features[0]
    cotangent = cotangent[0]
    row = lambda v: v.reshape(1, -1)
    step = functools.partial(in_one_step, layout[0, 0] >= 0)
    gain_two, offset_two = row(cross_norm_gain), row(cross_norm_bias)
    gain_three, offset_three = row(feed_norm_gain), row(feed_norm_bias)
    item, spot = lax.axis_index("batch"), lax.axis_index("seq")
    place = jnp.stack(
        [item & 1, item, spot, (spot >> 1) & 3, spot >> 3, (spot & 1) * 2 + (item >> 1)]
    ).astype(jnp.int32)

    message, modulation = call(
        prepare_kernel,
        (shape((PEERS, 240, 128), BF), shape((8, 1024))),
        (foreground, layout, tokens, features, camera, modulation_weight, modulation_bias, self_in_weight),
        flops=1e9, traffic=8e6, smem=(0, 1), late=(4, 5, 2, 7, 3, 6), far_out=(0,), limit=57,
        scratch=(pltpu.VMEM((PEERS, 240, 128), BF), pltpu.SemaphoreType.DMA((HEADS,))),
    )
    received = exchange(message)
    message, attended_turned, log_total, pairs_turned = call(
        attend_kernel,
        (shape((PEERS, 16, 128), BF), shape((64, QUERIES)), shape((8, QUERIES)), shape((128, TOKENS), BF)),
        (received,),
        scratch=(
            pltpu.VMEM((TOKENS, 128), BF), pltpu.VMEM((QUERIES, 128), BF), pltpu.VMEM((TOKENS, ROWS), F32),
            pltpu.VMEM((128, QUERIES), F32), pltpu.VMEM((QUERIES, 128), F32),
        ),
        flops=9e9, traffic=4e6,
    )
    back = exchange(message)
    keys, values, keys_turned, values_turned, every_turned, kept = call(
        pairs_kernel,
        (
            shape((PATCHES, WIDTH), BF), shape((PATCHES, WIDTH), BF), shape((WIDTH, PATCHES), BF),
            shape((WIDTH, PATCHES), BF), shape((384, PATCHES), BF),
            shape((PEERS, 144, 128), BF),
        ),
        (received, cross_pair_weight),
        scratch=(pltpu.VMEM((PATCHES, 384), BF),),
        flops=3e9, traffic=8e6, late=(1,), away=(5, 0, 1, 2, 3, 4),
    )
    (
        block_out, early_keep, early_send, vectors, message, self_grad, feature_message, pair_value,
    ) = call(
        middle_kernel,
        (
            shape((BLOCK, WIDTH)), shape((3072, WIDTH), BF), shape((3072, WIDTH), BF), shape((8, WIDTH)),
            shape((PEERS, 16, 128), BF), shape((BLOCK, WIDTH)), shape((PEERS, 96, 128), BF), shape((384, WIDTH), BF),
        ),
        (
            place, back, tokens, keys, keys_turned, values, values_turned, self_out_weight, gain_two, offset_two,
            cross_query_weight, cross_out_weight, gain_three, offset_three, up_weight, down_weight, cotangent,
            every_turned, cross_pair_weight,
        ),
        scratch=(
            pltpu.VMEM((2, 3072, WIDTH), BF), pltpu.SemaphoreType.DMA((2, 2)), pltpu.VMEM((PATCHES, WIDTH), BF),
            pltpu.VMEM((PATCHES, WIDTH), BF), pltpu.VMEM((BLOCK, WIDTH), F32), pltpu.VMEM((BLOCK, WIDTH), F32),
        ),
        flops=1.6e10, traffic=2e7, smem=(0,), late=(1, 7, 2, 8, 9, 10, 3, 6, 11, 12, 13, 14, 16, 15, 5, 4, 17, 18),
        limit=57,
        far_out=(1, 2),
    )

    def attend_back(message):
        given = exchange(message)
        total = sum_all((early_keep, swap_cores(early_send)))
        given, total = lax.optimization_barrier((given, total))
        pieces = scatter_chips(total)
        message = call(
            attend_back_kernel,
            shape((PEERS, 240, 128), BF),
            (kept, pairs_turned, attended_turned, log_total, given, feature_message),
            scratch=(
                pltpu.VMEM((TOKENS, 128), BF), pltpu.VMEM((TOKENS, 128), BF), pltpu.VMEM((QUERIES, 128), BF),
                pltpu.VMEM((QUERIES, 128), BF), pltpu.VMEM((8, QUERIES), F32),
                pltpu.VMEM((BACK_KEYS, QUERIES), BF), pltpu.VMEM((BACK_KEYS, QUERIES), BF),
                pltpu.VMEM((128, QUERIES), F32), pltpu.VMEM((QUERIES, 128), F32),
            ),
            flops=1.6e10, traffic=8e6, late=(0, 2, 1, 3),
        )
        message, pieces = lax.optimization_barrier((message, pieces))
        return message, call(sum_pieces_kernel, shape((48, WIDTH), BF), (pieces,), traffic=3e6)

    message, early = step(attend_back, message)
    early = lax.all_gather(early, AXES, axis=0, tiled=True, axis_index_groups=SAME_CORE)

    def finish(message):
        returned = exchange(message)
        token_grad, feature_grad, keep, send = call(
            finish_kernel,
            (shape((BLOCK, WIDTH)), shape((32, 384)), shape((1024, WIDTH), BF), shape((1024, WIDTH), BF)),
            (
                place, returned, tokens, camera, modulation, self_grad, self_in_weight, vectors,
                pair_value,
            ),
            flops=3e9, traffic=8e6, smem=(0,), late=(2, 6, 4, 5),
        )
        pieces = scatter_chips(sum_all((keep, swap_cores(send))))
        total = call(sum_pieces_kernel, shape(pieces.shape, BF), (pieces,), traffic=2e6)
        late = lax.all_to_all(
            total, AXES, 0, 0, tiled=True, axis_index_groups=SAME_CORE
        ).reshape(1024, WIDTH)
        return token_grad, feature_grad, late

    token_grad, feature_grad, late = step(finish, message)
    early, late = lax.optimization_barrier((early, late))
    early_other, late_other = swap_cores(early), swap_cores(late)
    square = shape((WIDTH, WIDTH))
    vector = shape((1, WIDTH))
    grads = (shape((WIDTH, 2048)), shape((2048, WIDTH)), shape((WIDTH, 3 * WIDTH)), shape((384, 1024))) + (square,) * 3
    halves = tuple(pltpu.VMEM((g.shape[0] // 2, g.shape[1]), F32) for g in grads)
    halves += (pltpu.SemaphoreType.DMA((7,)),)
    *grads, mod_weight_grad, mod_bias_grad, gain_two_grad, offset_two_grad, gain_three_grad, offset_three_grad = call(
        own_out_kernel, grads + (shape((1024, 1024)), shape((1, 1024))) + (vector,) * 4, (place, early, late),
        scratch=halves, traffic=1.4e7, smem=(0,), late=(1,), away=(7,), far_out=tuple(range(7)), limit=57,
    )
    up_grad, down_grad, self_in_grad, pair_grad, self_out_grad, cross_query_grad, cross_out_grad = call(
        other_out_kernel,
        tuple(shape(g.shape) for g in grads),
        (place, early_other, late_other, *grads),
        scratch=halves, traffic=1.4e7, smem=(0,), far_in=tuple(range(3, 10)), far_out=tuple(range(7)),
        aliases={3 + k: k for k in range(7)},
    )
    return (
        block_out[None],
        token_grad[None],
        feature_grad[None],
        mod_weight_grad,
        mod_bias_grad[0],
        self_in_grad,
        self_out_grad,
        gain_two_grad[0],
        offset_two_grad[0],
        cross_query_grad,
        pair_grad,
        cross_out_grad,
        gain_three_grad[0],
        offset_three_grad[0],
        up_grad,
        down_grad,
    )


def solution(mesh):
    split = P("batch", "seq", None)
    in_specs = (
        (split, P("batch", None), split, P("batch", None), P("batch", "seq")) + (P(),) * 13 + (split,)
    )
    out_specs = (split,) * 3 + (P(),) * 13
    return jax.shard_map(body, mesh=mesh, in_specs=in_specs, out_specs=out_specs, check_vma=False)
```
